32 devices in a mesh: src: 8 (over z, core), tgt: 4 (over y, x).
Axes of the slice: x: 2, y: 2, z: 4, core: 2. Of those that a mesh axis runs over, the one named last changes fastest.
Arguments:
- src_pts: float32 [64, 8192], P('tgt', 'src'), may hold values from -30 to 30
- tgt_pts: float32 [64, 8192], P('src', 'tgt'), may hold values from -6 to 6
- src_mass: float32 [8192], P('src'), may hold values from 0.1 to 1
- tgt_mass: float32 [8192], P('tgt'), may hold values from 0.1 to 1
- init_pot: float32 [8192], P('tgt'), may hold values from -3 to 3
Outputs:
- src_pot: float32 [8192], P('src')
- tgt_pot: float32 [8192], P('tgt')
- mapped: float32 [64, 8192], P('tgt', 'src')
The draws below stay inside these ranges and needn't reach their ends.
All inputs are finite; a program needn't handle non-finite values.
Results may differ from the reference program's by a relative error of at most 0.0003.
Values sent between devices are 32-bit elements; how exact they have to be, the bound alone decides.
No kernel may reach another device: no remote copies, remote signals or barrier semaphores. Data moves between devices by JAX's collectives and lax.ppermute only.
A program may use at most 64 MiB of HBM per device.

```python
import math
import jax
import jax.numpy as jnp
from jax import lax

K = 64
ITERS = 3
NS = 8192
NT = 8192


def draw_src_pts(key, part):
    key = jax.random.fold_in(key, 11)
    base_key = jax.random.fold_in(key, 0)
    mark_key = jax.random.fold_in(key, 2)
    pick_key = jax.random.fold_in(key, 3)
    values = jnp.clip(jax.random.normal(base_key, (K, NS), jnp.float32), -6.0, 6.0)
    marks = jax.random.randint(mark_key, (NS,), 0, 32)
    chosen = jax.random.randint(pick_key, (), 0, NS)
    columns = jnp.arange(NS)
    distant = jnp.logical_or(marks == 0, columns == chosen)
    values = jnp.where(distant[None, :], jnp.float32(25.0), values)
    return values


def draw_tgt_pts(key, part):
    key = jax.random.fold_in(key, 23)
    base_key, mark_key, pick_key = jax.random.split(key, 3)
    values = jnp.clip(jax.random.normal(base_key, (K, NT), jnp.float32), -6.0, 6.0)
    marks = jax.random.randint(mark_key, (NT,), 0, 32)
    chosen = jax.random.randint(pick_key, (), 0, NT)
    columns = jnp.arange(NT)
    upper = jnp.logical_or(marks == 0, columns == chosen)
    lower = jnp.logical_and(marks == 1, columns != chosen)
    values = jnp.where(upper[None, :], jnp.float32(6.0), values)
    values = jnp.where(lower[None, :], jnp.float32(-6.0), values)
    return values


def steps_of(own_key, dims, cuts, low, high):
    level, own = 1.0, jax.random.fold_in(own_key, 6)
    for dim, shards_of in cuts:
        draws = jnp.exp(jax.random.uniform(jax.random.fold_in(own, dim), (shards_of,), jnp.float32, low / len(cuts), high / len(cuts)))
        level = level * jnp.repeat(draws, dims[dim] // shards_of).reshape([-1 if axis == dim else 1 for axis in range(len(dims))])
    return level


def scatter_about(rng, dims, scale, reach, cuts=(), kind=jnp.bfloat16):
    loudness = steps_of(rng, dims, cuts, -0.22, 0.18) if cuts else 1.0
    result = jax.random.normal(rng, dims, jnp.float32) * scale * loudness
    return jnp.minimum(jnp.maximum(result, -reach), reach).astype(kind)


def setup_inputs(seed: int = 0) -> dict:
    seeds = jax.random.split(jax.random.key(seed), 6)
    return {
        "src_pts": draw_src_pts(jax.random.fold_in(seeds[5], 71), 0),
        "tgt_pts": draw_tgt_pts(jax.random.fold_in(seeds[5], 71), 0),
        "src_mass": jnp.clip(jnp.exp(math.log(1.0) - 2.3025851 * jax.random.uniform(seeds[2], (NS,), jnp.float32) ** steps_of(seeds[2], (NS,), ((0, 8),), -0.2, 0.2)), 0.1, 1.0),
        "tgt_mass": jnp.clip(jnp.exp(math.log(1.0) - 2.3025851 * jax.random.uniform(seeds[3], (NT,), jnp.float32) ** steps_of(seeds[3], (NT,), ((0, 4),), -0.2, 0.2)), 0.1, 1.0),
        "init_pot": scatter_about(seeds[4], (NT,), 0.5, 3.0, ((0, 4),), jnp.float32),
    }


EPS = 0.1


def cost_block(xblk, ys, ynorm):
    xnorm = jnp.sum(xblk * xblk, axis=0)
    cross = jnp.dot(xblk.T, ys, precision=lax.Precision.HIGHEST, preferred_element_type=jnp.float32)
    return (xnorm[:, None] + ynorm[None, :] - 2.0 * cross) / K


def reference(src_pts, tgt_pts, src_mass, tgt_mass, init_pot):
    rows = min(512, NS)
    nblk = NS // rows
    xblocks = src_pts.reshape(K, nblk, rows).transpose(1, 0, 2)
    ablocks = src_mass.reshape(nblk, rows)
    ynorm = jnp.sum(tgt_pts * tgt_pts, axis=0)

    def src_update(tgt_pot):
        def one(item):
            xblk, ablk = item
            score = (tgt_pot[None, :] - cost_block(xblk, tgt_pts, ynorm)) / EPS
            top = jnp.max(score, axis=1)
            lse = top + jnp.log(jnp.sum(jnp.exp(score - top[:, None]), axis=1))
            return EPS * jnp.log(ablk) - EPS * lse
        return lax.map(one, (xblocks, ablocks)).reshape(NS)

    def tgt_update(src_pot):
        fblocks = src_pot.reshape(nblk, rows)

        def one(carry, item):
            top, total = carry
            xblk, fblk = item
            score = (fblk[:, None] - cost_block(xblk, tgt_pts, ynorm)) / EPS
            btop = jnp.max(score, axis=0)
            new_top = jnp.maximum(top, btop)
            bsum = jnp.sum(jnp.exp(score - btop[None, :]), axis=0)
            total = total * jnp.exp(top - new_top) + bsum * jnp.exp(btop - new_top)
            return (new_top, total), None

        init = (jnp.full((NT,), -jnp.inf, jnp.float32), jnp.zeros((NT,), jnp.float32))
        (top, total), _ = lax.scan(one, init, (xblocks, fblocks))
        return EPS * jnp.log(tgt_mass) - EPS * (top + jnp.log(total))

    tgt_pot = init_pot
    src_pot = jnp.zeros((NS,), jnp.float32)
    for step in range(ITERS):
        src_pot = src_update(tgt_pot)
        tgt_pot = tgt_update(src_pot)

    fblocks = src_pot.reshape(nblk, rows)

    def proj(item):
        xblk, fblk = item
        weight = jnp.exp((fblk[:, None] + tgt_pot[None, :] - cost_block(xblk, tgt_pts, ynorm)) / EPS)
        num = jnp.dot(tgt_pts, weight.T, precision=lax.Precision.HIGHEST, preferred_element_type=jnp.float32)
        den = jnp.sum(weight, axis=1)
        return num / den[None, :]

    mapped = lax.map(proj, (xblocks, fblocks)).transpose(1, 0, 2).reshape(K, NS)
    return src_pot, tgt_pot, mapped
```

```python
import functools
import math

import jax
import jax.numpy as jnp
from jax import lax
from jax.experimental import pallas as pl
from jax.experimental.pallas import tpu as pltpu
from jax.sharding import PartitionSpec as P

ITERS = 3
EPS = 0.1
UNIT = EPS * math.log(2.0)

F32 = jnp.float32
BF16 = jnp.bfloat16
VMEM = pl.BlockSpec(memory_space=pltpu.VMEM)
LANES = 128


def pieces(v):
    a = v.astype(BF16)
    r = v - a.astype(F32)
    b = r.astype(BF16)
    c = (r - b.astype(F32)).astype(BF16)
    return a, b, c


def tree(op, items):
    items = list(items)
    while len(items) > 1:
        half = (len(items) + 1) // 2
        rest = items[half:]
        items = [op(items[k], rest[k]) if k < len(rest) else items[k] for k in range(half)]
    return items[0]


def whole_log_sum(parts):
    top = tree(jnp.maximum, parts)
    return top + jnp.log2(tree(jnp.add, [jnp.exp2(p - top) for p in parts]))


def rows_log_sum(s_ref, pot, top_ref, sum_ref):
    n, width = s_ref.shape
    cols = width // LANES
    pot8 = jnp.broadcast_to(pot, (8, width))

    def strip(k, _):
        rows = pl.ds(pl.multiple_of(k * 8, 8), 8)
        z = [s_ref[rows, pl.ds(c * LANES, LANES)] + pot8[:, c * LANES : (c + 1) * LANES] for c in range(cols)]
        top = tree(jnp.maximum, z)
        top_ref[rows, :] = top
        sum_ref[rows, :] = tree(jnp.add, [jnp.exp2(v - top) for v in z])
        return 0

    lax.fori_loop(0, n // 8, strip, 0, unroll=4)
    tops = top_ref[...].T
    top = jnp.max(tops, axis=0, keepdims=True)
    total = jnp.sum(sum_ref[...].T * jnp.exp2(tops - top), axis=0, keepdims=True)
    return top + jnp.log2(total)


def across(pot, out_ref):
    n = pot.shape[1]
    out_ref[...] = jnp.broadcast_to(pot, (LANES, n)).T


def cols_log_sum(s_ref, pot_ref):
    n, width = s_ref.shape
    cols = width // LANES

    def load(k):
        rows = pl.ds(pl.multiple_of(k * 8, 8), 8)
        f = pot_ref[rows, :]
        return [s_ref[rows, pl.ds(c * LANES, LANES)] + f for c in range(cols)]

    def find(k, top):
        return tuple(jnp.maximum(t, v) for t, v in zip(top, load(k)))

    top = lax.fori_loop(1, n // 8, find, tuple(load(0)), unroll=4)

    def add(k, total):
        return tuple(a + jnp.exp2(v - t) for a, v, t in zip(total, load(k), top))

    zero = tuple(jnp.zeros((8, LANES), F32) for _ in range(cols))
    total = lax.fori_loop(0, n // 8, add, zero, unroll=4)
    out = []
    for t, a in zip(top, total):
        m = jnp.max(t, axis=0, keepdims=True)
        out.append(m + jnp.log2(jnp.sum(a * jnp.exp2(t - m), axis=0, keepdims=True)))
    return jnp.concatenate(out, axis=1)


def first_kernel(x_ref, y_ref, pot_ref, s_ref, l_ref, xn_ref, yn_ref, xw, yw, top_ref, sum_ref):
    k = x_ref.shape[0]
    x = x_ref[...]
    y = y_ref[...]
    xn = jnp.sum(x * x, axis=0, keepdims=True) / k
    yn = jnp.sum(y * y, axis=0, keepdims=True) / k
    xn_ref[...] = xn
    yn_ref[...] = yn
    x1, x2, x3 = pieces(x)
    y1, y2, y3 = pieces(y * (2.0 / (k * UNIT)))
    for p, (xp, yp) in enumerate(((x1, y1), (x1, y2), (x2, y1), (x2, y2), (x1, y3), (x3, y1))):
        xw[pl.ds(p * k, k), :] = xp
        yw[pl.ds(p * k, k), :] = yp
    step = 256

    def block(b, _):
        rows = pl.ds(pl.multiple_of(b * step, step), step)
        s_ref[rows, :] = lax.dot_general(
            xw[:, rows], yw[...], (((0,), (0,)), ((), ())), preferred_element_type=F32
        )
        return 0

    lax.fori_loop(0, s_ref.shape[0] // step, block, 0)
    pot = (pot_ref[...] - yn) * (1.0 / UNIT)
    l_ref[...] = rows_log_sum(s_ref, pot, top_ref, sum_ref)


def src_kernel(count, s_ref, mass_ref, *refs):
    parts, (f_ref, l_ref, wide) = refs[:count], refs[count:]
    f = jnp.log2(mass_ref[...]) - whole_log_sum([p[...] for p in parts])
    f_ref[...] = f
    across(f, wide)
    l_ref[...] = cols_log_sum(s_ref, wide)


def tgt_kernel(count, s_ref, mass_ref, *refs):
    parts, (l_ref, top_ref, sum_ref) = refs[:count], refs[count:]
    g = jnp.log2(mass_ref[...]) - whole_log_sum([p[...] for p in parts])
    l_ref[...] = rows_log_sum(s_ref, g, top_ref, sum_ref)


def last_kernel(count, peers, me_ref, s_ref, mass_ref, f_ref, xn_ref, yn_ref, y_ref, *refs):
    parts, refs = refs[:count], refs[count:]
    sp_ref, tp_ref, outs, (wide, yw, acc, flat) = refs[0], refs[1], refs[2 : 2 + peers], refs[2 + peers :]
    k = y_ref.shape[0]
    n, width = s_ref.shape
    g = jnp.log2(mass_ref[...]) - whole_log_sum([p[...] for p in parts])
    f = f_ref[...]
    sp_ref[...] = f * UNIT + xn_ref[...]
    tp_ref[...] = g * UNIT + yn_ref[...]
    across(f, wide)
    y1, y2, _ = pieces(y_ref[...])
    yw[pl.ds(0, k), :] = y1
    yw[pl.ds(k, k), :] = y2
    yw[pl.ds(2 * k, 16), :] = jnp.ones((16, width), BF16)
    step = 128

    def block(b, _):
        rows = pl.ds(pl.multiple_of(b * step, step), step)
        fb = wide[rows, :]
        w = jnp.exp2(s_ref[rows, :] + g + jnp.concatenate([fb] * (width // LANES), axis=1))
        w1 = w.astype(BF16)
        w2 = (w - w1.astype(F32)).astype(BF16)
        dims = (((1,), (1,)), ((), ()))
        one = lax.dot_general(w1, yw[...], dims, preferred_element_type=F32)
        two = lax.dot_general(w2, yw[...], dims, preferred_element_type=F32)
        acc[rows, :] = one + two
        return 0

    lax.fori_loop(0, n // step, block, 0)
    whole = acc[:, : 2 * k].T
    num = whole[:k, :] + whole[k:, :]
    own = k // peers
    for t in range(peers):
        flat[t] = num[t * own : (t + 1) * own, :]
    den = jnp.broadcast_to(acc[:, 2 * k : 2 * k + 1], (n, LANES)).T[0:1, :]
    me = me_ref[0]
    for d, out in enumerate(outs):
        out[pl.ds(0, own), :] = flat[lax.rem(me + d, peers)]
        out[pl.ds(own, 1), :] = den


def join_kernel(own, *refs):
    parts, out_ref = refs[:-1], refs[-1]
    num = tree(jnp.add, [p[pl.ds(0, own), :] for p in parts])
    den = tree(jnp.add, [p[pl.ds(own, 1), :] for p in parts])
    out_ref[...] = num / den


def call(kernel, outs, scratch, *args, scalars=0):
    smem = pl.BlockSpec(memory_space=pltpu.SMEM)
    return pl.pallas_call(
        kernel,
        out_shape=[jax.ShapeDtypeStruct(s, F32) for s in outs],
        in_specs=[smem] * scalars + [VMEM] * (len(args) - scalars),
        out_specs=[VMEM] * len(outs),
        scratch_shapes=scratch,
        compiler_params=pltpu.CompilerParams(vmem_limit_bytes=32 * 2**20),
    )(*args)


def everyone(v, axis, size):
    return [v] + [lax.ppermute(v, axis, [(i, (i + d) % size) for i in range(size)]) for d in range(1, size)]


def shards(peers_src, peers_tgt, src_pts, tgt_pts, src_mass, tgt_mass, init_pot):
    own = src_pts.shape[0]
    n, width = src_pts.shape[1], tgt_pts.shape[1]
    xs = lax.all_gather(src_pts, "tgt", axis=0, tiled=True)
    ys = lax.all_gather(tgt_pts, "src", axis=0, tiled=True)
    k = xs.shape[0]
    src_mass = src_mass.reshape(1, n)
    tgt_mass = tgt_mass.reshape(1, width)
    row, col = (1, n), (1, width)
    lane = pltpu.VMEM((n, LANES), F32)
    s, l, xn, yn = call(
        first_kernel,
        [(n, width), row, row, col],
        [pltpu.VMEM((6 * k, n), BF16), pltpu.VMEM((6 * k, width), BF16), lane, lane],
        xs,
        ys,
        init_pot.reshape(1, width),
    )
    for step in range(ITERS):
        parts = everyone(l, "tgt", peers_tgt)
        f, l = call(functools.partial(src_kernel, len(parts)), [row, col], [lane], s, src_mass, *parts)
        parts = everyone(l, "src", peers_src)
        if step < ITERS - 1:
            (l,) = call(functools.partial(tgt_kernel, len(parts)), [row], [lane, lane], s, tgt_mass, *parts)
    me = lax.axis_index("tgt").astype(jnp.int32).reshape(1)
    src_pot, tgt_pot, *blocks = call(
        functools.partial(last_kernel, len(parts), peers_tgt),
        [row, col] + [(own + 1, n)] * peers_tgt,
        [lane, pltpu.VMEM((2 * k + 16, width), BF16), pltpu.VMEM((n, 2 * k + 16), F32), pltpu.VMEM((peers_tgt, own, n), F32)],
        me,
        s,
        tgt_mass,
        f,
        xn,
        yn,
        ys,
        *parts,
        scalars=1,
    )
    came = [blocks[0]] + [
        lax.ppermute(blocks[d], "tgt", [(i, (i + d) % peers_tgt) for i in range(peers_tgt)])
        for d in range(1, peers_tgt)
    ]
    (mapped,) = call(functools.partial(join_kernel, own), [(own, n)], [], *came)
    return src_pot.reshape(n), tgt_pot.reshape(width), mapped


def solution(mesh):
    return jax.shard_map(
        functools.partial(shards, mesh.shape["src"], mesh.shape["tgt"]),
        mesh=mesh,
        in_specs=(P("tgt", "src"), P("src", "tgt"), P("src"), P("tgt"), P("tgt")),
        out_specs=(P("src"), P("tgt"), P("tgt", "src")),
        check_vma=False,
    )
```

```python
import functools
import math

import jax
import jax.numpy as jnp
from jax import lax
from jax.experimental import pallas as pl
from jax.experimental.pallas import tpu as pltpu
from jax.sharding import PartitionSpec as P

ITERS = 3
EPS = 0.1
UNIT = EPS * math.log(2.0)

F32 = jnp.float32
BF16 = jnp.bfloat16
VMEM = pl.BlockSpec(memory_space=pltpu.VMEM)
LANES = 128


def pieces(v):
    a = v.astype(BF16)
    r = v - a.astype(F32)
    b = r.astype(BF16)
    c = (r - b.astype(F32)).astype(BF16)
    return a, b, c


def tree(op, items):
    items = list(items)
    while len(items) > 1:
        half = (len(items) + 1) // 2
        rest = items[half:]
        items = [op(items[k], rest[k]) if k < len(rest) else items[k] for k in range(half)]
    return items[0]


def whole_log_sum(parts_ref):
    parts = [parts_ref[t] for t in range(parts_ref.shape[0])]
    top = tree(jnp.maximum, parts)
    return top + jnp.log2(tree(jnp.add, [jnp.exp2(p - top) for p in parts]))


def rows_log_sum(s_ref, pot, top_ref, sum_ref):
    n, width = s_ref.shape
    cols = width // LANES
    pot8 = jnp.broadcast_to(pot, (8, width))

    def strip(k, _):
        rows = pl.ds(pl.multiple_of(k * 8, 8), 8)
        z = [s_ref[rows, pl.ds(c * LANES, LANES)] + pot8[:, c * LANES : (c + 1) * LANES] for c in range(cols)]
        top = tree(jnp.maximum, z)
        top_ref[rows, :] = top
        sum_ref[rows, :] = tree(jnp.add, [jnp.exp2(v - top) for v in z])
        return 0

    lax.fori_loop(0, n // 8, strip, 0, unroll=4)
    tops = top_ref[...].T
    top = jnp.max(tops, axis=0, keepdims=True)
    total = jnp.sum(sum_ref[...].T * jnp.exp2(tops - top), axis=0, keepdims=True)
    return top + jnp.log2(total)


def across(pot, out_ref):
    n = pot.shape[1]
    out_ref[...] = jnp.broadcast_to(pot, (LANES, n)).T


def cols_log_sum(s_ref, pot_ref):
    n, width = s_ref.shape
    cols = width // LANES

    def load(k):
        rows = pl.ds(pl.multiple_of(k * 8, 8), 8)
        f = pot_ref[rows, :]
        return [s_ref[rows, pl.ds(c * LANES, LANES)] + f for c in range(cols)]

    def find(k, top):
        return tuple(jnp.maximum(t, v) for t, v in zip(top, load(k)))

    top = lax.fori_loop(1, n // 8, find, tuple(load(0)), unroll=4)

    def add(k, total):
        return tuple(a + jnp.exp2(v - t) for a, v, t in zip(total, load(k), top))

    zero = tuple(jnp.zeros((8, LANES), F32) for _ in range(cols))
    total = lax.fori_loop(0, n // 8, add, zero, unroll=4)
    out = []
    for t, a in zip(top, total):
        m = jnp.max(t, axis=0, keepdims=True)
        out.append(m + jnp.log2(jnp.sum(a * jnp.exp2(t - m), axis=0, keepdims=True)))
    return jnp.concatenate(out, axis=1)


def repeat(v, out_ref):
    for t in range(out_ref.shape[0]):
        out_ref[t] = v


def first_kernel(count, me_ref, pot_ref, y_ref, *refs):
    parts, (s_ref, l_ref, xn_ref, yn_ref, yo_ref, xs, xw, yw, top_ref, sum_ref) = refs[:count], refs[count:]
    k = y_ref.shape[0]
    if count == 1:
        x = parts[0][...]
    else:
        for d, part in enumerate(parts):
            xs[lax.rem(me_ref[0] - d + count, count)] = part[...]
        x = jnp.concatenate([xs[t] for t in range(count)], axis=0)
    y = y_ref[...]
    xn = jnp.sum(x * x, axis=0, keepdims=True) / k
    yn = jnp.sum(y * y, axis=0, keepdims=True) / k
    xn_ref[...] = xn
    yn_ref[...] = yn
    x1, x2, x3 = pieces(x)
    y1, y2, y3 = pieces(y * (2.0 / (k * UNIT)))
    for p, (xp, yp) in enumerate(((x1, y1), (x1, y2), (x2, y1), (x2, y2), (x1, y3), (x3, y1))):
        xw[pl.ds(p * k, k), :] = xp
        yw[pl.ds(p * k, k), :] = yp
    yo_ref[pl.ds(0, k), :] = y1
    yo_ref[pl.ds(k, k), :] = y2
    yo_ref[pl.ds(2 * k, 16), :] = jnp.ones((16, y.shape[1]), BF16)
    step = 256

    def block(b, _):
        rows = pl.ds(pl.multiple_of(b * step, step), step)
        s_ref[rows, :] = lax.dot_general(
            xw[:, rows], yw[...], (((0,), (0,)), ((), ())), preferred_element_type=F32
        )
        return 0

    lax.fori_loop(0, s_ref.shape[0] // step, block, 0)
    pot = (pot_ref[...] - yn) * (1.0 / UNIT)
    repeat(rows_log_sum(s_ref, pot, top_ref, sum_ref), l_ref)


def src_kernel(s_ref, mass_ref, parts_ref, f_ref, l_ref, wide):
    f = jnp.log2(mass_ref[...]) - whole_log_sum(parts_ref)
    f_ref[...] = f
    across(f, wide)
    repeat(cols_log_sum(s_ref, wide), l_ref)


def tgt_kernel(s_ref, mass_ref, parts_ref, l_ref, top_ref, sum_ref):
    g = jnp.log2(mass_ref[...]) - whole_log_sum(parts_ref)
    repeat(rows_log_sum(s_ref, g, top_ref, sum_ref), l_ref)


def last_kernel(s_ref, mass_ref, f_ref, xn_ref, yn_ref, yw, parts_ref, sp_ref, tp_ref, out_ref, wide, acc):
    n, width = s_ref.shape
    peers, own = out_ref.shape[0], out_ref.shape[1] - 1
    k = peers * own
    g = jnp.log2(mass_ref[...]) - whole_log_sum(parts_ref)
    f = f_ref[...]
    sp_ref[...] = f * UNIT + xn_ref[...]
    tp_ref[...] = g * UNIT + yn_ref[...]
    across(f, wide)
    step = 128

    def block(b, _):
        rows = pl.ds(pl.multiple_of(b * step, step), step)
        fb = wide[rows, :]
        w = jnp.exp2(s_ref[rows, :] + g + jnp.concatenate([fb] * (width // LANES), axis=1))
        w1 = w.astype(BF16)
        w2 = (w - w1.astype(F32)).astype(BF16)
        dims = (((1,), (1,)), ((), ()))
        one = lax.dot_general(w1, yw[...], dims, preferred_element_type=F32)
        two = lax.dot_general(w2, yw[...], dims, preferred_element_type=F32)
        acc[rows, :] = one + two
        return 0

    lax.fori_loop(0, n // step, block, 0)
    whole = acc[:, : 2 * k].T
    num = (whole[:k, :] + whole[k:, :]) * (k * UNIT / 2.0)
    den = jnp.broadcast_to(acc[:, 2 * k : 2 * k + 1], (n, LANES)).T[0:1, :]
    for t in range(peers):
        out_ref[t, pl.ds(0, own), :] = num[t * own : (t + 1) * own, :]
        out_ref[t, pl.ds(own, 1), :] = den


def join_kernel(parts_ref, out_ref):
    peers, own = parts_ref.shape[0], parts_ref.shape[1] - 1
    num = tree(jnp.add, [parts_ref[t, pl.ds(0, own), :] for t in range(peers)])
    den = tree(jnp.add, [parts_ref[t, pl.ds(own, 1), :] for t in range(peers)])
    out_ref[...] = num / den


def call(kernel, outs, scratch, *args, scalars=0):
    smem = pl.BlockSpec(memory_space=pltpu.SMEM)
    return pl.pallas_call(
        kernel,
        out_shape=[o if isinstance(o, jax.ShapeDtypeStruct) else jax.ShapeDtypeStruct(o, F32) for o in outs],
        in_specs=[smem] * scalars + [VMEM] * (len(args) - scalars),
        out_specs=[VMEM] * len(outs),
        scratch_shapes=scratch,
        compiler_params=pltpu.CompilerParams(vmem_limit_bytes=32 * 2**20),
    )(*args)


def swap(v, axis):
    return lax.all_to_all(v, axis, 0, 0, tiled=True)


def shards(peers_src, peers_tgt, src_pts, tgt_pts, src_mass, tgt_mass, init_pot):
    own = src_pts.shape[0]
    n, width = src_pts.shape[1], tgt_pts.shape[1]
    if own % 8 == 0:
        xs = [src_pts] + [
            lax.ppermute(src_pts, "tgt", [(i, (i + d) % peers_tgt) for i in range(peers_tgt)])
            for d in range(1, peers_tgt)
        ]
    else:
        xs = [lax.all_gather(src_pts, "tgt", axis=0, tiled=True)]
    ys = lax.all_gather(tgt_pts, "src", axis=0, tiled=True)
    k = ys.shape[0]
    src_mass = src_mass.reshape(1, n)
    tgt_mass = tgt_mass.reshape(1, width)
    row, col = (1, n), (1, width)
    rows, cols = (peers_tgt, 1, n), (peers_src, 1, width)
    lane = pltpu.VMEM((n, LANES), F32)
    s, l, xn, yn, yo = call(
        functools.partial(first_kernel, len(xs)),
        [(n, width), rows, row, col, jax.ShapeDtypeStruct((2 * k + 16, width), BF16)],
        [pltpu.VMEM((peers_tgt, own, n), F32), pltpu.VMEM((6 * k, n), BF16), pltpu.VMEM((6 * k, width), BF16), lane, lane],
        lax.axis_index("tgt").astype(jnp.int32).reshape(1),
        init_pot.reshape(1, width),
        ys,
        *xs,
        scalars=1,
    )
    for step in range(ITERS):
        f, l = call(src_kernel, [row, cols], [lane], s, src_mass, swap(l, "tgt"))
        l = swap(l, "src")
        if step < ITERS - 1:
            (l,) = call(tgt_kernel, [rows], [lane, lane], s, tgt_mass, l)
    src_pot, tgt_pot, blocks = call(
        last_kernel,
        [row, col, (peers_tgt, own + 1, n)],
        [lane, pltpu.VMEM((n, 2 * k + 16), F32)],
        s,
        tgt_mass,
        f,
        xn,
        yn,
        yo,
        l,
    )
    (mapped,) = call(join_kernel, [(own, n)], [], swap(blocks, "tgt"))
    return src_pot.reshape(n), tgt_pot.reshape(width), mapped


def solution(mesh):
    return jax.shard_map(
        functools.partial(shards, mesh.shape["src"], mesh.shape["tgt"]),
        mesh=mesh,
        in_specs=(P("tgt", "src"), P("src", "tgt"), P("src"), P("tgt"), P("tgt")),
        out_specs=(P("src"), P("tgt"), P("tgt", "src")),
        check_vma=False,
    )
```

```python
import functools
import math

import jax
import jax.numpy as jnp
from jax import lax
from jax.experimental import pallas as pl
from jax.experimental.pallas import tpu as pltpu
from jax.sharding import PartitionSpec as P

ITERS = 3
EPS = 0.1
UNIT = EPS * math.log(2.0)

F32 = jnp.float32
BF16 = jnp.bfloat16
VMEM = pl.BlockSpec(memory_space=pltpu.VMEM)
LANES = 128


def pieces(v):
    a = v.astype(BF16)
    r = v - a.astype(F32)
    b = r.astype(BF16)
    c = (r - b.astype(F32)).astype(BF16)
    return a, b, c


def tree(op, items):
    items = list(items)
    while len(items) > 1:
        half = (len(items) + 1) // 2
        rest = items[half:]
        items = [op(items[k], rest[k]) if k < len(rest) else items[k] for k in range(half)]
    return items[0]


def whole_log_sum(parts_ref):
    parts = [parts_ref[t] for t in range(parts_ref.shape[0])]
    top = tree(jnp.maximum, parts)
    return top + jnp.log2(tree(jnp.add, [jnp.exp2(p - top) for p in parts]))


def rows_log_sum(s_ref, pot, top_ref, sum_ref):
    n, width = s_ref.shape
    cols = width // LANES
    pot8 = jnp.broadcast_to(pot, (8, width))

    def strip(k, _):
        rows = pl.ds(pl.multiple_of(k * 8, 8), 8)
        z = [s_ref[rows, pl.ds(c * LANES, LANES)] + pot8[:, c * LANES : (c + 1) * LANES] for c in range(cols)]
        top = tree(jnp.maximum, z)
        top_ref[rows, :] = top
        sum_ref[rows, :] = tree(jnp.add, [jnp.exp2(v - top) for v in z])
        return 0

    lax.fori_loop(0, n // 8, strip, 0, unroll=4)
    tops = top_ref[...].T
    top = jnp.max(tops, axis=0, keepdims=True)
    total = jnp.sum(sum_ref[...].T * jnp.exp2(tops - top), axis=0, keepdims=True)
    return top + jnp.log2(total)


def across(pot, out_ref):
    n = pot.shape[1]
    out_ref[...] = jnp.broadcast_to(pot, (LANES, n)).T


def cols_log_sum(s_ref, pot_ref):
    n, width = s_ref.shape
    cols = width // LANES

    def load(k):
        rows = pl.ds(pl.multiple_of(k * 8, 8), 8)
        f = pot_ref[rows, :]
        return [s_ref[rows, pl.ds(c * LANES, LANES)] + f for c in range(cols)]

    def find(k, top):
        return tuple(jnp.maximum(t, v) for t, v in zip(top, load(k)))

    top = lax.fori_loop(1, n // 8, find, tuple(load(0)), unroll=4)

    def add(k, total):
        return tuple(a + jnp.exp2(v - t) for a, v, t in zip(total, load(k), top))

    zero = tuple(jnp.zeros((8, LANES), F32) for _ in range(cols))
    total = lax.fori_loop(0, n // 8, add, zero, unroll=4)
    out = []
    for t, a in zip(top, total):
        m = jnp.max(t, axis=0, keepdims=True)
        out.append(m + jnp.log2(jnp.sum(a * jnp.exp2(t - m), axis=0, keepdims=True)))
    return jnp.concatenate(out, axis=1)


def first_kernel(peers_tgt, xplan, yplan, me_ref, pot_ref, *refs):
    xcount = len(xplan)
    xparts, refs = refs[:xcount], refs[xcount:]
    yparts, (s_ref, l_ref, xn_ref, yn_ref, yo_ref, xs, ys, xw, yw, top_ref, sum_ref) = refs[:-11], refs[-11:]
    k = xs.shape[0]
    me_src, me_tgt = me_ref[0] // peers_tgt, lax.rem(me_ref[0], peers_tgt)
    for parts, plan, me, all_ref in ((xparts, xplan, me_tgt, xs), (yparts, yplan, me_src, ys)):
        for part, owners in zip(parts, plan):
            if owners is None:
                all_ref[...] = part[...]
                continue
            own = part.shape[0] // len(owners)
            for b, d in enumerate(owners):
                rows = pl.ds(pl.multiple_of((me ^ d) * own, 8), own)
                all_ref[rows, :] = part[pl.ds(b * own, own), :]
    x = xs[...]
    y = ys[...]
    xn = jnp.sum(x * x, axis=0, keepdims=True) / k
    yn = jnp.sum(y * y, axis=0, keepdims=True) / k
    xn_ref[...] = xn
    yn_ref[...] = yn
    x1, x2, x3 = pieces(x)
    y1, y2, y3 = pieces(y * (2.0 / (k * UNIT)))
    for p, (xp, yp) in enumerate(((x1, y1), (x1, y2), (x2, y1), (x2, y2), (x1, y3), (x3, y1))):
        xw[pl.ds(p * k, k), :] = xp
        yw[pl.ds(p * k, k), :] = yp
    yo_ref[pl.ds(0, k), :] = y1
    yo_ref[pl.ds(k, k), :] = y2
    yo_ref[pl.ds(2 * k, 16), :] = jnp.ones((16, y.shape[1]), BF16)
    step = 256

    def block(b, _):
        rows = pl.ds(pl.multiple_of(b * step, step), step)
        s_ref[rows, :] = lax.dot_general(
            xw[:, rows], yw[...], (((0,), (0,)), ((), ())), preferred_element_type=F32
        )
        return 0

    lax.fori_loop(0, s_ref.shape[0] // step, block, 0)
    pot = (pot_ref[...] - yn) * (1.0 / UNIT)
    l_ref[...] = rows_log_sum(s_ref, pot, top_ref, sum_ref)


def src_kernel(s_ref, mass_ref, parts_ref, f_ref, l_ref, wide):
    f = jnp.log2(mass_ref[...]) - whole_log_sum(parts_ref)
    f_ref[...] = f
    across(f, wide)
    l_ref[...] = cols_log_sum(s_ref, wide)


def tgt_kernel(s_ref, mass_ref, parts_ref, l_ref, top_ref, sum_ref):
    g = jnp.log2(mass_ref[...]) - whole_log_sum(parts_ref)
    l_ref[...] = rows_log_sum(s_ref, g, top_ref, sum_ref)


def last_kernel(me_ref, s_ref, mass_ref, f_ref, xn_ref, yn_ref, yw, parts_ref, sp_ref, tp_ref, *refs):
    outs, (wide, acc, flat) = refs[:-3], refs[-3:]
    n, width = s_ref.shape
    peers, own = len(outs), outs[0].shape[0] - 1
    k = peers * own
    g = jnp.log2(mass_ref[...]) - whole_log_sum(parts_ref)
    f = f_ref[...]
    sp_ref[...] = f * UNIT + xn_ref[...]
    tp_ref[...] = g * UNIT + yn_ref[...]
    across(f, wide)
    step = 128

    def block(b, _):
        rows = pl.ds(pl.multiple_of(b * step, step), step)
        fb = wide[rows, :]
        w = jnp.exp2(s_ref[rows, :] + g + jnp.concatenate([fb] * (width // LANES), axis=1))
        w1 = w.astype(BF16)
        w2 = (w - w1.astype(F32)).astype(BF16)
        dims = (((1,), (1,)), ((), ()))
        one = lax.dot_general(w1, yw[...], dims, preferred_element_type=F32)
        two = lax.dot_general(w2, yw[...], dims, preferred_element_type=F32)
        acc[rows, :] = one + two
        return 0

    lax.fori_loop(0, n // step, block, 0)
    whole = acc[:, : 2 * k].T
    num = (whole[:k, :] + whole[k:, :]) * (k * UNIT / 2.0)
    den = jnp.broadcast_to(acc[:, 2 * k : 2 * k + 1], (n, LANES)).T[0:1, :]
    for t in range(peers):
        flat[t] = num[t * own : (t + 1) * own, :]
    for d, out in enumerate(outs):
        out[pl.ds(0, own), :] = flat[lax.rem(me_ref[0], peers) ^ d]
        out[pl.ds(own, 1), :] = den


def join_kernel(*refs):
    parts, out_ref = refs[:-1], refs[-1]
    own = out_ref.shape[0]
    num = tree(jnp.add, [p[pl.ds(0, own), :] for p in parts])
    den = tree(jnp.add, [p[pl.ds(own, 1), :] for p in parts])
    out_ref[...] = num / den


def call(kernel, outs, scratch, *args, scalars=0):
    smem = pl.BlockSpec(memory_space=pltpu.SMEM)
    return pl.pallas_call(
        kernel,
        out_shape=[o if isinstance(o, jax.ShapeDtypeStruct) else jax.ShapeDtypeStruct(o, F32) for o in outs],
        in_specs=[smem] * scalars + [VMEM] * (len(args) - scalars),
        out_specs=[VMEM] * len(outs),
        scratch_shapes=scratch,
        compiler_params=pltpu.CompilerParams(vmem_limit_bytes=32 * 2**20),
    )(*args)


def everyone(v, axis):
    return lax.all_gather(v, axis, axis=0, tiled=False)


def flip(v, axis, size, bit):
    return lax.ppermute(v, axis, [(i, i ^ bit) for i in range(size)])


def gather(v, axis, size, pair):
    if v.shape[0] % 8 or size & (size - 1):
        return [lax.all_gather(v, axis, axis=0, tiled=True)], [None]
    step = 2 if pair else 1
    blocks = [v] + [flip(v, axis, size, d) for d in range(step, size, step)]
    order = list(range(0, size, step))
    if not pair:
        return blocks, [[d] for d in order]
    mine = jnp.concatenate(blocks, axis=0)
    return [mine, flip(mine, axis, size, 1)], [order, [d + 1 for d in order]]


def shards(peers_src, peers_tgt, src_pts, tgt_pts, src_mass, tgt_mass, init_pot):
    own = src_pts.shape[0]
    n, width = src_pts.shape[1], tgt_pts.shape[1]
    ys, yplan = gather(tgt_pts, "src", peers_src, True)
    xs, xplan = gather(src_pts, "tgt", peers_tgt, False)
    k = own * peers_tgt
    me = lax.axis_index(("src", "tgt")).astype(jnp.int32).reshape(1)
    src_mass = src_mass.reshape(1, n)
    tgt_mass = tgt_mass.reshape(1, width)
    row, col = (1, n), (1, width)
    lane = pltpu.VMEM((n, LANES), F32)
    s, l, xn, yn, yo = call(
        functools.partial(first_kernel, peers_tgt, xplan, yplan),
        [(n, width), row, row, col, jax.ShapeDtypeStruct((2 * k + 16, width), BF16)],
        [
            pltpu.VMEM((k, n), F32),
            pltpu.VMEM((k, width), F32),
            pltpu.VMEM((6 * k, n), BF16),
            pltpu.VMEM((6 * k, width), BF16),
            lane,
            lane,
        ],
        me,
        init_pot.reshape(1, width),
        *xs,
        *ys,
        scalars=1,
    )
    for step in range(ITERS):
        f, l = call(src_kernel, [row, col], [lane], s, src_mass, everyone(l, "tgt"))
        l = everyone(l, "src")
        if step < ITERS - 1:
            (l,) = call(tgt_kernel, [row], [lane, lane], s, tgt_mass, l)
    src_pot, tgt_pot, *blocks = call(
        last_kernel,
        [row, col] + [(own + 1, n)] * peers_tgt,
        [lane, pltpu.VMEM((n, 2 * k + 16), F32), pltpu.VMEM((peers_tgt, own, n), F32)],
        me,
        s,
        tgt_mass,
        f,
        xn,
        yn,
        yo,
        l,
        scalars=1,
    )
    came = [blocks[0]] + [flip(blocks[d], "tgt", peers_tgt, d) for d in range(1, peers_tgt)]
    (mapped,) = call(join_kernel, [(own, n)], [], *came)
    return src_pot.reshape(n), tgt_pot.reshape(width), mapped


def solution(mesh):
    return jax.shard_map(
        functools.partial(shards, mesh.shape["src"], mesh.shape["tgt"]),
        mesh=mesh,
        in_specs=(P("tgt", "src"), P("src", "tgt"), P("src"), P("tgt"), P("tgt")),
        out_specs=(P("src"), P("tgt"), P("tgt", "src")),
        check_vma=False,
    )
```

```python
import functools
import math

import jax
import jax.numpy as jnp
from jax import lax
from jax.experimental import pallas as pl
from jax.experimental.pallas import tpu as pltpu
from jax.sharding import PartitionSpec as P

ITERS = 3
EPS = 0.1
UNIT = EPS * math.log(2.0)
LOW = 2.0**-40
HIGH = 2.0**20

F32 = jnp.float32
BF16 = jnp.bfloat16
VMEM = pl.BlockSpec(memory_space=pltpu.VMEM)
SMEM = pl.BlockSpec(memory_space=pltpu.SMEM)
HBM = pl.BlockSpec(memory_space=pltpu.HBM)
LANES = 128


def pieces(v):
    a = v.astype(BF16)
    r = v - a.astype(F32)
    b = r.astype(BF16)
    c = (r - b.astype(F32)).astype(BF16)
    return a, b, c


def tree(op, items):
    items = list(items)
    while len(items) > 1:
        half = (len(items) + 1) // 2
        rest = items[half:]
        items = [op(items[k], rest[k]) if k < len(rest) else items[k] for k in range(half)]
    return items[0]


def whole_log_sum(part_refs):
    if len(part_refs) == 1:
        parts = [part_refs[0][t] for t in range(part_refs[0].shape[0])]
    else:
        parts = [p[0] for p in part_refs]
    top = tree(jnp.maximum, parts)
    return top + jnp.log2(tree(jnp.add, [jnp.exp2(p - top) for p in parts]))


def to_row(wide):
    split = jnp.concatenate(pieces(wide), axis=1)
    ones = jnp.ones((16, split.shape[1]), BF16)
    return lax.dot_general(ones, split, (((1,), (1,)), ((), ())), preferred_element_type=F32)[0:1, :]


def across(row, out_ref):
    n = row.shape[1]
    a, b, c = [p.astype(F32) for p in pieces(row)]
    at = lax.broadcasted_iota(jnp.int32, (16, n), 0)
    split = jnp.where(at == 0, a, jnp.where(at == 1, b, jnp.where(at == 2, c, 0.0))).astype(BF16)
    ones = jnp.ones((16, LANES), BF16)
    out_ref[...] = lax.dot_general(split, ones, (((0,), (0,)), ((), ())), preferred_element_type=F32)


def eight(k):
    return pl.ds(pl.multiple_of(k * 8, 8), 8)


def chunk(c):
    return pl.ds(c * LANES, LANES)


def lanes_log_sum(s_ref, rows, pot8, top_ref, sum_ref):
    cols = s_ref.shape[1] // LANES
    z = [s_ref[rows, chunk(c)] + pot8[:, c * LANES : (c + 1) * LANES] for c in range(cols)]
    top = tree(jnp.maximum, z)
    top_ref[rows, :] = top
    sum_ref[rows, :] = tree(jnp.add, [jnp.exp2(v - top) for v in z])


def join_lanes(top_ref, sum_ref):
    def strip(k, _):
        rows = eight(k)
        part = top_ref[rows, :]
        top = jnp.broadcast_to(jnp.max(part, axis=1, keepdims=True), part.shape)
        sum_ref[rows, :] = sum_ref[rows, :] * jnp.exp2(part - top)
        top_ref[rows, :] = top * (1.0 / LANES)
        return 0

    lax.fori_loop(0, top_ref.shape[0] // 8, strip, 0, unroll=16)
    return to_row(top_ref[...]) + jnp.log2(to_row(sum_ref[...]))


def rows_log_sum(s_ref, pot, top_ref, sum_ref):
    n, width = s_ref.shape
    pot8 = jnp.broadcast_to(pot, (8, width))

    def strip(k, _):
        lanes_log_sum(s_ref, eight(k), pot8, top_ref, sum_ref)
        return 0

    lax.fori_loop(0, n // 8, strip, 0, unroll=4)
    return join_lanes(top_ref, sum_ref)


def cols_log_sum(s_ref, pot_ref):
    n, width = s_ref.shape
    cols = width // LANES

    def load(k):
        rows = eight(k)
        f = pot_ref[rows, :]
        return [s_ref[rows, chunk(c)] + f for c in range(cols)]

    def find(k, top):
        return tuple(jnp.maximum(t, v) for t, v in zip(top, load(k)))

    top = lax.fori_loop(1, n // 8, find, tuple(load(0)), unroll=4)

    def add(k, total):
        return tuple(a + jnp.exp2(v - t) for a, v, t in zip(total, load(k), top))

    zero = tuple(jnp.zeros((8, LANES), F32) for _ in range(cols))
    total = lax.fori_loop(0, n // 8, add, zero, unroll=4)
    out = []
    for t, a in zip(top, total):
        m = jnp.max(t, axis=0, keepdims=True)
        out.append(m + jnp.log2(jnp.sum(a * jnp.exp2(t - m), axis=0, keepdims=True)))
    return jnp.concatenate(out, axis=1)


def repeat(row, out_ref):
    for t in range(out_ref.shape[0]):
        out_ref[t] = row


def early_kernel(sm_ref, tm_ref, pot_ref, x_ref, ls_ref, lt_ref, to_ref, xo_ref):
    ls_ref[...] = jnp.log2(sm_ref[...])
    lt_ref[...] = jnp.log2(tm_ref[...])
    to_ref[...] = pot_ref[...]
    xo_ref[...] = x_ref[...]


def first_kernel(peers, xplan, yplan, me_ref, pot_ref, *refs):
    xcount, ycount = len(xplan), len(yplan)
    xparts, yparts, refs = refs[:xcount], refs[xcount : xcount + ycount], refs[xcount + ycount :]
    s_ref, l_ref, xn_ref, yn_ref, yo_ref, xs, xw, yw, top_ref, sum_ref = refs
    k = xs.shape[0]
    me_src, me_tgt = me_ref[0] // peers, lax.rem(me_ref[0], peers)
    for part, owners in zip(yparts, yplan):
        if owners is None:
            yo_ref[...] = part[...]
            continue
        own = part.shape[0] // len(owners)
        for b, d in enumerate(owners):
            yo_ref[pl.ds(pl.multiple_of((me_src ^ d) * own, 8), own), :] = part[pl.ds(b * own, own), :]
    for part, d in zip(xparts, xplan):
        if d is None:
            xs[...] = part[...]
            continue
        own = part.shape[0]
        xs[pl.ds(pl.multiple_of(lax.rem(me_tgt - d + peers, peers) * own, 8), own), :] = part[...]
    y = yo_ref[...]
    yn = jnp.sum(y * y, axis=0, keepdims=True) / k
    yn_ref[...] = yn
    y1, y2, y3 = pieces(y * (2.0 / (k * UNIT)))
    x = xs[...]
    xn_ref[...] = jnp.sum(x * x, axis=0, keepdims=True) / k
    x1, x2, x3 = pieces(x)
    for p, (xp, yp) in enumerate(((x1, y1), (x1, y2), (x2, y1), (x2, y2), (x1, y3), (x3, y1))):
        xw[pl.ds(p * k, k), :] = xp
        yw[pl.ds(p * k, k), :] = yp
    n, width = s_ref.shape
    pot8 = jnp.broadcast_to((pot_ref[...] - yn) * (1.0 / UNIT), (8, width))
    step = 256
    for b in range(n // step + 1):
        if b < n // step:
            s_ref[pl.ds(b * step, step), :] = lax.dot_general(
                xw[:, pl.ds(b * step, step)], yw[...], (((0,), (0,)), ((), ())), preferred_element_type=F32
            )
        if b > 0:
            for r in range((b - 1) * step, b * step, 8):
                lanes_log_sum(s_ref, pl.ds(r, 8), pot8, top_ref, sum_ref)
    l_ref[0] = join_lanes(top_ref, sum_ref)


def src_first_kernel(count, s_ref, mass_ref, *refs):
    parts, (f_ref, wide_ref, l_ref) = refs[:count], refs[count:]
    f = mass_ref[...] - whole_log_sum(parts)
    f_ref[...] = f
    across(f, wide_ref)
    repeat(cols_log_sum(s_ref, wide_ref), l_ref)


def tgt_first_kernel(count, s_ref, mass_ref, f_ref, wide_ref, *refs):
    parts, (g_ref, p_ref, l_ref, top_ref, sum_ref) = refs[:count], refs[count:]
    n, width = s_ref.shape
    g = mass_ref[...] - whole_log_sum(parts)
    g_ref[...] = g
    g8 = jnp.broadcast_to(g, (8, width))

    def strip(k, _):
        rows = eight(k)
        f = wide_ref[rows, :]
        out = []
        for c in range(width // LANES):
            p = jnp.exp2((s_ref[rows, chunk(c)] + f) + g8[:, c * LANES : (c + 1) * LANES])
            p_ref[rows, chunk(c)] = p
            out.append(p)
        sum_ref[rows, :] = tree(jnp.add, out)
        return 0

    lax.fori_loop(0, n // 8, strip, 0, unroll=4)
    total = to_row(sum_ref[...])
    l_ref[0] = jnp.log2(total)

    @pl.when(jnp.logical_not(jnp.min(total) >= LOW))
    def _():
        l_ref[0] = f_ref[...] + rows_log_sum(s_ref, g, top_ref, sum_ref)


def src_kernel(count, s_ref, p_ref, mass_ref, f_ref, g_ref, *refs):
    parts, (u_ref, l_ref, wide) = refs[:count], refs[count:]
    n, width = p_ref.shape
    cols = width // LANES
    change = mass_ref[...] - whole_log_sum(parts)
    u_ref[...] = change
    u = jnp.exp2(change)
    across(u, wide)

    def add(k, total):
        rows = eight(k)
        f = wide[rows, :]
        return tuple(a + p_ref[rows, chunk(c)] * f for c, a in enumerate(total))

    zero = tuple(jnp.zeros((8, LANES), F32) for _ in range(cols))
    parts = lax.fori_loop(0, n // 8, add, zero, unroll=4)
    total = jnp.concatenate([jnp.sum(a, axis=0, keepdims=True) for a in parts], axis=1)
    repeat(jnp.log2(total), l_ref)
    fine = jnp.logical_and(jnp.min(total) >= LOW, jnp.max(u) <= HIGH)

    @pl.when(jnp.logical_not(fine))
    def _():
        across(f_ref[...] + change, wide)
        repeat(g_ref[...] + cols_log_sum(s_ref, wide), l_ref)


def tgt_kernel(count, s_ref, p_ref, mass_ref, f_ref, g_ref, *refs):
    parts, (l_ref, top_ref, sum_ref) = refs[:count], refs[count:]
    n, width = p_ref.shape
    change = mass_ref[...] - whole_log_sum(parts)
    v = jnp.exp2(change)
    v8 = jnp.broadcast_to(v, (8, width))

    def strip(k, _):
        rows = eight(k)
        sum_ref[rows, :] = tree(
            jnp.add, [p_ref[rows, chunk(c)] * v8[:, c * LANES : (c + 1) * LANES] for c in range(width // LANES)]
        )
        return 0

    lax.fori_loop(0, n // 8, strip, 0, unroll=4)
    total = to_row(sum_ref[...])
    l_ref[0] = jnp.log2(total)
    fine = jnp.logical_and(jnp.min(total) >= LOW, jnp.max(v) <= HIGH)

    @pl.when(jnp.logical_not(fine))
    def _():
        l_ref[0] = f_ref[...] + rows_log_sum(s_ref, g_ref[...] + change, top_ref, sum_ref)


def last_kernel(count, me_ref, s_ref, p_ref, mass_ref, f_ref, g_ref, u_ref, xn_ref, yn_ref, y_ref, *refs):
    parts, refs = refs[:count], refs[count:]
    sp_any, tp_any, outs = refs[0], refs[1], refs[2:-7]
    sp, tp, yw, acc, flat, wide, sem = refs[-7:]
    k = y_ref.shape[0]
    n, width = s_ref.shape
    peers = len(outs)
    own = k // peers
    change = mass_ref[...] - whole_log_sum(parts)
    g = g_ref[...] + change
    f = f_ref[...] + u_ref[...]
    sp[...] = f * UNIT + xn_ref[...]
    tp[...] = g * UNIT + yn_ref[...]
    copies = [pltpu.make_async_copy(sp, sp_any, sem.at[0]), pltpu.make_async_copy(tp, tp_any, sem.at[1])]
    for copy in copies:
        copy.start()
    u = jnp.exp2(u_ref[...])
    v = jnp.exp2(change)
    step = 256

    def project(weight, scale, rescale):
        y1, y2, _ = pieces(y_ref[...] * scale)
        s1, s2, _ = [p.astype(F32) for p in pieces(scale)]
        yw[pl.ds(0, k), :] = y1
        at = lax.broadcasted_iota(jnp.int32, (LANES - k, width), 0)
        yw[pl.ds(k, LANES - k), :] = jnp.where(at == 0, s1, jnp.where(at == 1, s2, 0.0)).astype(BF16)
        yw[pl.ds(LANES, k), :] = y2
        yw[pl.ds(LANES + k, LANES - k), :] = jnp.zeros((LANES - k, width), BF16)
        for b in range(n // step):
            w = weight(pl.ds(b * step, step))
            w1 = w.astype(BF16)
            w2 = (w - w1.astype(F32)).astype(BF16)
            dims = (((1,), (1,)), ((), ()))
            out = lax.dot_general(w1, yw[...], dims, preferred_element_type=F32) + lax.dot_general(
                w2, yw[...], dims, preferred_element_type=F32
            )
            acc[pl.ds(b * step, step), :] = out[:, :LANES] + out[:, LANES:]
        total = acc[...].T * rescale
        den = total[k : k + 1, :] + total[k + 1 : k + 2, :]
        for t in range(peers):
            flat[t] = total[t * own : (t + 1) * own, :]
        for d, out in enumerate(outs):
            out[pl.ds(0, own), :] = flat[lax.rem(me_ref[0] + d, peers)]
            out[pl.ds(own, 1), :] = den
        return den

    den = project(lambda rows: p_ref[rows, :], v, u)
    fine = jnp.logical_and(jnp.min(den) >= LOW, jnp.logical_and(jnp.max(u) <= HIGH, jnp.max(v) <= HIGH))

    @pl.when(jnp.logical_not(fine))
    def _():
        across(f, wide)

        def weight(rows):
            fb = jnp.concatenate([wide[rows, :]] * (width // LANES), axis=1)
            return jnp.exp2((s_ref[rows, :] + fb) + g)

        project(weight, jnp.ones_like(v), jnp.ones_like(u))

    for copy in copies:
        copy.wait()


def join_kernel(*refs):
    parts, out_ref = refs[:-1], refs[-1]
    own = out_ref.shape[0]
    num = tree(jnp.add, [p[pl.ds(0, own), :] for p in parts])
    den = tree(jnp.add, [p[pl.ds(own, 1), :] for p in parts])
    out_ref[...] = num / den


def call(kernel, outs, scratch, ins, out_specs=None):
    return pl.pallas_call(
        kernel,
        out_shape=[jax.ShapeDtypeStruct(o, F32) for o in outs],
        in_specs=[spec for spec, _ in ins],
        out_specs=out_specs or [VMEM] * len(outs),
        scratch_shapes=scratch,
        compiler_params=pltpu.CompilerParams(vmem_limit_bytes=20 * 2**20),
    )(*[a for _, a in ins])


def put(*arrays):
    return [(VMEM, a) for a in arrays]


def turn(v, axis, size, d):
    return lax.ppermute(v, axis, [(i, (i + d) % size) for i in range(size)])


def flip(v, axis, size, bit):
    return lax.ppermute(v, axis, [(i, i ^ bit) for i in range(size)])


def few(size):
    return size <= 4


def everyone(v, axis, size):
    if few(size):
        return [v] + [turn(v, axis, size, d) for d in range(1, size)]
    return [lax.all_to_all(v, axis, 0, 0, tiled=True)]


def copies_of(size):
    return 1 if few(size) else size


def gather_src(v, size):
    if v.shape[0] % 8 or not few(size):
        return [lax.all_gather(v, "tgt", axis=0, tiled=True)], [None]
    return [v] + [turn(v, "tgt", size, d) for d in range(1, size)], list(range(size))


def gather_tgt(v, size, other):
    if v.shape[0] % 8 or size & (size - 1):
        return [lax.all_gather(v, "src", axis=0, tiled=True)], [None], other
    order = list(range(0, size, 2))
    mine = jnp.concatenate([v] + [flip(v, "src", size, d) for d in order[1:]], axis=0)
    mine, *early = lax.optimization_barrier([mine] + other[:-1])
    other = early + other[-1:]
    return [mine, flip(mine, "src", size, 1)], [order, [d + 1 for d in order]], other


def shards(peers_src, peers_tgt, src_pts, tgt_pts, src_mass, tgt_mass, init_pot):
    own = src_pts.shape[0]
    n, width = src_pts.shape[1], tgt_pts.shape[1]
    k = own * peers_tgt
    xs, xplan = gather_src(src_pts, peers_tgt)
    row, col = (1, n), (1, width)
    early = call(
        early_kernel,
        [row, col, col, src_pts.shape],
        [],
        put(src_mass.reshape(row), tgt_mass.reshape(col), init_pot.reshape(col), src_pts),
    )
    sm, tm, pot, x = early
    if xplan[0] is not None:
        xs[0] = x
    ys, yplan, (sm, tm, pot, *xs) = gather_tgt(tgt_pts, peers_src, [sm, tm, pot] + xs)
    me = lax.axis_index(("src", "tgt")).astype(jnp.int32).reshape(1)
    rows, cols = (copies_of(peers_tgt), 1, n), (copies_of(peers_src), 1, width)
    lane = pltpu.VMEM((n, LANES), F32)
    s, l, xn, yn, yo = call(
        functools.partial(first_kernel, peers_tgt, xplan, yplan),
        [(n, width), rows, row, col, (k, width)],
        [
            pltpu.VMEM((k, n), F32),
            pltpu.VMEM((6 * k, n), BF16),
            pltpu.VMEM((6 * k, width), BF16),
            lane,
            lane,
        ],
        [(SMEM, me)] + put(pot, *xs, *ys),
    )
    parts = everyone(l, "tgt", peers_tgt)
    f, wide, l = call(
        functools.partial(src_first_kernel, len(parts)), [row, (n, LANES), cols], [], put(s, sm, *parts)
    )
    parts = everyone(l, "src", peers_src)
    g, p, l = call(
        functools.partial(tgt_first_kernel, len(parts)),
        [col, (n, width), rows],
        [lane, lane],
        put(s, tm, f, wide, *parts),
    )
    for step in range(1, ITERS):
        parts = everyone(l, "tgt", peers_tgt)
        u, l = call(functools.partial(src_kernel, len(parts)), [row, cols], [lane], put(s, p, sm, f, g, *parts))
        parts = everyone(l, "src", peers_src)
        if step < ITERS - 1:
            (l,) = call(functools.partial(tgt_kernel, len(parts)), [rows], [lane, lane], put(s, p, tm, f, g, *parts))
    src_pot, tgt_pot, *blocks = call(
        functools.partial(last_kernel, len(parts)),
        [row, col] + [(own + 1, n)] * peers_tgt,
        [
            pltpu.VMEM(row, F32),
            pltpu.VMEM(col, F32),
            pltpu.VMEM((2 * LANES, width), BF16),
            lane,
            pltpu.VMEM((peers_tgt, own, n), F32),
            lane,
            pltpu.SemaphoreType.DMA((2,)),
        ],
        [(SMEM, me)] + put(s, p, tm, f, g, u, xn, yn, yo, *parts),
        [HBM, HBM] + [VMEM] * peers_tgt,
    )
    came = [blocks[0]] + [turn(blocks[d], "tgt", peers_tgt, d) for d in range(1, peers_tgt)]
    (mapped,) = call(join_kernel, [(own, n)], [], put(*came))
    return src_pot.reshape(n), tgt_pot.reshape(width), mapped


def solution(mesh):
    return jax.shard_map(
        functools.partial(shards, mesh.shape["src"], mesh.shape["tgt"]),
        mesh=mesh,
        in_specs=(P("tgt", "src"), P("src", "tgt"), P("src"), P("tgt"), P("tgt")),
        out_specs=(P("src"), P("tgt"), P("tgt", "src")),
        check_vma=False,
    )
```

```python
import functools
import math

import jax
import jax.numpy as jnp
from jax import lax
from jax.experimental import pallas as pl
from jax.experimental.pallas import tpu as pltpu
from jax.sharding import PartitionSpec as P

ITERS = 3
EPS = 0.1
UNIT = EPS * math.log(2.0)
LOW = 2.0**-40
HIGH = 2.0**20

F32 = jnp.float32
BF16 = jnp.bfloat16
VMEM = pl.BlockSpec(memory_space=pltpu.VMEM)
SMEM = pl.BlockSpec(memory_space=pltpu.SMEM)
HBM = pl.BlockSpec(memory_space=pltpu.HBM)
LANES = 128


def pieces(v):
    a = v.astype(BF16)
    r = v - a.astype(F32)
    b = r.astype(BF16)
    c = (r - b.astype(F32)).astype(BF16)
    return a, b, c


def tree(op, items):
    items = list(items)
    while len(items) > 1:
        half = (len(items) + 1) // 2
        rest = items[half:]
        items = [op(items[k], rest[k]) if k < len(rest) else items[k] for k in range(half)]
    return items[0]


def whole_log_sum(part_refs):
    if len(part_refs) == 1:
        parts = [part_refs[0][t] for t in range(part_refs[0].shape[0])]
    else:
        parts = [p[0] for p in part_refs]
    top = tree(jnp.maximum, parts)
    return top + jnp.log2(tree(jnp.add, [jnp.exp2(p - top) for p in parts]))


def to_row(wide):
    split = jnp.concatenate(pieces(wide), axis=1)
    ones = jnp.ones((16, split.shape[1]), BF16)
    return lax.dot_general(ones, split, (((1,), (1,)), ((), ())), preferred_element_type=F32)[0:1, :]


def across(row, out_ref):
    n = row.shape[1]
    a, b, c = [p.astype(F32) for p in pieces(row)]
    at = lax.broadcasted_iota(jnp.int32, (16, n), 0)
    split = jnp.where(at == 0, a, jnp.where(at == 1, b, jnp.where(at == 2, c, 0.0))).astype(BF16)
    ones = jnp.ones((16, LANES), BF16)
    out_ref[...] = lax.dot_general(split, ones, (((0,), (0,)), ((), ())), preferred_element_type=F32)


def eight(k):
    return pl.ds(pl.multiple_of(k * 8, 8), 8)


def chunk(c):
    return pl.ds(c * LANES, LANES)


def lanes_log_sum(s_ref, rows, pot8, top_ref, sum_ref):
    cols = s_ref.shape[1] // LANES
    z = [s_ref[rows, chunk(c)] + pot8[:, c * LANES : (c + 1) * LANES] for c in range(cols)]
    top = tree(jnp.maximum, z)
    top_ref[rows, :] = top
    sum_ref[rows, :] = tree(jnp.add, [jnp.exp2(v - top) for v in z])


def join_lanes(top_ref, sum_ref):
    def strip(k, _):
        rows = eight(k)
        part = top_ref[rows, :]
        top = jnp.broadcast_to(jnp.max(part, axis=1, keepdims=True), part.shape)
        sum_ref[rows, :] = sum_ref[rows, :] * jnp.exp2(part - top)
        top_ref[rows, :] = top * (1.0 / LANES)
        return 0

    lax.fori_loop(0, top_ref.shape[0] // 8, strip, 0, unroll=16)
    return to_row(top_ref[...]) + jnp.log2(to_row(sum_ref[...]))


def rows_log_sum(s_ref, pot, top_ref, sum_ref):
    n, width = s_ref.shape
    pot8 = jnp.broadcast_to(pot, (8, width))

    def strip(k, _):
        lanes_log_sum(s_ref, eight(k), pot8, top_ref, sum_ref)
        return 0

    lax.fori_loop(0, n // 8, strip, 0, unroll=4)
    return join_lanes(top_ref, sum_ref)


def cols_log_sum(s_ref, pot_ref):
    n, width = s_ref.shape
    cols = width // LANES

    def load(k):
        rows = eight(k)
        f = pot_ref[rows, :]
        return [s_ref[rows, chunk(c)] + f for c in range(cols)]

    def find(k, top):
        return tuple(jnp.maximum(t, v) for t, v in zip(top, load(k)))

    top = lax.fori_loop(1, n // 8, find, tuple(load(0)), unroll=4)

    def add(k, total):
        return tuple(a + jnp.exp2(v - t) for a, v, t in zip(total, load(k), top))

    zero = tuple(jnp.zeros((8, LANES), F32) for _ in range(cols))
    total = lax.fori_loop(0, n // 8, add, zero, unroll=4)
    out = []
    for t, a in zip(top, total):
        m = jnp.max(t, axis=0, keepdims=True)
        out.append(m + jnp.log2(jnp.sum(a * jnp.exp2(t - m), axis=0, keepdims=True)))
    return jnp.concatenate(out, axis=1)


def repeat(row, out_ref):
    for t in range(out_ref.shape[0]):
        out_ref[t] = row


def early_kernel(peers, xplan, me_ref, mass_ref, pot_ref, *refs):
    parts, (ls_ref, to_ref, xn_ref, xt_ref, xs, xw) = refs[: len(xplan)], refs[len(xplan) :]
    k = xs.shape[0]
    ls_ref[...] = jnp.log2(mass_ref[...])
    to_ref[...] = pot_ref[...]
    me = lax.rem(me_ref[0], peers)
    for part, d in zip(parts, xplan):
        if d is None:
            xs[...] = part[...]
            continue
        own = part.shape[0]
        xs[pl.ds(pl.multiple_of(lax.rem(me - d + peers, peers) * own, 8), own), :] = part[...]
    x = xs[...]
    xn_ref[...] = jnp.sum(x * x, axis=0, keepdims=True) / k
    x1, x2, x3 = pieces(x)
    for p, piece in enumerate((x1, x1, x2, x2, x1, x3)):
        xw[pl.ds(p * k, k), :] = piece
    xt_ref[...] = xw[...].T


def first_kernel(peers, yplan, me_ref, pot_ref, xt_ref, *refs):
    ycount = len(yplan)
    yparts, (s_ref, l_ref, yn_ref, yo_ref, yw, top_ref, sum_ref) = refs[:ycount], refs[ycount:]
    me = me_ref[0] // peers
    for part, owners in zip(yparts, yplan):
        if owners is None:
            yo_ref[...] = part[...]
            continue
        own = part.shape[0] // len(owners)
        for b, d in enumerate(owners):
            yo_ref[pl.ds(pl.multiple_of((me ^ d) * own, 8), own), :] = part[pl.ds(b * own, own), :]
    y = yo_ref[...]
    yn = jnp.sum(y * y, axis=0, keepdims=True) / y.shape[0]
    yn_ref[...] = yn
    k = y.shape[0]
    y1, y2, y3 = pieces(y * (2.0 / (k * UNIT)))
    for p, piece in enumerate((y1, y2, y1, y2, y3, y1)):
        yw[pl.ds(p * k, k), :] = piece
    n, width = s_ref.shape
    pot8 = jnp.broadcast_to((pot_ref[...] - yn) * (1.0 / UNIT), (8, width))
    step = 256
    for b in range(n // step + 1):
        if b < n // step:
            s_ref[pl.ds(b * step, step), :] = jnp.dot(
                xt_ref[pl.ds(b * step, step), :], yw[...], preferred_element_type=F32
            )
        if b > 0:
            for r in range((b - 1) * step, b * step, 8):
                lanes_log_sum(s_ref, pl.ds(r, 8), pot8, top_ref, sum_ref)
    l_ref[0] = join_lanes(top_ref, sum_ref)


def src_first_kernel(count, s_ref, mass_ref, *refs):
    parts, (f_ref, wide_ref, l_ref) = refs[:count], refs[count:]
    f = mass_ref[...] - whole_log_sum(parts)
    f_ref[...] = f
    across(f, wide_ref)
    repeat(cols_log_sum(s_ref, wide_ref), l_ref)


def tgt_first_kernel(count, s_ref, mass_ref, f_ref, wide_ref, *refs):
    parts, (g_ref, p_ref, l_ref, top_ref, sum_ref) = refs[:count], refs[count:]
    n, width = s_ref.shape
    g = jnp.log2(mass_ref[...]) - whole_log_sum(parts)
    g_ref[...] = g
    g8 = jnp.broadcast_to(g, (8, width))

    def strip(k, _):
        rows = eight(k)
        f = wide_ref[rows, :]
        out = []
        for c in range(width // LANES):
            p = jnp.exp2((s_ref[rows, chunk(c)] + f) + g8[:, c * LANES : (c + 1) * LANES])
            p_ref[rows, chunk(c)] = p
            out.append(p)
        sum_ref[rows, :] = tree(jnp.add, out)
        return 0

    lax.fori_loop(0, n // 8, strip, 0, unroll=4)
    total = to_row(sum_ref[...])
    l_ref[0] = jnp.log2(total)

    @pl.when(jnp.logical_not(jnp.min(total) >= LOW))
    def _():
        l_ref[0] = f_ref[...] + rows_log_sum(s_ref, g, top_ref, sum_ref)


def src_kernel(count, s_ref, p_ref, mass_ref, f_ref, g_ref, *refs):
    parts, (u_ref, l_ref, wide) = refs[:count], refs[count:]
    n, width = p_ref.shape
    cols = width // LANES
    change = mass_ref[...] - whole_log_sum(parts)
    u_ref[...] = change
    u = jnp.exp2(change)
    across(u, wide)

    def add(k, total):
        rows = eight(k)
        f = wide[rows, :]
        return tuple(a + p_ref[rows, chunk(c)] * f for c, a in enumerate(total))

    zero = tuple(jnp.zeros((8, LANES), F32) for _ in range(cols))
    parts = lax.fori_loop(0, n // 8, add, zero, unroll=4)
    total = jnp.concatenate([jnp.sum(a, axis=0, keepdims=True) for a in parts], axis=1)
    repeat(jnp.log2(total), l_ref)
    fine = jnp.logical_and(jnp.min(total) >= LOW, jnp.max(u) <= HIGH)

    @pl.when(jnp.logical_not(fine))
    def _():
        across(f_ref[...] + change, wide)
        repeat(g_ref[...] + cols_log_sum(s_ref, wide), l_ref)


def tgt_kernel(count, s_ref, p_ref, mass_ref, f_ref, g_ref, *refs):
    parts, (l_ref, top_ref, sum_ref) = refs[:count], refs[count:]
    n, width = p_ref.shape
    change = jnp.log2(mass_ref[...]) - whole_log_sum(parts)
    v = jnp.exp2(change)
    v8 = jnp.broadcast_to(v, (8, width))

    def strip(k, _):
        rows = eight(k)
        sum_ref[rows, :] = tree(
            jnp.add, [p_ref[rows, chunk(c)] * v8[:, c * LANES : (c + 1) * LANES] for c in range(width // LANES)]
        )
        return 0

    lax.fori_loop(0, n // 8, strip, 0, unroll=4)
    total = to_row(sum_ref[...])
    l_ref[0] = jnp.log2(total)
    fine = jnp.logical_and(jnp.min(total) >= LOW, jnp.max(v) <= HIGH)

    @pl.when(jnp.logical_not(fine))
    def _():
        l_ref[0] = f_ref[...] + rows_log_sum(s_ref, g_ref[...] + change, top_ref, sum_ref)


def last_kernel(count, me_ref, s_ref, p_ref, mass_ref, f_ref, g_ref, u_ref, xn_ref, yn_ref, y_ref, *refs):
    parts, refs = refs[:count], refs[count:]
    sp_any, tp_any, outs = refs[0], refs[1], refs[2:-7]
    sp, tp, yw, acc, flat, wide, sem = refs[-7:]
    k = y_ref.shape[0]
    n, width = s_ref.shape
    peers = len(outs)
    own = k // peers
    block = own + 1
    change = jnp.log2(mass_ref[...]) - whole_log_sum(parts)
    g = g_ref[...] + change
    f = f_ref[...] + u_ref[...]
    sp[...] = f * UNIT + xn_ref[...]
    tp[...] = g * UNIT + yn_ref[...]
    copies = [pltpu.make_async_copy(sp, sp_any, sem.at[0]), pltpu.make_async_copy(tp, tp_any, sem.at[1])]
    for copy in copies:
        copy.start()
    u = jnp.exp2(u_ref[...])
    v = jnp.exp2(change)
    step = 256

    def project(weight, scale, rescale):
        y1, y2, _ = pieces(y_ref[...] * scale)
        s1, s2, _ = [p.astype(F32) for p in pieces(scale)]
        yw[pl.ds(0, k), :] = y1
        at = lax.broadcasted_iota(jnp.int32, (LANES - k, width), 0)
        yw[pl.ds(k, LANES - k), :] = jnp.where(at == 0, s1, jnp.where(at == 1, s2, 0.0)).astype(BF16)
        yw[pl.ds(LANES, k), :] = y2
        yw[pl.ds(LANES + k, LANES - k), :] = jnp.zeros((LANES - k, width), BF16)
        for b in range(n // step):
            w = weight(pl.ds(b * step, step))
            w1 = w.astype(BF16)
            w2 = (w - w1.astype(F32)).astype(BF16)
            dims = (((1,), (1,)), ((), ()))
            out = lax.dot_general(w1, yw[...], dims, preferred_element_type=F32) + lax.dot_general(
                w2, yw[...], dims, preferred_element_type=F32
            )
            acc[pl.ds(b * step, step), :] = out[:, :LANES] + out[:, LANES:]
        total = acc[...].T * rescale
        den = total[k : k + 1, :] + total[k + 1 : k + 2, :]
        for t in range(peers):
            for c in range(n // LANES):
                at = slice(c * LANES, (c + 1) * LANES)
                flat[t, pl.ds(c * block, own), :] = total[t * own : (t + 1) * own, at]
                flat[t, pl.ds(c * block + own, 1), :] = den[:, at]
        for d, out in enumerate(outs):
            out[...] = flat[lax.rem(me_ref[0] + d, peers)]
        return den

    den = project(lambda rows: p_ref[rows, :], v, u)
    fine = jnp.logical_and(jnp.min(den) >= LOW, jnp.logical_and(jnp.max(u) <= HIGH, jnp.max(v) <= HIGH))

    @pl.when(jnp.logical_not(fine))
    def _():
        across(f, wide)

        def weight(rows):
            fb = jnp.concatenate([wide[rows, :]] * (width // LANES), axis=1)
            return jnp.exp2((s_ref[rows, :] + fb) + g)

        project(weight, jnp.ones_like(v), jnp.ones_like(u))

    for copy in copies:
        copy.wait()


def join_kernel(*refs):
    parts, out_ref = refs[:-1], refs[-1]
    own, n = out_ref.shape
    for c in range(n // LANES):
        at = c * (own + 1)
        num = tree(jnp.add, [p[pl.ds(at, own), :] for p in parts])
        den = tree(jnp.add, [p[pl.ds(at + own, 1), :] for p in parts])
        out_ref[:, chunk(c)] = num / den


def call(kernel, outs, scratch, ins, out_specs=None):
    return pl.pallas_call(
        kernel,
        out_shape=[o if isinstance(o, jax.ShapeDtypeStruct) else jax.ShapeDtypeStruct(o, F32) for o in outs],
        in_specs=[spec for spec, _ in ins],
        out_specs=out_specs or [VMEM] * len(outs),
        scratch_shapes=scratch,
        compiler_params=pltpu.CompilerParams(vmem_limit_bytes=20 * 2**20),
    )(*[a for _, a in ins])


def put(*arrays):
    return [(VMEM, a) for a in arrays]


def turn(v, axis, size, d):
    return lax.ppermute(v, axis, [(i, (i + d) % size) for i in range(size)])


def flip(v, axis, size, bit):
    return lax.ppermute(v, axis, [(i, i ^ bit) for i in range(size)])


def few(size):
    return size <= 4


def everyone(v, axis, size):
    if few(size):
        return [v] + [turn(v, axis, size, d) for d in range(1, size)]
    return [lax.all_to_all(v, axis, 0, 0, tiled=True)]


def copies_of(size):
    return 1 if few(size) else size


def gather_src(v, size):
    if v.shape[0] % 8 or not few(size):
        return [lax.all_gather(v, "tgt", axis=0, tiled=True)], [None]
    return [v] + [turn(v, "tgt", size, d) for d in range(1, size)], list(range(size))


def gather_tgt(v, size, other):
    if v.shape[0] % 8 or size & (size - 1):
        return [lax.all_gather(v, "src", axis=0, tiled=True)], [None], other
    order = list(range(0, size, 2))
    mine = jnp.concatenate([v] + [flip(v, "src", size, d) for d in order[1:]], axis=0)
    mine, *other = lax.optimization_barrier([mine] + other)
    return [mine, flip(mine, "src", size, 1)], [order, [d + 1 for d in order]], other


def shards(peers_src, peers_tgt, src_pts, tgt_pts, src_mass, tgt_mass, init_pot):
    own = src_pts.shape[0]
    n, width = src_pts.shape[1], tgt_pts.shape[1]
    k = own * peers_tgt
    pack = (own + 1) * (n // LANES)
    row, col = (1, n), (1, width)
    rows, cols = (copies_of(peers_tgt), 1, n), (copies_of(peers_src), 1, width)
    lane = pltpu.VMEM((n, LANES), F32)
    me = lax.axis_index(("src", "tgt")).astype(jnp.int32).reshape(1)
    xs, xplan = gather_src(src_pts, peers_tgt)
    ys, yplan, xs = gather_tgt(tgt_pts, peers_src, xs)
    tm = tgt_mass.reshape(col)
    sm, pot, xn, xt = call(
        functools.partial(early_kernel, peers_tgt, xplan),
        [row, col, row, jax.ShapeDtypeStruct((n, 6 * k), BF16)],
        [pltpu.VMEM((k, n), F32), pltpu.VMEM((6 * k, n), BF16)],
        [(SMEM, me)] + put(src_mass.reshape(row), init_pot.reshape(col), *xs),
    )
    s, l, yn, yo = call(
        functools.partial(first_kernel, peers_tgt, yplan),
        [(n, width), rows, col, (k, width)],
        [pltpu.VMEM((6 * k, width), BF16), lane, lane],
        [(SMEM, me)] + put(pot, xt, *ys),
    )
    parts = everyone(l, "tgt", peers_tgt)
    f, wide, l = call(
        functools.partial(src_first_kernel, len(parts)), [row, (n, LANES), cols], [], put(s, sm, *parts)
    )
    parts = everyone(l, "src", peers_src)
    g, p, l = call(
        functools.partial(tgt_first_kernel, len(parts)),
        [col, (n, width), rows],
        [lane, lane],
        put(s, tm, f, wide, *parts),
    )
    for step in range(1, ITERS):
        parts = everyone(l, "tgt", peers_tgt)
        u, l = call(functools.partial(src_kernel, len(parts)), [row, cols], [lane], put(s, p, sm, f, g, *parts))
        parts = everyone(l, "src", peers_src)
        if step < ITERS - 1:
            (l,) = call(functools.partial(tgt_kernel, len(parts)), [rows], [lane, lane], put(s, p, tm, f, g, *parts))
    src_pot, tgt_pot, *blocks = call(
        functools.partial(last_kernel, len(parts)),
        [row, col] + [(pack, LANES)] * peers_tgt,
        [
            pltpu.VMEM(row, F32),
            pltpu.VMEM(col, F32),
            pltpu.VMEM((2 * LANES, width), BF16),
            lane,
            pltpu.VMEM((peers_tgt, pack, LANES), F32),
            lane,
            pltpu.SemaphoreType.DMA((2,)),
        ],
        [(SMEM, me)] + put(s, p, tm, f, g, u, xn, yn, yo, *parts),
        [HBM, HBM] + [VMEM] * peers_tgt,
    )
    came = [blocks[0]] + [turn(blocks[d], "tgt", peers_tgt, d) for d in range(1, peers_tgt)]
    (mapped,) = call(join_kernel, [(own, n)], [], put(*came))
    return src_pot.reshape(n), tgt_pot.reshape(width), mapped


def solution(mesh):
    return jax.shard_map(
        functools.partial(shards, mesh.shape["src"], mesh.shape["tgt"]),
        mesh=mesh,
        in_specs=(P("tgt", "src"), P("src", "tgt"), P("src"), P("tgt"), P("tgt")),
        out_specs=(P("src"), P("tgt"), P("tgt", "src")),
        check_vma=False,
    )
```

```python
import functools
import math

import jax
import jax.numpy as jnp
from jax import lax
from jax.experimental import pallas as pl
from jax.experimental.pallas import tpu as pltpu
from jax.sharding import PartitionSpec as P

ITERS = 3
EPS = 0.1
UNIT = EPS * math.log(2.0)
LOW = 2.0**-40
HIGH = 2.0**20

F32 = jnp.float32
BF16 = jnp.bfloat16
VMEM = pl.BlockSpec(memory_space=pltpu.VMEM)
SMEM = pl.BlockSpec(memory_space=pltpu.SMEM)
HBM = pl.BlockSpec(memory_space=pltpu.HBM)
LANES = 128


def pieces(v):
    a = v.astype(BF16)
    r = v - a.astype(F32)
    b = r.astype(BF16)
    c = (r - b.astype(F32)).astype(BF16)
    return a, b, c


def tree(op, items):
    items = list(items)
    while len(items) > 1:
        half = (len(items) + 1) // 2
        rest = items[half:]
        items = [op(items[k], rest[k]) if k < len(rest) else items[k] for k in range(half)]
    return items[0]


def whole_log_sum(part_refs):
    if len(part_refs) == 1:
        parts = [part_refs[0][t] for t in range(part_refs[0].shape[0])]
    else:
        parts = [p[0] for p in part_refs]
    top = tree(jnp.maximum, parts)
    return top + jnp.log2(tree(jnp.add, [jnp.exp2(p - top) for p in parts]))


def to_row(wide):
    split = jnp.concatenate(pieces(wide), axis=1)
    ones = jnp.ones((16, split.shape[1]), BF16)
    return lax.dot_general(ones, split, (((1,), (1,)), ((), ())), preferred_element_type=F32)[0:1, :]


def across(row, out_ref):
    n = row.shape[1]
    a, b, c = [p.astype(F32) for p in pieces(row)]
    at = lax.broadcasted_iota(jnp.int32, (16, n), 0)
    split = jnp.where(at == 0, a, jnp.where(at == 1, b, jnp.where(at == 2, c, 0.0))).astype(BF16)
    ones = jnp.ones((16, LANES), BF16)
    out_ref[...] = lax.dot_general(split, ones, (((0,), (0,)), ((), ())), preferred_element_type=F32)


def eight(k):
    return pl.ds(pl.multiple_of(k * 8, 8), 8)


def chunk(c):
    return pl.ds(c * LANES, LANES)


def lanes_log_sum(s_ref, rows, pot8, top_ref, sum_ref):
    cols = s_ref.shape[1] // LANES
    z = [s_ref[rows, chunk(c)] + pot8[:, c * LANES : (c + 1) * LANES] for c in range(cols)]
    top = tree(jnp.maximum, z)
    top_ref[rows, :] = top
    sum_ref[rows, :] = tree(jnp.add, [jnp.exp2(v - top) for v in z])


def join_lanes(top_ref, sum_ref):
    def strip(k, _):
        rows = eight(k)
        part = top_ref[rows, :]
        top = jnp.broadcast_to(jnp.max(part, axis=1, keepdims=True), part.shape)
        sum_ref[rows, :] = sum_ref[rows, :] * jnp.exp2(part - top)
        top_ref[rows, :] = top * (1.0 / LANES)
        return 0

    lax.fori_loop(0, top_ref.shape[0] // 8, strip, 0, unroll=16)
    return to_row(top_ref[...]) + jnp.log2(to_row(sum_ref[...]))


def rows_log_sum(s_ref, pot, top_ref, sum_ref):
    n, width = s_ref.shape
    pot8 = jnp.broadcast_to(pot, (8, width))

    def strip(k, _):
        lanes_log_sum(s_ref, eight(k), pot8, top_ref, sum_ref)
        return 0

    lax.fori_loop(0, n // 8, strip, 0, unroll=4)
    return join_lanes(top_ref, sum_ref)


def cols_log_sum(s_ref, pot_ref):
    n, width = s_ref.shape
    cols = width // LANES

    def load(k):
        rows = eight(k)
        f = pot_ref[rows, :]
        return [s_ref[rows, chunk(c)] + f for c in range(cols)]

    def find(k, top):
        return tuple(jnp.maximum(t, v) for t, v in zip(top, load(k)))

    top = lax.fori_loop(1, n // 8, find, tuple(load(0)), unroll=4)

    def add(k, total):
        return tuple(a + jnp.exp2(v - t) for a, v, t in zip(total, load(k), top))

    zero = tuple(jnp.zeros((8, LANES), F32) for _ in range(cols))
    total = lax.fori_loop(0, n // 8, add, zero, unroll=4)
    out = []
    for t, a in zip(top, total):
        m = jnp.max(t, axis=0, keepdims=True)
        out.append(m + jnp.log2(jnp.sum(a * jnp.exp2(t - m), axis=0, keepdims=True)))
    return jnp.concatenate(out, axis=1)


def repeat(row, out_ref):
    for t in range(out_ref.shape[0]):
        out_ref[t] = row


def sum_kernel(*refs):
    refs[-1][0] = whole_log_sum(refs[:-1])


def early_kernel(mass_ref, pot_ref, x_ref, ls_ref, to_ref, xn_ref, xt_ref, xw):
    k = x_ref.shape[0]
    ls_ref[...] = jnp.log2(mass_ref[...])
    to_ref[...] = pot_ref[...]
    x = x_ref[...]
    xn_ref[...] = jnp.sum(x * x, axis=0, keepdims=True) / k
    x1, x2, x3 = pieces(x)
    for p, piece in enumerate((x1, x1, x2, x2, x1, x3)):
        xw[pl.ds(p * k, k), :] = piece
    xt_ref[...] = xw[...].T


def first_kernel(peers, yplan, me_ref, pot_ref, xt_ref, *refs):
    ycount = len(yplan)
    yparts, (s_ref, l_ref, yn_ref, yo_ref, yw, top_ref, sum_ref) = refs[:ycount], refs[ycount:]
    me = me_ref[0] // peers
    for part, owners in zip(yparts, yplan):
        if owners is None:
            yo_ref[...] = part[...]
            continue
        own = part.shape[0] // len(owners)
        for b, d in enumerate(owners):
            yo_ref[pl.ds(pl.multiple_of((me ^ d) * own, 8), own), :] = part[pl.ds(b * own, own), :]
    y = yo_ref[...]
    yn = jnp.sum(y * y, axis=0, keepdims=True) / y.shape[0]
    yn_ref[...] = yn
    k = y.shape[0]
    y1, y2, y3 = pieces(y * (2.0 / (k * UNIT)))
    for p, piece in enumerate((y1, y2, y1, y2, y3, y1)):
        yw[pl.ds(p * k, k), :] = piece
    n, width = s_ref.shape
    pot8 = jnp.broadcast_to((pot_ref[...] - yn) * (1.0 / UNIT), (8, width))
    step = 256
    for b in range(n // step + 1):
        if b < n // step:
            s_ref[pl.ds(b * step, step), :] = jnp.dot(
                xt_ref[pl.ds(b * step, step), :], yw[...], preferred_element_type=F32
            )
        if b > 0:
            for r in range((b - 1) * step, b * step, 8):
                lanes_log_sum(s_ref, pl.ds(r, 8), pot8, top_ref, sum_ref)
    l_ref[0] = join_lanes(top_ref, sum_ref)


def src_first_kernel(count, s_ref, mass_ref, *refs):
    parts, (f_ref, wide_ref, l_ref) = refs[:count], refs[count:]
    f = mass_ref[...] - whole_log_sum(parts)
    f_ref[...] = f
    across(f, wide_ref)
    repeat(cols_log_sum(s_ref, wide_ref), l_ref)


def tgt_first_kernel(count, s_ref, mass_ref, f_ref, wide_ref, *refs):
    parts, (g_ref, p_ref, l_ref, top_ref, sum_ref) = refs[:count], refs[count:]
    n, width = s_ref.shape
    g = jnp.log2(mass_ref[...]) - whole_log_sum(parts)
    g_ref[...] = g
    g8 = jnp.broadcast_to(g, (8, width))

    def strip(k, _):
        rows = eight(k)
        f = wide_ref[rows, :]
        out = []
        for c in range(width // LANES):
            p = jnp.exp2((s_ref[rows, chunk(c)] + f) + g8[:, c * LANES : (c + 1) * LANES])
            p_ref[rows, chunk(c)] = p
            out.append(p)
        sum_ref[rows, :] = tree(jnp.add, out)
        return 0

    lax.fori_loop(0, n // 8, strip, 0, unroll=4)
    total = to_row(sum_ref[...])
    l_ref[0] = jnp.log2(total)

    @pl.when(jnp.logical_not(jnp.min(total) >= LOW))
    def _():
        l_ref[0] = f_ref[...] + rows_log_sum(s_ref, g, top_ref, sum_ref)


def src_kernel(count, s_ref, p_ref, mass_ref, f_ref, g_ref, *refs):
    parts, (u_ref, l_ref, wide) = refs[:count], refs[count:]
    n, width = p_ref.shape
    cols = width // LANES
    change = mass_ref[...] - whole_log_sum(parts)
    u_ref[...] = change
    u = jnp.exp2(change)
    across(u, wide)

    def add(k, total):
        rows = eight(k)
        f = wide[rows, :]
        return tuple(a + p_ref[rows, chunk(c)] * f for c, a in enumerate(total))

    zero = tuple(jnp.zeros((8, LANES), F32) for _ in range(cols))
    parts = lax.fori_loop(0, n // 8, add, zero, unroll=4)
    total = jnp.concatenate([jnp.sum(a, axis=0, keepdims=True) for a in parts], axis=1)
    repeat(jnp.log2(total), l_ref)
    fine = jnp.logical_and(jnp.min(total) >= LOW, jnp.max(u) <= HIGH)

    @pl.when(jnp.logical_not(fine))
    def _():
        across(f_ref[...] + change, wide)
        repeat(g_ref[...] + cols_log_sum(s_ref, wide), l_ref)


def tgt_kernel(count, s_ref, p_ref, mass_ref, f_ref, g_ref, *refs):
    parts, (l_ref, top_ref, sum_ref) = refs[:count], refs[count:]
    n, width = p_ref.shape
    change = jnp.log2(mass_ref[...]) - whole_log_sum(parts)
    v = jnp.exp2(change)
    v8 = jnp.broadcast_to(v, (8, width))

    def strip(k, _):
        rows = eight(k)
        sum_ref[rows, :] = tree(
            jnp.add, [p_ref[rows, chunk(c)] * v8[:, c * LANES : (c + 1) * LANES] for c in range(width // LANES)]
        )
        return 0

    lax.fori_loop(0, n // 8, strip, 0, unroll=4)
    total = to_row(sum_ref[...])
    l_ref[0] = jnp.log2(total)
    fine = jnp.logical_and(jnp.min(total) >= LOW, jnp.max(v) <= HIGH)

    @pl.when(jnp.logical_not(fine))
    def _():
        l_ref[0] = f_ref[...] + rows_log_sum(s_ref, g_ref[...] + change, top_ref, sum_ref)


def last_kernel(count, me_ref, s_ref, p_ref, mass_ref, f_ref, g_ref, u_ref, xn_ref, yn_ref, y_ref, *refs):
    parts, refs = refs[:count], refs[count:]
    sp_any, tp_any, outs = refs[0], refs[1], refs[2:-7]
    sp, tp, yw, acc, flat, wide, sem = refs[-7:]
    k = y_ref.shape[0]
    n, width = s_ref.shape
    peers = len(outs)
    own = k // peers
    block = own + 1
    change = jnp.log2(mass_ref[...]) - whole_log_sum(parts)
    g = g_ref[...] + change
    f = f_ref[...] + u_ref[...]
    sp[...] = f * UNIT + xn_ref[...]
    tp[...] = g * UNIT + yn_ref[...]
    copies = [pltpu.make_async_copy(sp, sp_any, sem.at[0]), pltpu.make_async_copy(tp, tp_any, sem.at[1])]
    for copy in copies:
        copy.start()
    u = jnp.exp2(u_ref[...])
    v = jnp.exp2(change)
    step = 256

    def project(weight, scale, rescale):
        y1, y2, _ = pieces(y_ref[...] * scale)
        s1, s2, _ = [p.astype(F32) for p in pieces(scale)]
        yw[pl.ds(0, k), :] = y1
        at = lax.broadcasted_iota(jnp.int32, (LANES - k, width), 0)
        yw[pl.ds(k, LANES - k), :] = jnp.where(at == 0, s1, jnp.where(at == 1, s2, 0.0)).astype(BF16)
        yw[pl.ds(LANES, k), :] = y2
        yw[pl.ds(LANES + k, LANES - k), :] = jnp.zeros((LANES - k, width), BF16)
        for b in range(n // step):
            w = weight(pl.ds(b * step, step))
            w1 = w.astype(BF16)
            w2 = (w - w1.astype(F32)).astype(BF16)
            dims = (((1,), (1,)), ((), ()))
            out = lax.dot_general(w1, yw[...], dims, preferred_element_type=F32) + lax.dot_general(
                w2, yw[...], dims, preferred_element_type=F32
            )
            acc[pl.ds(b * step, step), :] = out[:, :LANES] + out[:, LANES:]
        total = acc[...].T * rescale
        den = total[k : k + 1, :] + total[k + 1 : k + 2, :]
        for t in range(peers):
            for c in range(n // LANES):
                at = slice(c * LANES, (c + 1) * LANES)
                flat[t, pl.ds(c * block, own), :] = total[t * own : (t + 1) * own, at]
                flat[t, pl.ds(c * block + own, 1), :] = den[:, at]
        for d, out in enumerate(outs):
            out[...] = flat[lax.rem(me_ref[0] + d, peers)]
        return den

    den = project(lambda rows: p_ref[rows, :], v, u)
    fine = jnp.logical_and(jnp.min(den) >= LOW, jnp.logical_and(jnp.max(u) <= HIGH, jnp.max(v) <= HIGH))

    @pl.when(jnp.logical_not(fine))
    def _():
        across(f, wide)

        def weight(rows):
            fb = jnp.concatenate([wide[rows, :]] * (width // LANES), axis=1)
            return jnp.exp2((s_ref[rows, :] + fb) + g)

        project(weight, jnp.ones_like(v), jnp.ones_like(u))

    for copy in copies:
        copy.wait()


def join_kernel(*refs):
    parts, out_ref = refs[:-1], refs[-1]
    own, n = out_ref.shape
    for c in range(n // LANES):
        at = c * (own + 1)
        num = tree(jnp.add, [p[pl.ds(at, own), :] for p in parts])
        den = tree(jnp.add, [p[pl.ds(at + own, 1), :] for p in parts])
        out_ref[:, chunk(c)] = num / den


def call(kernel, outs, scratch, ins, out_specs=None):
    return pl.pallas_call(
        kernel,
        out_shape=[o if isinstance(o, jax.ShapeDtypeStruct) else jax.ShapeDtypeStruct(o, F32) for o in outs],
        in_specs=[spec for spec, _ in ins],
        out_specs=out_specs or [VMEM] * len(outs),
        scratch_shapes=scratch,
        compiler_params=pltpu.CompilerParams(vmem_limit_bytes=20 * 2**20),
    )(*[a for _, a in ins])


def put(*arrays):
    return [(VMEM, a) for a in arrays]


def turn(v, axis, size, d):
    return lax.ppermute(v, axis, [(i, (i + d) % size) for i in range(size)])


def flip(v, axis, size, bit):
    return lax.ppermute(v, axis, [(i, i ^ bit) for i in range(size)])


def join_rows(v, axis, size):
    if spread(axis, size) > 1:
        return [lax.all_to_all(v, axis, 0, 0, tiled=True)]
    if axis == "tgt":
        return [v] + [turn(v, axis, size, d) for d in range(1, size)]
    parts = [v] + [flip(v, axis, size, d) for d in range(2, size, 2)]
    (v,) = call(sum_kernel, [v.shape], [], put(*parts))
    return [v, flip(v, axis, size, 1)]


def spread(axis, size):
    small = size in (2, 4) if axis == "tgt" else size in (4, 8)
    return 1 if small else size


def gather_tgt(v, size, other):
    if v.shape[0] % 8 or size & (size - 1):
        return [lax.all_gather(v, "src", axis=0, tiled=True)], [None], other
    order = list(range(0, size, 2))
    mine = jnp.concatenate([v] + [flip(v, "src", size, d) for d in order[1:]], axis=0)
    mine, other = lax.optimization_barrier((mine, other))
    return [mine, flip(mine, "src", size, 1)], [order, [d + 1 for d in order]], other


def shards(peers_src, peers_tgt, src_pts, tgt_pts, src_mass, tgt_mass, init_pot):
    own = src_pts.shape[0]
    n, width = src_pts.shape[1], tgt_pts.shape[1]
    k = own * peers_tgt
    pack = (own + 1) * (n // LANES)
    row, col = (1, n), (1, width)
    rows, cols = (spread("tgt", peers_tgt), 1, n), (spread("src", peers_src), 1, width)
    lane = pltpu.VMEM((n, LANES), F32)
    me = lax.axis_index(("src", "tgt")).astype(jnp.int32).reshape(1)
    xs = lax.all_gather(src_pts, "tgt", axis=0, tiled=True)
    ys, yplan, xs = gather_tgt(tgt_pts, peers_src, xs)
    tm = tgt_mass.reshape(col)
    sm, pot, xn, xt = call(
        early_kernel,
        [row, col, row, jax.ShapeDtypeStruct((n, 6 * k), BF16)],
        [pltpu.VMEM((6 * k, n), BF16)],
        put(src_mass.reshape(row), init_pot.reshape(col), xs),
    )
    s, l, yn, yo = call(
        functools.partial(first_kernel, peers_tgt, yplan),
        [(n, width), rows, col, (k, width)],
        [pltpu.VMEM((6 * k, width), BF16), lane, lane],
        [(SMEM, me)] + put(pot, xt, *ys),
    )
    parts = join_rows(l, "tgt", peers_tgt)
    f, wide, l = call(
        functools.partial(src_first_kernel, len(parts)), [row, (n, LANES), cols], [], put(s, sm, *parts)
    )
    parts = join_rows(l, "src", peers_src)
    g, p, l = call(
        functools.partial(tgt_first_kernel, len(parts)),
        [col, (n, width), rows],
        [lane, lane],
        put(s, tm, f, wide, *parts),
    )
    for step in range(1, ITERS):
        parts = join_rows(l, "tgt", peers_tgt)
        u, l = call(functools.partial(src_kernel, len(parts)), [row, cols], [lane], put(s, p, sm, f, g, *parts))
        parts = join_rows(l, "src", peers_src)
        if step < ITERS - 1:
            (l,) = call(functools.partial(tgt_kernel, len(parts)), [rows], [lane, lane], put(s, p, tm, f, g, *parts))
    src_pot, tgt_pot, *blocks = call(
        functools.partial(last_kernel, len(parts)),
        [row, col] + [(pack, LANES)] * peers_tgt,
        [
            pltpu.VMEM(row, F32),
            pltpu.VMEM(col, F32),
            pltpu.VMEM((2 * LANES, width), BF16),
            lane,
            pltpu.VMEM((peers_tgt, pack, LANES), F32),
            lane,
            pltpu.SemaphoreType.DMA((2,)),
        ],
        [(SMEM, me)] + put(s, p, tm, f, g, u, xn, yn, yo, *parts),
        [HBM, HBM] + [VMEM] * peers_tgt,
    )
    came = [blocks[0]] + [turn(blocks[d], "tgt", peers_tgt, d) for d in range(1, peers_tgt)]
    (mapped,) = call(join_kernel, [(own, n)], [], put(*came))
    return src_pot.reshape(n), tgt_pot.reshape(width), mapped


def solution(mesh):
    return jax.shard_map(
        functools.partial(shards, mesh.shape["src"], mesh.shape["tgt"]),
        mesh=mesh,
        in_specs=(P("tgt", "src"), P("src", "tgt"), P("src"), P("tgt"), P("tgt")),
        out_specs=(P("src"), P("tgt"), P("tgt", "src")),
        check_vma=False,
    )
```

```python
import functools
import math

import jax
import jax.numpy as jnp
from jax import lax
from jax.experimental import pallas as pl
from jax.experimental.pallas import tpu as pltpu
from jax.sharding import PartitionSpec as P

ITERS = 3
EPS = 0.1
UNIT = EPS * math.log(2.0)
LOW = 2.0**-40
HIGH = 2.0**20

F32 = jnp.float32
BF16 = jnp.bfloat16
VMEM = pl.BlockSpec(memory_space=pltpu.VMEM)
SMEM = pl.BlockSpec(memory_space=pltpu.SMEM)
HBM = pl.BlockSpec(memory_space=pltpu.HBM)
LANES = 128


def pieces(v):
    a = v.astype(BF16)
    r = v - a.astype(F32)
    b = r.astype(BF16)
    c = (r - b.astype(F32)).astype(BF16)
    return a, b, c


def tree(op, items):
    items = list(items)
    while len(items) > 1:
        half = (len(items) + 1) // 2
        rest = items[half:]
        items = [op(items[k], rest[k]) if k < len(rest) else items[k] for k in range(half)]
    return items[0]


def whole_log_sum(part_refs):
    if len(part_refs) == 1:
        parts = [part_refs[0][t] for t in range(part_refs[0].shape[0])]
    else:
        parts = [p[0] for p in part_refs]
    top = tree(jnp.maximum, parts)
    return top + jnp.log2(tree(jnp.add, [jnp.exp2(p - top) for p in parts]))


def to_row(wide):
    split = jnp.concatenate(pieces(wide), axis=1)
    ones = jnp.ones((16, split.shape[1]), BF16)
    return lax.dot_general(ones, split, (((1,), (1,)), ((), ())), preferred_element_type=F32)[0:1, :]


def across(row, out_ref):
    n = row.shape[1]
    a, b, c = [p.astype(F32) for p in pieces(row)]
    at = lax.broadcasted_iota(jnp.int32, (16, n), 0)
    split = jnp.where(at == 0, a, jnp.where(at == 1, b, jnp.where(at == 2, c, 0.0))).astype(BF16)
    ones = jnp.ones((16, LANES), BF16)
    out_ref[...] = lax.dot_general(split, ones, (((0,), (0,)), ((), ())), preferred_element_type=F32)


def eight(k):
    return pl.ds(pl.multiple_of(k * 8, 8), 8)


def chunk(c):
    return pl.ds(c * LANES, LANES)


def lanes_log_sum(s_ref, rows, pot8, top_ref, sum_ref):
    cols = s_ref.shape[1] // LANES
    z = [s_ref[rows, chunk(c)] + pot8[:, c * LANES : (c + 1) * LANES] for c in range(cols)]
    top = tree(jnp.maximum, z)
    top_ref[rows, :] = top
    sum_ref[rows, :] = tree(jnp.add, [jnp.exp2(v - top) for v in z])


def join_lanes(top_ref, sum_ref):
    def strip(k, _):
        rows = eight(k)
        part = top_ref[rows, :]
        top = jnp.broadcast_to(jnp.max(part, axis=1, keepdims=True), part.shape)
        sum_ref[rows, :] = sum_ref[rows, :] * jnp.exp2(part - top)
        top_ref[rows, :] = top * (1.0 / LANES)
        return 0

    lax.fori_loop(0, top_ref.shape[0] // 8, strip, 0, unroll=16)
    return to_row(top_ref[...]) + jnp.log2(to_row(sum_ref[...]))


def rows_log_sum(s_ref, pot, top_ref, sum_ref):
    n, width = s_ref.shape
    pot8 = jnp.broadcast_to(pot, (8, width))

    def strip(k, _):
        lanes_log_sum(s_ref, eight(k), pot8, top_ref, sum_ref)
        return 0

    lax.fori_loop(0, n // 8, strip, 0, unroll=4)
    return join_lanes(top_ref, sum_ref)


def cols_log_sum(s_ref, pot_ref):
    n, width = s_ref.shape
    cols = width // LANES

    def load(k):
        rows = eight(k)
        f = pot_ref[rows, :]
        return [s_ref[rows, chunk(c)] + f for c in range(cols)]

    def find(k, top):
        return tuple(jnp.maximum(t, v) for t, v in zip(top, load(k)))

    top = lax.fori_loop(1, n // 8, find, tuple(load(0)), unroll=4)

    def add(k, total):
        return tuple(a + jnp.exp2(v - t) for a, v, t in zip(total, load(k), top))

    zero = tuple(jnp.zeros((8, LANES), F32) for _ in range(cols))
    total = lax.fori_loop(0, n // 8, add, zero, unroll=4)
    out = []
    for t, a in zip(top, total):
        m = jnp.max(t, axis=0, keepdims=True)
        out.append(m + jnp.log2(jnp.sum(a * jnp.exp2(t - m), axis=0, keepdims=True)))
    return jnp.concatenate(out, axis=1)


def repeat(row, out_ref):
    for t in range(out_ref.shape[0]):
        out_ref[t] = row


def sum_kernel(*refs):
    refs[-1][0] = whole_log_sum(refs[:-1])


def early_kernel(mass_ref, pot_ref, x_ref, ls_ref, to_ref, xo_ref):
    ls_ref[...] = jnp.log2(mass_ref[...])
    to_ref[...] = pot_ref[...]
    xo_ref[...] = x_ref[...]


def first_kernel(peers, xplan, yplan, me_ref, pot_ref, *refs):
    xcount, ycount = len(xplan), len(yplan)
    xparts, yparts, refs = refs[:xcount], refs[xcount : xcount + ycount], refs[xcount + ycount :]
    s_ref, l_ref, xn_ref, yn_ref, yo_ref, xs, xw, yw, top_ref, sum_ref = refs
    me_src, me_tgt = me_ref[0] // peers, lax.rem(me_ref[0], peers)
    for part, d in zip(xparts, xplan):
        if d is None:
            xs[...] = part[...]
            continue
        own = part.shape[0]
        xs[pl.ds(pl.multiple_of(lax.rem(me_tgt - d + peers, peers) * own, 8), own), :] = part[...]
    x = xs[...]
    xn_ref[...] = jnp.sum(x * x, axis=0, keepdims=True) / x.shape[0]
    x1, x2, x3 = pieces(x)
    for part, owners in zip(yparts, yplan):
        if owners is None:
            yo_ref[...] = part[...]
            continue
        own = part.shape[0] // len(owners)
        for b, d in enumerate(owners):
            yo_ref[pl.ds(pl.multiple_of((me_src ^ d) * own, 8), own), :] = part[pl.ds(b * own, own), :]
    y = yo_ref[...]
    yn = jnp.sum(y * y, axis=0, keepdims=True) / y.shape[0]
    yn_ref[...] = yn
    k = y.shape[0]
    y1, y2, y3 = pieces(y * (2.0 / (k * UNIT)))
    for p, (xp, yp) in enumerate(((x1, y1), (x1, y2), (x2, y1), (x2, y2), (x1, y3), (x3, y1))):
        xw[pl.ds(p * k, k), :] = xp
        yw[pl.ds(p * k, k), :] = yp
    n, width = s_ref.shape
    pot8 = jnp.broadcast_to((pot_ref[...] - yn) * (1.0 / UNIT), (8, width))
    step = 256
    for b in range(n // step + 1):
        if b < n // step:
            s_ref[pl.ds(b * step, step), :] = lax.dot_general(
                xw[:, pl.ds(b * step, step)], yw[...], (((0,), (0,)), ((), ())), preferred_element_type=F32
            )
        if b > 0:
            for r in range((b - 1) * step, b * step, 8):
                lanes_log_sum(s_ref, pl.ds(r, 8), pot8, top_ref, sum_ref)
    l_ref[0] = join_lanes(top_ref, sum_ref)


def src_first_kernel(count, s_ref, mass_ref, *refs):
    parts, (f_ref, wide_ref, l_ref) = refs[:count], refs[count:]
    f = mass_ref[...] - whole_log_sum(parts)
    f_ref[...] = f
    across(f, wide_ref)
    repeat(cols_log_sum(s_ref, wide_ref), l_ref)


def tgt_first_kernel(count, s_ref, mass_ref, f_ref, wide_ref, *refs):
    parts, (g_ref, p_ref, l_ref, top_ref, sum_ref) = refs[:count], refs[count:]
    n, width = s_ref.shape
    g = jnp.log2(mass_ref[...]) - whole_log_sum(parts)
    g_ref[...] = g
    g8 = jnp.broadcast_to(g, (8, width))

    def strip(k, _):
        rows = eight(k)
        f = wide_ref[rows, :]
        out = []
        for c in range(width // LANES):
            p = jnp.exp2((s_ref[rows, chunk(c)] + f) + g8[:, c * LANES : (c + 1) * LANES])
            p_ref[rows, chunk(c)] = p
            out.append(p)
        sum_ref[rows, :] = tree(jnp.add, out)
        return 0

    lax.fori_loop(0, n // 8, strip, 0, unroll=4)
    total = to_row(sum_ref[...])
    l_ref[0] = jnp.log2(total)

    @pl.when(jnp.logical_not(jnp.min(total) >= LOW))
    def _():
        l_ref[0] = f_ref[...] + rows_log_sum(s_ref, g, top_ref, sum_ref)


def src_kernel(count, s_ref, p_ref, mass_ref, f_ref, g_ref, *refs):
    parts, (*u_refs, l_ref, wide) = refs[:count], refs[count:]
    n, width = p_ref.shape
    cols = width // LANES
    change = mass_ref[...] - whole_log_sum(parts)
    for u_ref in u_refs:
        u_ref[...] = change
    u = jnp.exp2(change)
    across(u, wide)

    def add(k, total):
        rows = eight(k)
        f = wide[rows, :]
        return tuple(a + p_ref[rows, chunk(c)] * f for c, a in enumerate(total))

    zero = tuple(jnp.zeros((8, LANES), F32) for _ in range(cols))
    parts = lax.fori_loop(0, n // 8, add, zero, unroll=4)
    total = jnp.concatenate([jnp.sum(a, axis=0, keepdims=True) for a in parts], axis=1)
    repeat(jnp.log2(total), l_ref)
    fine = jnp.logical_and(jnp.min(total) >= LOW, jnp.max(u) <= HIGH)

    @pl.when(jnp.logical_not(fine))
    def _():
        across(f_ref[...] + change, wide)
        repeat(g_ref[...] + cols_log_sum(s_ref, wide), l_ref)


def tgt_kernel(count, s_ref, p_ref, mass_ref, f_ref, g_ref, *refs):
    parts, (l_ref, top_ref, sum_ref) = refs[:count], refs[count:]
    n, width = p_ref.shape
    change = jnp.log2(mass_ref[...]) - whole_log_sum(parts)
    v = jnp.exp2(change)
    v8 = jnp.broadcast_to(v, (8, width))

    def strip(k, _):
        rows = eight(k)
        sum_ref[rows, :] = tree(
            jnp.add, [p_ref[rows, chunk(c)] * v8[:, c * LANES : (c + 1) * LANES] for c in range(width // LANES)]
        )
        return 0

    lax.fori_loop(0, n // 8, strip, 0, unroll=4)
    total = to_row(sum_ref[...])
    l_ref[0] = jnp.log2(total)
    fine = jnp.logical_and(jnp.min(total) >= LOW, jnp.max(v) <= HIGH)

    @pl.when(jnp.logical_not(fine))
    def _():
        l_ref[0] = f_ref[...] + rows_log_sum(s_ref, g_ref[...] + change, top_ref, sum_ref)


def last_kernel(count, me_ref, s_ref, p_ref, mass_ref, f_ref, g_ref, u_ref, xn_ref, yn_ref, y_ref, *refs):
    parts, refs = refs[:count], refs[count:]
    sp_any, tp_any, outs = refs[0], refs[1], refs[2:-7]
    sp, tp, yw, acc, flat, wide, sem = refs[-7:]
    k = y_ref.shape[0]
    n, width = s_ref.shape
    peers = len(outs)
    own = k // peers
    block = own + 1
    change = jnp.log2(mass_ref[...]) - whole_log_sum(parts)
    g = g_ref[...] + change
    f = f_ref[...] + u_ref[...]
    sp[...] = f * UNIT + xn_ref[...]
    tp[...] = g * UNIT + yn_ref[...]
    copies = [pltpu.make_async_copy(sp, sp_any, sem.at[0]), pltpu.make_async_copy(tp, tp_any, sem.at[1])]
    for copy in copies:
        copy.start()
    u = jnp.exp2(u_ref[...])
    v = jnp.exp2(change)
    step = 256

    def project(weight, scale, rescale):
        y1, y2, _ = pieces(y_ref[...] * scale)
        s1, s2, _ = [p.astype(F32) for p in pieces(scale)]
        yw[pl.ds(0, k), :] = y1
        at = lax.broadcasted_iota(jnp.int32, (LANES - k, width), 0)
        yw[pl.ds(k, LANES - k), :] = jnp.where(at == 0, s1, jnp.where(at == 1, s2, 0.0)).astype(BF16)
        yw[pl.ds(LANES, k), :] = y2
        yw[pl.ds(LANES + k, LANES - k), :] = jnp.zeros((LANES - k, width), BF16)
        for b in range(n // step):
            w = weight(pl.ds(b * step, step))
            w1 = w.astype(BF16)
            w2 = (w - w1.astype(F32)).astype(BF16)
            dims = (((1,), (1,)), ((), ()))
            out = lax.dot_general(w1, yw[...], dims, preferred_element_type=F32) + lax.dot_general(
                w2, yw[...], dims, preferred_element_type=F32
            )
            acc[pl.ds(b * step, step), :] = out[:, :LANES] + out[:, LANES:]
        total = acc[...].T * rescale
        den = total[k : k + 1, :] + total[k + 1 : k + 2, :]
        for t in range(peers):
            for c in range(n // LANES):
                at = slice(c * LANES, (c + 1) * LANES)
                flat[t, pl.ds(c * block, own), :] = total[t * own : (t + 1) * own, at]
                flat[t, pl.ds(c * block + own, 1), :] = den[:, at]
        for d, out in enumerate(outs):
            out[...] = flat[lax.rem(me_ref[0] + d, peers)]
        return den

    den = project(lambda rows: p_ref[rows, :], v, u)
    fine = jnp.logical_and(jnp.min(den) >= LOW, jnp.logical_and(jnp.max(u) <= HIGH, jnp.max(v) <= HIGH))

    @pl.when(jnp.logical_not(fine))
    def _():
        across(f, wide)

        def weight(rows):
            fb = jnp.concatenate([wide[rows, :]] * (width // LANES), axis=1)
            return jnp.exp2((s_ref[rows, :] + fb) + g)

        project(weight, jnp.ones_like(v), jnp.ones_like(u))

    for copy in copies:
        copy.wait()


def join_kernel(*refs):
    parts, out_ref = refs[:-1], refs[-1]
    own, n = out_ref.shape
    for c in range(n // LANES):
        at = c * (own + 1)
        num = tree(jnp.add, [p[pl.ds(at, own), :] for p in parts])
        den = tree(jnp.add, [p[pl.ds(at + own, 1), :] for p in parts])
        out_ref[:, chunk(c)] = num / den


def call(kernel, outs, scratch, ins, out_specs=None):
    return pl.pallas_call(
        kernel,
        out_shape=[o if isinstance(o, jax.ShapeDtypeStruct) else jax.ShapeDtypeStruct(o, F32) for o in outs],
        in_specs=[spec for spec, _ in ins],
        out_specs=out_specs or [VMEM] * len(outs),
        scratch_shapes=scratch,
        compiler_params=pltpu.CompilerParams(vmem_limit_bytes=20 * 2**20),
    )(*[a for _, a in ins])


def put(*arrays):
    return [(VMEM, a) for a in arrays]


def turn(v, axis, size, d):
    return lax.ppermute(v, axis, [(i, (i + d) % size) for i in range(size)])


def flip(v, axis, size, bit):
    return lax.ppermute(v, axis, [(i, i ^ bit) for i in range(size)])


def join_rows(v, axis, size):
    if spread(size) > 1:
        return [lax.all_to_all(v, axis, 0, 0, tiled=True)]
    parts, bit = [v], 1
    while bit < size:
        if bit > 1:
            parts = call(sum_kernel, [v.shape], [], put(*parts))
        parts = [parts[0], flip(parts[0], axis, size, bit)]
        bit *= 2
    return parts


def spread(size):
    return 1 if size in (2, 4, 8) else size


def gather_src(v, size):
    if v.shape[0] % 8 or size > 4:
        return [lax.all_gather(v, "tgt", axis=0, tiled=True)], [None]
    return [v] + [turn(v, "tgt", size, d) for d in range(1, size)], list(range(size))


def gather_tgt(v, size, other):
    if v.shape[0] % 8 or size & (size - 1):
        return [lax.all_gather(v, "src", axis=0, tiled=True)], [None], other
    order = list(range(0, size, 2))
    mine = jnp.concatenate([v] + [flip(v, "src", size, d) for d in order[1:]], axis=0)
    mine, *early = lax.optimization_barrier([mine] + other[:-1])
    other = early + other[-1:]
    return [mine, flip(mine, "src", size, 1)], [order, [d + 1 for d in order]], other


def shards(peers_src, peers_tgt, src_pts, tgt_pts, src_mass, tgt_mass, init_pot):
    own = src_pts.shape[0]
    n, width = src_pts.shape[1], tgt_pts.shape[1]
    k = own * peers_tgt
    pack = (own + 1) * (n // LANES)
    row, col = (1, n), (1, width)
    rows, cols = (spread(peers_tgt), 1, n), (spread(peers_src), 1, width)
    lane = pltpu.VMEM((n, LANES), F32)
    me = lax.axis_index(("src", "tgt")).astype(jnp.int32).reshape(1)
    xs, xplan = gather_src(src_pts, peers_tgt)
    sm, pot = src_mass.reshape(row), init_pot.reshape(col)
    ys, yplan, (sm, pot, *xs) = gather_tgt(tgt_pts, peers_src, [sm, pot] + xs)
    tm = tgt_mass.reshape(col)
    sm, pot, x = call(early_kernel, [row, col, xs[0].shape], [], put(sm, pot, xs[0]))
    s, l, xn, yn, yo = call(
        functools.partial(first_kernel, peers_tgt, xplan, yplan),
        [(n, width), rows, row, col, (k, width)],
        [pltpu.VMEM((k, n), F32), pltpu.VMEM((6 * k, n), BF16), pltpu.VMEM((6 * k, width), BF16), lane, lane],
        [(SMEM, me)] + put(pot, x, *xs[1:], *ys),
    )
    parts = join_rows(l, "tgt", peers_tgt)
    f, wide, l = call(
        functools.partial(src_first_kernel, len(parts)), [row, (n, LANES), cols], [], put(s, sm, *parts)
    )
    parts = join_rows(l, "src", peers_src)
    g, p, l = call(
        functools.partial(tgt_first_kernel, len(parts)),
        [col, (n, width), rows],
        [lane, lane],
        put(s, tm, f, wide, *parts),
    )
    for step in range(1, ITERS):
        parts = join_rows(l, "tgt", peers_tgt)
        *u, l = call(
            functools.partial(src_kernel, len(parts)),
            [row, cols] if step == ITERS - 1 else [cols],
            [lane],
            put(s, p, sm, f, g, *parts),
        )
        parts = join_rows(l, "src", peers_src)
        if step < ITERS - 1:
            (l,) = call(functools.partial(tgt_kernel, len(parts)), [rows], [lane, lane], put(s, p, tm, f, g, *parts))
    src_pot, tgt_pot, *blocks = call(
        functools.partial(last_kernel, len(parts)),
        [row, col] + [(pack, LANES)] * peers_tgt,
        [
            pltpu.VMEM(row, F32),
            pltpu.VMEM(col, F32),
            pltpu.VMEM((2 * LANES, width), BF16),
            lane,
            pltpu.VMEM((peers_tgt, pack, LANES), F32),
            lane,
            pltpu.SemaphoreType.DMA((2,)),
        ],
        [(SMEM, me)] + put(s, p, tm, f, g, *u, xn, yn, yo, *parts),
        [HBM, HBM] + [VMEM] * peers_tgt,
    )
    came = [blocks[0]] + [turn(blocks[d], "tgt", peers_tgt, d) for d in range(1, peers_tgt)]
    (mapped,) = call(join_kernel, [(own, n)], [], put(*came))
    return src_pot.reshape(n), tgt_pot.reshape(width), mapped


def solution(mesh):
    return jax.shard_map(
        functools.partial(shards, mesh.shape["src"], mesh.shape["tgt"]),
        mesh=mesh,
        in_specs=(P("tgt", "src"), P("src", "tgt"), P("src"), P("tgt"), P("tgt")),
        out_specs=(P("src"), P("tgt"), P("tgt", "src")),
        check_vma=False,
    )
```

```python
import functools
import math

import jax
import jax.numpy as jnp
from jax import lax
from jax.experimental import pallas as pl
from jax.experimental.pallas import tpu as pltpu
from jax.sharding import PartitionSpec as P

ITERS = 3
EPS = 0.1
UNIT = EPS * math.log(2.0)
LOW = 2.0**-40
HIGH = 2.0**20

F32 = jnp.float32
BF16 = jnp.bfloat16
VMEM = pl.BlockSpec(memory_space=pltpu.VMEM)
SMEM = pl.BlockSpec(memory_space=pltpu.SMEM)
HBM = pl.BlockSpec(memory_space=pltpu.HBM)
LANES = 128


def pieces(v):
    a = v.astype(BF16)
    r = v - a.astype(F32)
    b = r.astype(BF16)
    c = (r - b.astype(F32)).astype(BF16)
    return a, b, c


def tree(op, items):
    items = list(items)
    while len(items) > 1:
        half = (len(items) + 1) // 2
        rest = items[half:]
        items = [op(items[k], rest[k]) if k < len(rest) else items[k] for k in range(half)]
    return items[0]


def whole_log_sum(part_refs):
    if len(part_refs) == 1:
        parts = [part_refs[0][t] for t in range(part_refs[0].shape[0])]
    else:
        parts = [p[0] for p in part_refs]
    top = tree(jnp.maximum, parts)
    return top + jnp.log2(tree(jnp.add, [jnp.exp2(p - top) for p in parts]))


def to_row(wide):
    split = jnp.concatenate(pieces(wide), axis=1)
    ones = jnp.ones((16, split.shape[1]), BF16)
    return lax.dot_general(ones, split, (((1,), (1,)), ((), ())), preferred_element_type=F32)[0:1, :]


def across(row, out_ref):
    n = row.shape[1]
    a, b, c = [p.astype(F32) for p in pieces(row)]
    at = lax.broadcasted_iota(jnp.int32, (16, n), 0)
    split = jnp.where(at == 0, a, jnp.where(at == 1, b, jnp.where(at == 2, c, 0.0))).astype(BF16)
    ones = jnp.ones((16, LANES), BF16)
    out_ref[...] = lax.dot_general(split, ones, (((0,), (0,)), ((), ())), preferred_element_type=F32)


def eight(k):
    return pl.ds(pl.multiple_of(k * 8, 8), 8)


def chunk(c):
    return pl.ds(c * LANES, LANES)


def lanes_log_sum(s_ref, rows, pot8, top_ref, sum_ref):
    cols = s_ref.shape[1] // LANES
    z = [s_ref[rows, chunk(c)] + pot8[:, c * LANES : (c + 1) * LANES] for c in range(cols)]
    top = tree(jnp.maximum, z)
    top_ref[rows, :] = top
    sum_ref[rows, :] = tree(jnp.add, [jnp.exp2(v - top) for v in z])


def join_lanes(top_ref, sum_ref):
    def strip(k, _):
        rows = eight(k)
        part = top_ref[rows, :]
        top = jnp.broadcast_to(jnp.max(part, axis=1, keepdims=True), part.shape)
        sum_ref[rows, :] = sum_ref[rows, :] * jnp.exp2(part - top)
        top_ref[rows, :] = top * (1.0 / LANES)
        return 0

    lax.fori_loop(0, top_ref.shape[0] // 8, strip, 0, unroll=16)
    return to_row(top_ref[...]) + jnp.log2(to_row(sum_ref[...]))


def rows_log_sum(s_ref, pot, top_ref, sum_ref):
    n, width = s_ref.shape
    pot8 = jnp.broadcast_to(pot, (8, width))

    def strip(k, _):
        lanes_log_sum(s_ref, eight(k), pot8, top_ref, sum_ref)
        return 0

    lax.fori_loop(0, n // 8, strip, 0, unroll=4)
    return join_lanes(top_ref, sum_ref)


def cols_log_sum(s_ref, pot_ref):
    n, width = s_ref.shape
    cols = width // LANES

    def load(k):
        rows = eight(k)
        f = pot_ref[rows, :]
        return [s_ref[rows, chunk(c)] + f for c in range(cols)]

    def find(k, top):
        return tuple(jnp.maximum(t, v) for t, v in zip(top, load(k)))

    top = lax.fori_loop(1, n // 8, find, tuple(load(0)), unroll=4)

    def add(k, total):
        return tuple(a + jnp.exp2(v - t) for a, v, t in zip(total, load(k), top))

    zero = tuple(jnp.zeros((8, LANES), F32) for _ in range(cols))
    total = lax.fori_loop(0, n // 8, add, zero, unroll=4)
    out = []
    for t, a in zip(top, total):
        m = jnp.max(t, axis=0, keepdims=True)
        out.append(m + jnp.log2(jnp.sum(a * jnp.exp2(t - m), axis=0, keepdims=True)))
    return jnp.concatenate(out, axis=1)


def repeat(row, out_ref):
    for t in range(out_ref.shape[0]):
        out_ref[t] = row


def sum_kernel(*refs):
    refs[-1][0] = whole_log_sum(refs[:-1])


def early_kernel(mass_ref, pot_ref, x_ref, ls_ref, to_ref, xo_ref):
    ls_ref[...] = jnp.log2(mass_ref[...])
    to_ref[...] = pot_ref[...]
    xo_ref[...] = x_ref[...]


def first_kernel(peers, xplan, yplan, me_ref, pot_ref, *refs):
    xcount, ycount = len(xplan), len(yplan)
    xparts, yparts, refs = refs[:xcount], refs[xcount : xcount + ycount], refs[xcount + ycount :]
    s_ref, l_ref, xn_ref, yn_ref, yo_ref, xs, xw, yw, top_ref, sum_ref = refs
    me_src, me_tgt = me_ref[0] // peers, lax.rem(me_ref[0], peers)
    for part, d in zip(xparts, xplan):
        if d is None:
            xs[...] = part[...]
            continue
        own = part.shape[0]
        xs[pl.ds(pl.multiple_of(lax.rem(me_tgt - d + peers, peers) * own, 8), own), :] = part[...]
    x = xs[...]
    xn_ref[...] = jnp.sum(x * x, axis=0, keepdims=True) / x.shape[0]
    x1, x2, x3 = pieces(x)
    for part, owners in zip(yparts, yplan):
        if owners is None:
            yo_ref[...] = part[...]
            continue
        own = part.shape[0] // len(owners)
        for b, d in enumerate(owners):
            yo_ref[pl.ds(pl.multiple_of((me_src ^ d) * own, 8), own), :] = part[pl.ds(b * own, own), :]
    y = yo_ref[...]
    yn = jnp.sum(y * y, axis=0, keepdims=True) / y.shape[0]
    yn_ref[...] = yn
    k = y.shape[0]
    y1, y2, y3 = pieces(y * (2.0 / (k * UNIT)))
    for p, (xp, yp) in enumerate(((x1, y1), (x1, y2), (x2, y1), (x2, y2), (x1, y3), (x3, y1))):
        xw[pl.ds(p * k, k), :] = xp
        yw[pl.ds(p * k, k), :] = yp
    n, width = s_ref.shape
    pot8 = jnp.broadcast_to((pot_ref[...] - yn) * (1.0 / UNIT), (8, width))
    step = 256
    for b in range(n // step + 1):
        if b < n // step:
            s_ref[pl.ds(b * step, step), :] = lax.dot_general(
                xw[:, pl.ds(b * step, step)], yw[...], (((0,), (0,)), ((), ())), preferred_element_type=F32
            )
        if b > 0:
            for r in range((b - 1) * step, b * step, 8):
                lanes_log_sum(s_ref, pl.ds(r, 8), pot8, top_ref, sum_ref)
    l_ref[0] = join_lanes(top_ref, sum_ref)


def src_first_kernel(count, s_ref, mass_ref, *refs):
    parts, (f_ref, p_ref, top_ref, l_ref, wide) = refs[:count], refs[count:]
    f = mass_ref[...] - whole_log_sum(parts)
    f_ref[...] = f
    across(f, wide)
    n, width = s_ref.shape
    cols = width // LANES

    def load(k):
        rows = eight(k)
        f = wide[rows, :]
        return [s_ref[rows, chunk(c)] + f for c in range(cols)]

    def find(k, top):
        return tuple(jnp.maximum(t, v) for t, v in zip(top, load(k)))

    tops = lax.fori_loop(1, n // 8, find, tuple(load(0)), unroll=4)
    top = jnp.concatenate([jnp.max(t, axis=0, keepdims=True) for t in tops], axis=1)
    top8 = jnp.broadcast_to(top, (8, width))

    def add(k, total):
        rows = eight(k)
        out = []
        for c, (a, v) in enumerate(zip(total, load(k))):
            e = jnp.exp2(v - top8[:, c * LANES : (c + 1) * LANES])
            p_ref[rows, chunk(c)] = e
            out.append(a + e)
        return tuple(out)

    zero = tuple(jnp.zeros((8, LANES), F32) for _ in range(cols))
    sums = lax.fori_loop(0, n // 8, add, zero, unroll=4)
    total = jnp.concatenate([jnp.sum(a, axis=0, keepdims=True) for a in sums], axis=1)
    top_ref[...] = top
    repeat(top + jnp.log2(total), l_ref)


def src_kernel(count, s_ref, p_ref, mass_ref, f_ref, g_ref, w_ref, *refs):
    parts, (*u_refs, l_ref, wide) = refs[:count], refs[count:]
    n, width = p_ref.shape
    cols = width // LANES
    change = mass_ref[...] - whole_log_sum(parts)
    for u_ref in u_refs:
        u_ref[...] = change
    u = jnp.exp2(change)
    across(u, wide)

    def add(k, total):
        rows = eight(k)
        f = wide[rows, :]
        return tuple(a + p_ref[rows, chunk(c)] * f for c, a in enumerate(total))

    zero = tuple(jnp.zeros((8, LANES), F32) for _ in range(cols))
    parts = lax.fori_loop(0, n // 8, add, zero, unroll=4)
    total = jnp.concatenate([jnp.sum(a, axis=0, keepdims=True) for a in parts], axis=1)
    repeat(jnp.log2(total) + w_ref[...], l_ref)
    fine = jnp.logical_and(jnp.min(total) >= LOW, jnp.max(u) <= HIGH)

    @pl.when(jnp.logical_not(fine))
    def _():
        across(f_ref[...] + change, wide)
        repeat(g_ref[...] + cols_log_sum(s_ref, wide), l_ref)


def tgt_kernel(first, count, s_ref, p_ref, mass_ref, f_ref, *refs):
    if first:
        top_ref, *refs = refs
        parts, (g_ref, w_ref, l_ref, top8_ref, sum_ref) = refs[:count], refs[count:]
        g = jnp.log2(mass_ref[...]) - whole_log_sum(parts)
        g_ref[...] = g
        w = g + top_ref[...]
        w_ref[...] = w
    else:
        g_ref, w_ref, *refs = refs
        parts, (l_ref, top8_ref, sum_ref) = refs[:count], refs[count:]
        change = jnp.log2(mass_ref[...]) - whole_log_sum(parts)
        g = g_ref[...] + change
        w = w_ref[...] + change
    n, width = p_ref.shape
    v = jnp.exp2(w)
    v8 = jnp.broadcast_to(v, (8, width))

    def strip(k, _):
        rows = eight(k)
        sum_ref[rows, :] = tree(
            jnp.add, [p_ref[rows, chunk(c)] * v8[:, c * LANES : (c + 1) * LANES] for c in range(width // LANES)]
        )
        return 0

    lax.fori_loop(0, n // 8, strip, 0, unroll=4)
    total = to_row(sum_ref[...])
    l_ref[0] = jnp.log2(total)
    fine = jnp.logical_and(jnp.min(total) >= LOW, jnp.max(v) <= HIGH)

    @pl.when(jnp.logical_not(fine))
    def _():
        l_ref[0] = f_ref[...] + rows_log_sum(s_ref, g, top8_ref, sum_ref)


def last_kernel(count, me_ref, s_ref, p_ref, mass_ref, f_ref, g_ref, w_ref, u_ref, xn_ref, yn_ref, y_ref, *refs):
    parts, refs = refs[:count], refs[count:]
    sp_any, tp_any, outs = refs[0], refs[1], refs[2:-7]
    sp, tp, yw, acc, flat, wide, sem = refs[-7:]
    k = y_ref.shape[0]
    n, width = s_ref.shape
    peers = len(outs)
    own = k // peers
    block = own + 1
    change = jnp.log2(mass_ref[...]) - whole_log_sum(parts)
    g = g_ref[...] + change
    f = f_ref[...] + u_ref[...]
    sp[...] = f * UNIT + xn_ref[...]
    tp[...] = g * UNIT + yn_ref[...]
    copies = [pltpu.make_async_copy(sp, sp_any, sem.at[0]), pltpu.make_async_copy(tp, tp_any, sem.at[1])]
    for copy in copies:
        copy.start()
    u = jnp.exp2(u_ref[...])
    v = jnp.exp2(w_ref[...] + change)
    step = 256

    def project(weight, scale, rescale):
        y1, y2, _ = pieces(y_ref[...] * scale)
        s1, s2, _ = [p.astype(F32) for p in pieces(scale)]
        yw[pl.ds(0, k), :] = y1
        at = lax.broadcasted_iota(jnp.int32, (LANES - k, width), 0)
        yw[pl.ds(k, LANES - k), :] = jnp.where(at == 0, s1, jnp.where(at == 1, s2, 0.0)).astype(BF16)
        yw[pl.ds(LANES, k), :] = y2
        yw[pl.ds(LANES + k, LANES - k), :] = jnp.zeros((LANES - k, width), BF16)
        for b in range(n // step):
            w = weight(pl.ds(b * step, step))
            w1 = w.astype(BF16)
            w2 = (w - w1.astype(F32)).astype(BF16)
            dims = (((1,), (1,)), ((), ()))
            out = lax.dot_general(w1, yw[...], dims, preferred_element_type=F32) + lax.dot_general(
                w2, yw[...], dims, preferred_element_type=F32
            )
            acc[pl.ds(b * step, step), :] = out[:, :LANES] + out[:, LANES:]
        total = acc[...].T * rescale
        den = total[k : k + 1, :] + total[k + 1 : k + 2, :]
        for t in range(peers):
            for c in range(n // LANES):
                at = slice(c * LANES, (c + 1) * LANES)
                flat[t, pl.ds(c * block, own), :] = total[t * own : (t + 1) * own, at]
                flat[t, pl.ds(c * block + own, 1), :] = den[:, at]
        for d, out in enumerate(outs):
            out[...] = flat[lax.rem(me_ref[0] + d, peers)]
        return den

    den = project(lambda rows: p_ref[rows, :], v, u)
    fine = jnp.logical_and(jnp.min(den) >= LOW, jnp.logical_and(jnp.max(u) <= HIGH, jnp.max(v) <= HIGH))

    @pl.when(jnp.logical_not(fine))
    def _():
        across(f, wide)

        def weight(rows):
            fb = jnp.concatenate([wide[rows, :]] * (width // LANES), axis=1)
            return jnp.exp2((s_ref[rows, :] + fb) + g)

        project(weight, jnp.ones_like(v), jnp.ones_like(u))

    for copy in copies:
        copy.wait()


def join_kernel(*refs):
    parts, out_ref = refs[:-1], refs[-1]
    own, n = out_ref.shape
    for c in range(n // LANES):
        at = c * (own + 1)
        num = tree(jnp.add, [p[pl.ds(at, own), :] for p in parts])
        den = tree(jnp.add, [p[pl.ds(at + own, 1), :] for p in parts])
        out_ref[:, chunk(c)] = num / den


def call(kernel, outs, scratch, ins, out_specs=None):
    return pl.pallas_call(
        kernel,
        out_shape=[o if isinstance(o, jax.ShapeDtypeStruct) else jax.ShapeDtypeStruct(o, F32) for o in outs],
        in_specs=[spec for spec, _ in ins],
        out_specs=out_specs or [VMEM] * len(outs),
        scratch_shapes=scratch,
        compiler_params=pltpu.CompilerParams(vmem_limit_bytes=20 * 2**20),
    )(*[a for _, a in ins])


def put(*arrays):
    return [(VMEM, a) for a in arrays]


def turn(v, axis, size, d):
    return lax.ppermute(v, axis, [(i, (i + d) % size) for i in range(size)])


def flip(v, axis, size, bit):
    return lax.ppermute(v, axis, [(i, i ^ bit) for i in range(size)])


def join_rows(v, axis, size):
    if spread(axis, size) > 1:
        return [lax.all_to_all(v, axis, 0, 0, tiled=True)]
    if axis == "tgt":
        return [v] + [turn(v, axis, size, d) for d in range(1, size)]
    if size > 2:
        (v,) = call(sum_kernel, [v.shape], [], put(v, *[turn(v, axis, size, d) for d in range(2, size, 2)]))
    return [v, flip(v, axis, size, 1)]


def spread(axis, size):
    return 1 if size in ((2, 4) if axis == "tgt" else (2, 4, 8)) else size


def gather_src(v, size):
    if v.shape[0] % 8 or size > 4:
        return [lax.all_gather(v, "tgt", axis=0, tiled=True)], [None]
    return [v] + [turn(v, "tgt", size, d) for d in range(1, size)], list(range(size))


def gather_tgt(v, size, other):
    if v.shape[0] % 8 or size & (size - 1):
        return [lax.all_gather(v, "src", axis=0, tiled=True)], [None], other
    order = list(range(0, size, 2))
    far = [flip(v, "src", size, d) for d in order[2:]]
    again, last = lax.optimization_barrier((v, other[-1]))
    near = [flip(again, "src", size, d) for d in order[1:2]]
    mine = jnp.concatenate([v] + near + far, axis=0)
    mine, *other = lax.optimization_barrier([mine] + other[:-1] + [last])
    return [mine, flip(mine, "src", size, 1)], [order, [d + 1 for d in order]], other


def shards(peers_src, peers_tgt, src_pts, tgt_pts, src_mass, tgt_mass, init_pot):
    own = src_pts.shape[0]
    n, width = src_pts.shape[1], tgt_pts.shape[1]
    k = own * peers_tgt
    pack = (own + 1) * (n // LANES)
    row, col = (1, n), (1, width)
    rows, cols = (spread("tgt", peers_tgt), 1, n), (spread("src", peers_src), 1, width)
    lane = pltpu.VMEM((n, LANES), F32)
    me = lax.axis_index(("src", "tgt")).astype(jnp.int32).reshape(1)
    xs, xplan = gather_src(src_pts, peers_tgt)
    sm, pot = src_mass.reshape(row), init_pot.reshape(col)
    ys, yplan, (sm, pot, *xs) = gather_tgt(tgt_pts, peers_src, [sm, pot] + xs)
    tm = tgt_mass.reshape(col)
    sm, pot, x = call(early_kernel, [row, col, xs[0].shape], [], put(sm, pot, xs[0]))
    s, l, xn, yn, yo = call(
        functools.partial(first_kernel, peers_tgt, xplan, yplan),
        [(n, width), rows, row, col, (k, width)],
        [pltpu.VMEM((k, n), F32), pltpu.VMEM((6 * k, n), BF16), pltpu.VMEM((6 * k, width), BF16), lane, lane],
        [(SMEM, me)] + put(pot, x, *xs[1:], *ys),
    )
    parts = join_rows(l, "tgt", peers_tgt)
    f, p, top, l = call(
        functools.partial(src_first_kernel, len(parts)), [row, (n, width), col, cols], [lane], put(s, sm, *parts)
    )
    parts = join_rows(l, "src", peers_src)
    g, w, l = call(
        functools.partial(tgt_kernel, True, len(parts)),
        [col, col, rows],
        [lane, lane],
        put(s, p, tm, f, top, *parts),
    )
    for step in range(1, ITERS):
        parts = join_rows(l, "tgt", peers_tgt)
        *u, l = call(
            functools.partial(src_kernel, len(parts)),
            [row, cols] if step == ITERS - 1 else [cols],
            [lane],
            put(s, p, sm, f, g, w, *parts),
        )
        parts = join_rows(l, "src", peers_src)
        if step < ITERS - 1:
            (l,) = call(
                functools.partial(tgt_kernel, False, len(parts)),
                [rows],
                [lane, lane],
                put(s, p, tm, f, g, w, *parts),
            )
    src_pot, tgt_pot, *blocks = call(
        functools.partial(last_kernel, len(parts)),
        [row, col] + [(pack, LANES)] * peers_tgt,
        [
            pltpu.VMEM(row, F32),
            pltpu.VMEM(col, F32),
            pltpu.VMEM((2 * LANES, width), BF16),
            lane,
            pltpu.VMEM((peers_tgt, pack, LANES), F32),
            lane,
            pltpu.SemaphoreType.DMA((2,)),
        ],
        [(SMEM, me)] + put(s, p, tm, f, g, w, *u, xn, yn, yo, *parts),
        [HBM, HBM] + [VMEM] * peers_tgt,
    )
    came = [blocks[0]] + [turn(blocks[d], "tgt", peers_tgt, d) for d in range(1, peers_tgt)]
    (mapped,) = call(join_kernel, [(own, n)], [], put(*came))
    return src_pot.reshape(n), tgt_pot.reshape(width), mapped


def solution(mesh):
    return jax.shard_map(
        functools.partial(shards, mesh.shape["src"], mesh.shape["tgt"]),
        mesh=mesh,
        in_specs=(P("tgt", "src"), P("src", "tgt"), P("src"), P("tgt"), P("tgt")),
        out_specs=(P("src"), P("tgt"), P("tgt", "src")),
        check_vma=False,
    )
```

```python
import functools
import math

import jax
import jax.numpy as jnp
from jax import lax
from jax.experimental import pallas as pl
from jax.experimental.pallas import tpu as pltpu
from jax.sharding import PartitionSpec as P

ITERS = 3
EPS = 0.1
UNIT = EPS * math.log(2.0)
LOW = 2.0**-40
HIGH = 2.0**20

F32 = jnp.float32
BF16 = jnp.bfloat16
VMEM = pl.BlockSpec(memory_space=pltpu.VMEM)
SMEM = pl.BlockSpec(memory_space=pltpu.SMEM)
HBM = pl.BlockSpec(memory_space=pltpu.HBM)
LANES = 128


def pieces(v):
    a = v.astype(BF16)
    r = v - a.astype(F32)
    b = r.astype(BF16)
    c = (r - b.astype(F32)).astype(BF16)
    return a, b, c


def tree(op, items):
    items = list(items)
    while len(items) > 1:
        half = (len(items) + 1) // 2
        rest = items[half:]
        items = [op(items[k], rest[k]) if k < len(rest) else items[k] for k in range(half)]
    return items[0]


def whole_log_sum(part_refs):
    if len(part_refs) == 1:
        parts = [part_refs[0][t] for t in range(part_refs[0].shape[0])]
    else:
        parts = [p[0] for p in part_refs]
    top = tree(jnp.maximum, parts)
    return top + jnp.log2(tree(jnp.add, [jnp.exp2(p - top) for p in parts]))


def to_row(wide):
    split = jnp.concatenate(pieces(wide), axis=1)
    ones = jnp.ones((16, split.shape[1]), BF16)
    return lax.dot_general(ones, split, (((1,), (1,)), ((), ())), preferred_element_type=F32)[0:1, :]


def across(row, out_ref):
    n = row.shape[1]
    a, b, c = [p.astype(F32) for p in pieces(row)]
    at = lax.broadcasted_iota(jnp.int32, (16, n), 0)
    split = jnp.where(at == 0, a, jnp.where(at == 1, b, jnp.where(at == 2, c, 0.0))).astype(BF16)
    ones = jnp.ones((16, LANES), BF16)
    out_ref[...] = lax.dot_general(split, ones, (((0,), (0,)), ((), ())), preferred_element_type=F32)


def eight(k):
    return pl.ds(pl.multiple_of(k * 8, 8), 8)


def chunk(c):
    return pl.ds(c * LANES, LANES)


def lanes_log_sum(s, rows, pot8, top_ref, sum_ref):
    z = [v + pot8[:, c * LANES : (c + 1) * LANES] for c, v in enumerate(s)]
    top = tree(jnp.maximum, z)
    top_ref[rows, :] = top
    sum_ref[rows, :] = tree(jnp.add, [jnp.exp2(v - top) for v in z])


def join_lanes(top_ref, sum_ref):
    def strip(k, _):
        rows = eight(k)
        part = top_ref[rows, :]
        top = jnp.broadcast_to(jnp.max(part, axis=1, keepdims=True), part.shape)
        sum_ref[rows, :] = sum_ref[rows, :] * jnp.exp2(part - top)
        top_ref[rows, :] = top * (1.0 / LANES)
        return 0

    lax.fori_loop(0, top_ref.shape[0] // 8, strip, 0, unroll=16)
    return to_row(top_ref[...]) + jnp.log2(to_row(sum_ref[...]))


def rows_log_sum(s_ref, pot, top_ref, sum_ref):
    n, width = s_ref.shape
    pot8 = jnp.broadcast_to(pot, (8, width))

    def strip(k, _):
        rows = eight(k)
        lanes_log_sum([s_ref[rows, chunk(c)] for c in range(width // LANES)], rows, pot8, top_ref, sum_ref)
        return 0

    lax.fori_loop(0, n // 8, strip, 0, unroll=4)
    return join_lanes(top_ref, sum_ref)


def cols_log_sum(s_ref, pot_ref):
    n, width = s_ref.shape
    cols = width // LANES

    def load(k):
        rows = eight(k)
        f = pot_ref[rows, :]
        return [s_ref[rows, chunk(c)] + f for c in range(cols)]

    def find(k, top):
        return tuple(jnp.maximum(t, v) for t, v in zip(top, load(k)))

    top = lax.fori_loop(1, n // 8, find, tuple(load(0)), unroll=4)

    def add(k, total):
        return tuple(a + jnp.exp2(v - t) for a, v, t in zip(total, load(k), top))

    zero = tuple(jnp.zeros((8, LANES), F32) for _ in range(cols))
    total = lax.fori_loop(0, n // 8, add, zero, unroll=4)
    out = []
    for t, a in zip(top, total):
        m = jnp.max(t, axis=0, keepdims=True)
        out.append(m + jnp.log2(jnp.sum(a * jnp.exp2(t - m), axis=0, keepdims=True)))
    return jnp.concatenate(out, axis=1)


def repeat(row, out_ref):
    for t in range(out_ref.shape[0]):
        out_ref[t] = row


def sum_kernel(*refs):
    refs[-1][0] = whole_log_sum(refs[:-1])


def early_kernel(*refs):
    for ref, out_ref in zip(refs[:3], refs[3:]):
        out_ref[...] = ref[...]


def log_kernel(mass_ref, out_ref):
    out_ref[...] = jnp.log2(mass_ref[...])


def stack_kernel(*refs):
    own = refs[0].shape[0]
    for b, ref in enumerate(refs[:-1]):
        refs[-1][pl.ds(b * own, own), :] = ref[...]


def first_kernel(peers, xplan, yplan, me_ref, pot_ref, *refs):
    xcount, ycount = len(xplan), len(yplan)
    xparts, yparts, refs = refs[:xcount], refs[xcount : xcount + ycount], refs[xcount + ycount :]
    s_ref, l_ref, xn_ref, yn_ref, yo_ref, xs, xw, xt, yw, top_ref, sum_ref = refs
    me_src, me_tgt = me_ref[0] // peers, lax.rem(me_ref[0], peers)
    for part, d in zip(xparts, xplan):
        if d is None:
            xs[...] = part[...]
            continue
        own = part.shape[0]
        xs[pl.ds(pl.multiple_of(lax.rem(me_tgt - d + peers, peers) * own, 8), own), :] = part[...]
    x = xs[...]
    xn_ref[...] = jnp.sum(x * x, axis=0, keepdims=True) / x.shape[0]
    x1, x2, x3 = pieces(x)
    for part, owners in zip(yparts, yplan):
        if owners is None:
            yo_ref[...] = part[...]
            continue
        own = part.shape[0] // len(owners)
        for b, d in enumerate(owners):
            yo_ref[pl.ds(pl.multiple_of((me_src ^ d) * own, 8), own), :] = part[pl.ds(b * own, own), :]
    y = yo_ref[...]
    yn = jnp.sum(y * y, axis=0, keepdims=True) / y.shape[0]
    yn_ref[...] = yn
    k = y.shape[0]
    y1, y2, y3 = pieces(y * (2.0 / (k * UNIT)))
    for p, (xp, yp) in enumerate(((x1, y1), (x1, y2), (x2, y1), (x2, y2), (x1, y3), (x3, y1))):
        xw[pl.ds(p * k, k), :] = xp
        yw[pl.ds(p * k, k), :] = yp
    n, width = s_ref.shape
    pot8 = jnp.broadcast_to((pot_ref[...] - yn) * (1.0 / UNIT), (8, width))
    xt[...] = xw[...].T
    s_ref[...] = jnp.dot(xt[...], yw[...], preferred_element_type=F32)

    def strip(r, _):
        rows = eight(r)
        lanes_log_sum([s_ref[rows, chunk(c)] for c in range(width // LANES)], rows, pot8, top_ref, sum_ref)
        return 0

    lax.fori_loop(0, n // 8, strip, 0, unroll=4)
    l_ref[0] = join_lanes(top_ref, sum_ref)


def src_first_kernel(count, s_ref, mass_ref, *refs):
    parts, (f_ref, p_ref, top_ref, l_ref, wide) = refs[:count], refs[count:]
    f = mass_ref[...] - whole_log_sum(parts)
    f_ref[...] = f
    across(f, wide)
    n, width = s_ref.shape
    cols = width // LANES

    def load(k):
        rows = eight(k)
        f = wide[rows, :]
        return [s_ref[rows, chunk(c)] + f for c in range(cols)]

    def find(k, top):
        return tuple(jnp.maximum(t, v) for t, v in zip(top, load(k)))

    tops = lax.fori_loop(1, n // 8, find, tuple(load(0)), unroll=4)
    top = jnp.concatenate([jnp.max(t, axis=0, keepdims=True) for t in tops], axis=1)
    top8 = jnp.broadcast_to(top, (8, width))

    def add(k, total):
        rows = eight(k)
        out = []
        for c, (a, v) in enumerate(zip(total, load(k))):
            e = jnp.exp2(v - top8[:, c * LANES : (c + 1) * LANES])
            p_ref[rows, chunk(c)] = e
            out.append(a + e)
        return tuple(out)

    zero = tuple(jnp.zeros((8, LANES), F32) for _ in range(cols))
    sums = lax.fori_loop(0, n // 8, add, zero, unroll=4)
    total = jnp.concatenate([jnp.sum(a, axis=0, keepdims=True) for a in sums], axis=1)
    top_ref[...] = top
    repeat(top + jnp.log2(total), l_ref)


def src_kernel(count, s_ref, p_ref, mass_ref, f_ref, g_ref, w_ref, *refs):
    parts, (*u_refs, l_ref, wide) = refs[:count], refs[count:]
    n, width = p_ref.shape
    cols = width // LANES
    change = mass_ref[...] - whole_log_sum(parts)
    for u_ref in u_refs:
        u_ref[...] = change
    u = jnp.exp2(change)
    across(u, wide)

    def add(k, total):
        rows = eight(k)
        f = wide[rows, :]
        return tuple(a + p_ref[rows, chunk(c)] * f for c, a in enumerate(total))

    zero = tuple(jnp.zeros((8, LANES), F32) for _ in range(cols))
    parts = lax.fori_loop(0, n // 8, add, zero, unroll=4)
    total = jnp.concatenate([jnp.sum(a, axis=0, keepdims=True) for a in parts], axis=1)
    repeat(jnp.log2(total) + w_ref[...], l_ref)
    fine = jnp.logical_and(jnp.min(total) >= LOW, jnp.max(u) <= HIGH)

    @pl.when(jnp.logical_not(fine))
    def _():
        across(f_ref[...] + change, wide)
        repeat(g_ref[...] + cols_log_sum(s_ref, wide), l_ref)


def tgt_kernel(first, count, s_ref, p_ref, mass_ref, f_ref, *refs):
    if first:
        top_ref, *refs = refs
        parts, (g_ref, w_ref, l_ref, top8_ref, sum_ref) = refs[:count], refs[count:]
        g = jnp.log2(mass_ref[...]) - whole_log_sum(parts)
        g_ref[...] = g
        w = g + top_ref[...]
        w_ref[...] = w
    else:
        g_ref, w_ref, *refs = refs
        parts, (l_ref, top8_ref, sum_ref) = refs[:count], refs[count:]
        change = jnp.log2(mass_ref[...]) - whole_log_sum(parts)
        g = g_ref[...] + change
        w = w_ref[...] + change
    n, width = p_ref.shape
    v = jnp.exp2(w)
    v8 = jnp.broadcast_to(v, (8, width))

    def strip(k, _):
        rows = eight(k)
        sum_ref[rows, :] = tree(
            jnp.add, [p_ref[rows, chunk(c)] * v8[:, c * LANES : (c + 1) * LANES] for c in range(width // LANES)]
        )
        return 0

    lax.fori_loop(0, n // 8, strip, 0, unroll=4)
    total = to_row(sum_ref[...])
    l_ref[0] = jnp.log2(total)
    fine = jnp.logical_and(jnp.min(total) >= LOW, jnp.max(v) <= HIGH)

    @pl.when(jnp.logical_not(fine))
    def _():
        l_ref[0] = f_ref[...] + rows_log_sum(s_ref, g, top8_ref, sum_ref)


def split_kernel(p_ref, high_ref, low_ref):
    def strip(k, _):
        rows = pl.ds(pl.multiple_of(k * 16, 16), 16)
        w = p_ref[rows, :]
        high = w.astype(BF16)
        high_ref[rows, :] = high
        low_ref[rows, :] = (w - high.astype(F32)).astype(BF16)
        return 0

    lax.fori_loop(0, p_ref.shape[0] // 16, strip, 0, unroll=2)


def last_kernel(count, me_ref, s_ref, high_ref, low_ref, mass_ref, f_ref, g_ref, w_ref, u_ref, xn_ref, yn_ref, y_ref, *refs):
    parts, refs = refs[:count], refs[count:]
    sp_any, tp_any, outs = refs[0], refs[1], refs[2:-9]
    sp, tp, yw, yt, acc, flat, wide, pot, sem = refs[-9:]
    k = y_ref.shape[0]
    n, width = s_ref.shape
    peers = len(outs)
    own = k // peers
    block = own + 1
    change = jnp.log2(mass_ref[...]) - whole_log_sum(parts)
    g = g_ref[...] + change
    f = f_ref[...] + u_ref[...]
    sp[...] = f * UNIT + xn_ref[...]
    tp[...] = g * UNIT + yn_ref[...]
    copies = [pltpu.make_async_copy(sp, sp_any, sem.at[0]), pltpu.make_async_copy(tp, tp_any, sem.at[1])]
    for copy in copies:
        copy.start()
    u = jnp.exp2(u_ref[...])
    v = jnp.exp2(w_ref[...] + change)

    def project(weight, step, scale, rescale):
        y1, y2, _ = pieces(y_ref[...] * scale)
        s1, s2, _ = [p.astype(F32) for p in pieces(scale)]
        yw[pl.ds(0, k), :] = y1
        at = lax.broadcasted_iota(jnp.int32, (LANES - k, width), 0)
        yw[pl.ds(k, LANES - k), :] = jnp.where(at == 0, s1, jnp.where(at == 1, s2, 0.0)).astype(BF16)
        yw[pl.ds(LANES, k), :] = y2
        yw[pl.ds(LANES + k, LANES - k), :] = jnp.zeros((LANES - k, width), BF16)
        yt[...] = yw[...].T
        for b in range(n // step):
            rows = pl.ds(b * step, step)
            w1, w2 = weight(rows)
            out = jnp.dot(w1, yt[...], preferred_element_type=F32) + jnp.dot(w2, yt[...], preferred_element_type=F32)
            acc[rows, :] = out[:, :LANES] + out[:, LANES:]
        total = acc[...].T * rescale
        den = total[k : k + 1, :] + total[k + 1 : k + 2, :]
        for t in range(peers):
            for c in range(n // LANES):
                at = slice(c * LANES, (c + 1) * LANES)
                flat[t, pl.ds(c * block, own), :] = total[t * own : (t + 1) * own, at]
                flat[t, pl.ds(c * block + own, 1), :] = den[:, at]
        for d, out in enumerate(outs):
            out[...] = flat[lax.rem(me_ref[0] + d, peers)]
        return den

    den = project(lambda rows: (high_ref[rows, :], low_ref[rows, :]), n, v, u)
    fine = jnp.logical_and(jnp.min(den) >= LOW, jnp.logical_and(jnp.max(u) <= HIGH, jnp.max(v) <= HIGH))

    @pl.when(jnp.logical_not(fine))
    def _():
        across(f, wide)
        pot[...] = g

        def weight(rows):
            fb = jnp.concatenate([wide[rows, :]] * (width // LANES), axis=1)
            return pieces(jnp.exp2((s_ref[rows, :] + fb) + pot[...]))[:2]

        project(weight, 128, jnp.ones_like(v), jnp.ones_like(u))

    for copy in copies:
        copy.wait()


def join_kernel(*refs):
    parts, out_ref = refs[:-1], refs[-1]
    own, n = out_ref.shape
    for c in range(n // LANES):
        at = c * (own + 1)
        num = tree(jnp.add, [p[pl.ds(at, own), :] for p in parts])
        den = tree(jnp.add, [p[pl.ds(at + own, 1), :] for p in parts])
        out_ref[:, chunk(c)] = num / den


def call(kernel, outs, scratch, ins, out_specs=None, cost=None):
    return pl.pallas_call(
        kernel,
        out_shape=[o if isinstance(o, jax.ShapeDtypeStruct) else jax.ShapeDtypeStruct(o, F32) for o in outs],
        in_specs=[spec for spec, _ in ins],
        out_specs=out_specs or [VMEM] * len(outs),
        scratch_shapes=scratch,
        cost_estimate=cost,
        compiler_params=pltpu.CompilerParams(vmem_limit_bytes=20 * 2**20),
    )(*[a for _, a in ins])


def put(*arrays):
    return [(VMEM, a) for a in arrays]


def turn(v, axis, size, d):
    return lax.ppermute(v, axis, [(i, (i + d) % size) for i in range(size)])


def flip(v, axis, size, bit):
    return lax.ppermute(v, axis, [(i, i ^ bit) for i in range(size)])


def join_rows(v, axis, size):
    if spread(axis, size) > 1:
        return [lax.all_to_all(v, axis, 0, 0, tiled=True)]
    if axis == "tgt":
        return [v] + [turn(v, axis, size, d) for d in range(1, size)]
    if size > 2:
        (v,) = call(sum_kernel, [v.shape], [], put(v, *[turn(v, axis, size, d) for d in range(2, size, 2)]))
    return [v, flip(v, axis, size, 1)]


def spread(axis, size):
    return 1 if size in ((2, 4) if axis == "tgt" else (2, 4, 8)) else size


def gather_src(v, size):
    if v.shape[0] % 8 or size > 4:
        return [lax.all_gather(v, "tgt", axis=0, tiled=True)], [None]
    return [v] + [turn(v, "tgt", size, d) for d in range(1, size)], list(range(size))


def gather_tgt(v, own, size, other):
    if v.shape[0] % 8 or size & (size - 1):
        return [lax.all_gather(v, "src", axis=0, tiled=True)], [None], other
    order = list(range(0, size, 2))
    far = [flip(v, "src", size, d) for d in order[2:]]
    again, last = lax.optimization_barrier((v, other[-1]))
    near = [flip(again, "src", size, d) for d in order[1:2]]
    (mine,) = call(stack_kernel, [(len(order) * v.shape[0], v.shape[1])], [], put(own, *near, *far))
    mine, *other = lax.optimization_barrier([mine] + other[:-1] + [last])
    return [mine, flip(mine, "src", size, 1)], [order, [d + 1 for d in order]], other


def shards(peers_src, peers_tgt, src_pts, tgt_pts, src_mass, tgt_mass, init_pot):
    own = src_pts.shape[0]
    n, width = src_pts.shape[1], tgt_pts.shape[1]
    k = own * peers_tgt
    pack = (own + 1) * (n // LANES)
    row, col = (1, n), (1, width)
    rows, cols = (spread("tgt", peers_tgt), 1, n), (spread("src", peers_src), 1, width)
    lane = pltpu.VMEM((n, LANES), F32)
    me = lax.axis_index(("src", "tgt")).astype(jnp.int32).reshape(1)
    xs, xplan = gather_src(src_pts, peers_tgt)
    pot, x, y = call(
        early_kernel, [col, src_pts.shape, tgt_pts.shape], [], put(init_pot.reshape(col), src_pts, tgt_pts)
    )
    if xplan[0] is not None:
        xs[0] = x
    ys, yplan, xs = gather_tgt(tgt_pts, y, peers_src, xs)
    sm, tm = src_mass.reshape(row), tgt_mass.reshape(col)
    s, l, xn, yn, yo = call(
        functools.partial(first_kernel, peers_tgt, xplan, yplan),
        [(n, width), rows, row, col, (k, width)],
        [
            pltpu.VMEM((k, n), F32),
            pltpu.VMEM((6 * k, n), BF16),
            pltpu.VMEM((n, 6 * k), BF16),
            pltpu.VMEM((6 * k, width), BF16),
            lane,
            lane,
        ],
        [(SMEM, me)] + put(pot, *xs, *ys),
        cost=pl.CostEstimate(flops=12 * k * n * width, transcendentals=n * width, bytes_accessed=8 * n * width),
    )
    sm, l = lax.optimization_barrier((sm, l))
    (sm,) = call(log_kernel, [row], [], put(sm), cost=pl.CostEstimate(flops=n, transcendentals=n, bytes_accessed=8 * n))
    parts = join_rows(l, "tgt", peers_tgt)
    f, p, top, l = call(
        functools.partial(src_first_kernel, len(parts)), [row, (n, width), col, cols], [lane], put(s, sm, *parts)
    )
    parts = join_rows(l, "src", peers_src)
    g, w, l = call(
        functools.partial(tgt_kernel, True, len(parts)),
        [col, col, rows],
        [lane, lane],
        put(s, p, tm, f, top, *parts),
    )
    for step in range(1, ITERS):
        parts = join_rows(l, "tgt", peers_tgt)
        *u, l = call(
            functools.partial(src_kernel, len(parts)),
            [row, cols] if step == ITERS - 1 else [cols],
            [lane],
            put(s, p, sm, f, g, w, *parts),
        )
        if step == ITERS - 1:
            p, l = lax.optimization_barrier((p, l))
            half = jax.ShapeDtypeStruct(p.shape, BF16)
            high, low = call(
                split_kernel,
                [half, half],
                [],
                put(p),
                cost=pl.CostEstimate(flops=4 * n * width, transcendentals=0, bytes_accessed=8 * n * width),
            )
        parts = join_rows(l, "src", peers_src)
        if step < ITERS - 1:
            (l,) = call(
                functools.partial(tgt_kernel, False, len(parts)),
                [rows],
                [lane, lane],
                put(s, p, tm, f, g, w, *parts),
            )
    src_pot, tgt_pot, *blocks = call(
        functools.partial(last_kernel, len(parts)),
        [row, col] + [(pack, LANES)] * peers_tgt,
        [
            pltpu.VMEM(row, F32),
            pltpu.VMEM(col, F32),
            pltpu.VMEM((2 * LANES, width), BF16),
            pltpu.VMEM((width, 2 * LANES), BF16),
            lane,
            pltpu.VMEM((peers_tgt, pack, LANES), F32),
            lane,
            pltpu.VMEM(col, F32),
            pltpu.SemaphoreType.DMA((2,)),
        ],
        [(SMEM, me)] + put(s, high, low, tm, f, g, w, *u, xn, yn, yo, *parts),
        [HBM, HBM] + [VMEM] * peers_tgt,
    )
    came = [blocks[0]] + [turn(blocks[d], "tgt", peers_tgt, d) for d in range(1, peers_tgt)]
    (mapped,) = call(join_kernel, [(own, n)], [], put(*came))
    return src_pot.reshape(n), tgt_pot.reshape(width), mapped


def solution(mesh):
    return jax.shard_map(
        functools.partial(shards, mesh.shape["src"], mesh.shape["tgt"]),
        mesh=mesh,
        in_specs=(P("tgt", "src"), P("src", "tgt"), P("src"), P("tgt"), P("tgt")),
        out_specs=(P("src"), P("tgt"), P("tgt", "src")),
        check_vma=False,
    )
```

```python
import functools
import math

import jax
import jax.numpy as jnp
from jax import lax
from jax.experimental import pallas as pl
from jax.experimental.pallas import tpu as pltpu
from jax.sharding import PartitionSpec as P

ITERS = 3
EPS = 0.1
UNIT = EPS * math.log(2.0)
LOW = 2.0**-40
HIGH = 2.0**20

F32 = jnp.float32
BF16 = jnp.bfloat16
VMEM = pl.BlockSpec(memory_space=pltpu.VMEM)
SMEM = pl.BlockSpec(memory_space=pltpu.SMEM)
HBM = pl.BlockSpec(memory_space=pltpu.HBM)
LANES = 128


def pieces(v):
    a = v.astype(BF16)
    r = v - a.astype(F32)
    b = r.astype(BF16)
    c = (r - b.astype(F32)).astype(BF16)
    return a, b, c


def tree(op, items):
    items = list(items)
    while len(items) > 1:
        half = (len(items) + 1) // 2
        rest = items[half:]
        items = [op(items[k], rest[k]) if k < len(rest) else items[k] for k in range(half)]
    return items[0]


def whole_log_sum(part_refs):
    if len(part_refs) == 1:
        parts = [part_refs[0][t] for t in range(part_refs[0].shape[0])]
    else:
        parts = [p[0] for p in part_refs]
    top = tree(jnp.maximum, parts)
    return top + jnp.log2(tree(jnp.add, [jnp.exp2(p - top) for p in parts]))


def to_row(wide):
    split = jnp.concatenate(pieces(wide), axis=1)
    ones = jnp.ones((16, split.shape[1]), BF16)
    return lax.dot_general(ones, split, (((1,), (1,)), ((), ())), preferred_element_type=F32)[0:1, :]


def across(row, out_ref):
    n = row.shape[1]
    a, b, c = [p.astype(F32) for p in pieces(row)]
    at = lax.broadcasted_iota(jnp.int32, (16, n), 0)
    split = jnp.where(at == 0, a, jnp.where(at == 1, b, jnp.where(at == 2, c, 0.0))).astype(BF16)
    ones = jnp.ones((16, LANES), BF16)
    out_ref[...] = lax.dot_general(split, ones, (((0,), (0,)), ((), ())), preferred_element_type=F32)


def eight(k):
    return pl.ds(pl.multiple_of(k * 8, 8), 8)


def chunk(c):
    return pl.ds(c * LANES, LANES)


def lanes_log_sum(s, rows, pot8, top_ref, sum_ref):
    z = [v + pot8[:, c * LANES : (c + 1) * LANES] for c, v in enumerate(s)]
    top = tree(jnp.maximum, z)
    top_ref[rows, :] = top
    sum_ref[rows, :] = tree(jnp.add, [jnp.exp2(v - top) for v in z])


def join_lanes(top_ref, sum_ref):
    def strip(k, _):
        rows = eight(k)
        part = top_ref[rows, :]
        top = jnp.broadcast_to(jnp.max(part, axis=1, keepdims=True), part.shape)
        sum_ref[rows, :] = sum_ref[rows, :] * jnp.exp2(part - top)
        top_ref[rows, :] = top * (1.0 / LANES)
        return 0

    lax.fori_loop(0, top_ref.shape[0] // 8, strip, 0, unroll=16)
    return to_row(top_ref[...]) + jnp.log2(to_row(sum_ref[...]))


def rows_log_sum(s_ref, pot, top_ref, sum_ref):
    n, width = s_ref.shape
    pot8 = jnp.broadcast_to(pot, (8, width))

    def strip(k, _):
        rows = eight(k)
        lanes_log_sum([s_ref[rows, chunk(c)] for c in range(width // LANES)], rows, pot8, top_ref, sum_ref)
        return 0

    lax.fori_loop(0, n // 8, strip, 0, unroll=4)
    return join_lanes(top_ref, sum_ref)


def cols_log_sum(s_ref, pot_ref):
    n, width = s_ref.shape
    cols = width // LANES

    def load(k):
        rows = eight(k)
        f = pot_ref[rows, :]
        return [s_ref[rows, chunk(c)] + f for c in range(cols)]

    def find(k, top):
        return tuple(jnp.maximum(t, v) for t, v in zip(top, load(k)))

    top = lax.fori_loop(1, n // 8, find, tuple(load(0)), unroll=4)

    def add(k, total):
        return tuple(a + jnp.exp2(v - t) for a, v, t in zip(total, load(k), top))

    zero = tuple(jnp.zeros((8, LANES), F32) for _ in range(cols))
    total = lax.fori_loop(0, n // 8, add, zero, unroll=4)
    out = []
    for t, a in zip(top, total):
        m = jnp.max(t, axis=0, keepdims=True)
        out.append(m + jnp.log2(jnp.sum(a * jnp.exp2(t - m), axis=0, keepdims=True)))
    return jnp.concatenate(out, axis=1)


def repeat(row, out_ref):
    for t in range(out_ref.shape[0]):
        out_ref[t] = row


def sum_kernel(*refs):
    refs[-1][0] = whole_log_sum(refs[:-1])


def early_kernel(*refs):
    for ref, out_ref in zip(refs[:3], refs[3:]):
        out_ref[...] = ref[...]


def log_kernel(mass_ref, out_ref):
    out_ref[...] = jnp.log2(mass_ref[...])


def stack_kernel(*refs):
    own = refs[0].shape[0]
    for b, ref in enumerate(refs[:-1]):
        refs[-1][pl.ds(b * own, own), :] = ref[...]


def first_kernel(peers, xplan, yplan, me_ref, pot_ref, *refs):
    xcount, ycount = len(xplan), len(yplan)
    xparts, yparts, refs = refs[:xcount], refs[xcount : xcount + ycount], refs[xcount + ycount :]
    s_ref, l_ref, xn_ref, yn_ref, yo_ref, xs, xw, yw, top_ref, sum_ref = refs
    me_src, me_tgt = me_ref[0] // peers, lax.rem(me_ref[0], peers)
    for part, d in zip(xparts, xplan):
        if d is None:
            xs[...] = part[...]
            continue
        own = part.shape[0]
        xs[pl.ds(pl.multiple_of(lax.rem(me_tgt - d + peers, peers) * own, 8), own), :] = part[...]
    x = xs[...]
    xn_ref[...] = jnp.sum(x * x, axis=0, keepdims=True) / x.shape[0]
    x1, x2, _ = pieces(x)
    for part, owners in zip(yparts, yplan):
        if owners is None:
            yo_ref[...] = part[...]
            continue
        own = part.shape[0] // len(owners)
        for b, d in enumerate(owners):
            yo_ref[pl.ds(pl.multiple_of((me_src ^ d) * own, 8), own), :] = part[pl.ds(b * own, own), :]
    y = yo_ref[...]
    yn = jnp.sum(y * y, axis=0, keepdims=True) / y.shape[0]
    yn_ref[...] = yn
    k = y.shape[0]
    y1, y2, _ = pieces(y * (2.0 / (k * UNIT)))
    for p, (xp, yp) in enumerate(((x1, y1), (x1, y2), (x2, y1), (x2, y2))):
        xw[pl.ds(p * k, k), :] = xp
        yw[pl.ds(p * k, k), :] = yp
    n, width = s_ref.shape
    pot8 = jnp.broadcast_to((pot_ref[...] - yn) * (1.0 / UNIT), (8, width))
    step = 256
    for b in range(n // step + 1):
        if b < n // step:
            rows = pl.ds(b * step, step)
            s_ref[rows, :] = lax.dot_general(
                xw[:, rows], yw[...], (((0,), (0,)), ((), ())), preferred_element_type=F32
            )
        if b > 0:
            for r in range((b - 1) * step, b * step, 8):
                rows = pl.ds(r, 8)
                lanes_log_sum([s_ref[rows, chunk(c)] for c in range(width // LANES)], rows, pot8, top_ref, sum_ref)
    l_ref[0] = join_lanes(top_ref, sum_ref)


def src_first_kernel(count, s_ref, mass_ref, *refs):
    parts, (f_ref, p_ref, top_ref, l_ref, wide) = refs[:count], refs[count:]
    f = mass_ref[...] - whole_log_sum(parts)
    f_ref[...] = f
    across(f, wide)
    n, width = s_ref.shape
    cols = width // LANES

    def load(k):
        rows = eight(k)
        f = wide[rows, :]
        return [s_ref[rows, chunk(c)] + f for c in range(cols)]

    def find(k, top):
        return tuple(jnp.maximum(t, v) for t, v in zip(top, load(k)))

    tops = lax.fori_loop(1, n // 8, find, tuple(load(0)), unroll=4)
    top = jnp.concatenate([jnp.max(t, axis=0, keepdims=True) for t in tops], axis=1)
    top8 = jnp.broadcast_to(top, (8, width))

    def add(k, total):
        rows = eight(k)
        out = []
        for c, (a, v) in enumerate(zip(total, load(k))):
            e = jnp.exp2(v - top8[:, c * LANES : (c + 1) * LANES])
            p_ref[rows, chunk(c)] = e
            out.append(a + e)
        return tuple(out)

    zero = tuple(jnp.zeros((8, LANES), F32) for _ in range(cols))
    sums = lax.fori_loop(0, n // 8, add, zero, unroll=4)
    total = jnp.concatenate([jnp.sum(a, axis=0, keepdims=True) for a in sums], axis=1)
    top_ref[...] = top
    repeat(top + jnp.log2(total), l_ref)


def src_kernel(count, s_ref, p_ref, mass_ref, f_ref, g_ref, w_ref, *refs):
    parts, (*u_refs, l_ref, wide) = refs[:count], refs[count:]
    n, width = p_ref.shape
    cols = width // LANES
    change = mass_ref[...] - whole_log_sum(parts)
    for u_ref in u_refs:
        u_ref[...] = change
    u = jnp.exp2(change)
    across(u, wide)

    def add(k, total):
        rows = eight(k)
        f = wide[rows, :]
        return tuple(a + p_ref[rows, chunk(c)] * f for c, a in enumerate(total))

    zero = tuple(jnp.zeros((8, LANES), F32) for _ in range(cols))
    parts = lax.fori_loop(0, n // 8, add, zero, unroll=4)
    total = jnp.concatenate([jnp.sum(a, axis=0, keepdims=True) for a in parts], axis=1)
    repeat(jnp.log2(total) + w_ref[...], l_ref)
    fine = jnp.logical_and(jnp.min(total) >= LOW, jnp.max(u) <= HIGH)

    @pl.when(jnp.logical_not(fine))
    def _():
        across(f_ref[...] + change, wide)
        repeat(g_ref[...] + cols_log_sum(s_ref, wide), l_ref)


def tgt_kernel(first, count, s_ref, p_ref, mass_ref, f_ref, *refs):
    if first:
        top_ref, *refs = refs
        parts, (g_ref, w_ref, l_ref, top8_ref, sum_ref) = refs[:count], refs[count:]
        g = jnp.log2(mass_ref[...]) - whole_log_sum(parts)
        g_ref[...] = g
        w = g + top_ref[...]
        w_ref[...] = w
    else:
        g_ref, w_ref, *refs = refs
        parts, (l_ref, top8_ref, sum_ref) = refs[:count], refs[count:]
        change = jnp.log2(mass_ref[...]) - whole_log_sum(parts)
        g = g_ref[...] + change
        w = w_ref[...] + change
    n, width = p_ref.shape
    v = jnp.exp2(w)
    v8 = jnp.broadcast_to(v, (8, width))

    def strip(k, _):
        rows = eight(k)
        sum_ref[rows, :] = tree(
            jnp.add, [p_ref[rows, chunk(c)] * v8[:, c * LANES : (c + 1) * LANES] for c in range(width // LANES)]
        )
        return 0

    lax.fori_loop(0, n // 8, strip, 0, unroll=4)
    total = to_row(sum_ref[...])
    l_ref[0] = jnp.log2(total)
    fine = jnp.logical_and(jnp.min(total) >= LOW, jnp.max(v) <= HIGH)

    @pl.when(jnp.logical_not(fine))
    def _():
        l_ref[0] = f_ref[...] + rows_log_sum(s_ref, g, top8_ref, sum_ref)


def last_kernel(count, me_ref, s_ref, p_ref, mass_ref, f_ref, g_ref, w_ref, u_ref, xn_ref, yn_ref, y_ref, *refs):
    parts, refs = refs[:count], refs[count:]
    sp_any, tp_any, outs = refs[0], refs[1], refs[2:-7]
    sp, tp, yw, acc, flat, wide, sem = refs[-7:]
    k = y_ref.shape[0]
    n, width = s_ref.shape
    peers = len(outs)
    own = k // peers
    block = own + 1
    change = jnp.log2(mass_ref[...]) - whole_log_sum(parts)
    g = g_ref[...] + change
    f = f_ref[...] + u_ref[...]
    sp[...] = f * UNIT + xn_ref[...]
    tp[...] = g * UNIT + yn_ref[...]
    copies = [pltpu.make_async_copy(sp, sp_any, sem.at[0]), pltpu.make_async_copy(tp, tp_any, sem.at[1])]
    for copy in copies:
        copy.start()
    u = jnp.exp2(u_ref[...])
    v = jnp.exp2(w_ref[...] + change)
    step = 256

    def project(weight, scale, rescale):
        y1, y2, _ = pieces(y_ref[...] * scale)
        s1, s2, _ = [p.astype(F32) for p in pieces(scale)]
        yw[pl.ds(0, k), :] = y1
        at = lax.broadcasted_iota(jnp.int32, (LANES - k, width), 0)
        yw[pl.ds(k, LANES - k), :] = jnp.where(at == 0, s1, jnp.where(at == 1, s2, 0.0)).astype(BF16)
        yw[pl.ds(LANES, k), :] = y2
        yw[pl.ds(LANES + k, LANES - k), :] = jnp.zeros((LANES - k, width), BF16)
        dims = (((1,), (1,)), ((), ()))
        for b in range(n // step):
            rows = pl.ds(b * step, step)
            w = weight(rows)
            w1 = w.astype(BF16)
            w2 = (w - w1.astype(F32)).astype(BF16)
            out = lax.dot_general(w1, yw[...], dims, preferred_element_type=F32) + lax.dot_general(
                w2, yw[...], dims, preferred_element_type=F32
            )
            acc[rows, :] = out[:, :LANES] + out[:, LANES:]
        total = acc[...].T * rescale
        den = total[k : k + 1, :] + total[k + 1 : k + 2, :]
        for t in range(peers):
            for c in range(n // LANES):
                at = slice(c * LANES, (c + 1) * LANES)
                flat[t, pl.ds(c * block, own), :] = total[t * own : (t + 1) * own, at]
                flat[t, pl.ds(c * block + own, 1), :] = den[:, at]
        for d, out in enumerate(outs):
            out[...] = flat[lax.rem(me_ref[0] + d, peers)]
        return den

    den = project(lambda rows: p_ref[rows, :], v, u)
    fine = jnp.logical_and(jnp.min(den) >= LOW, jnp.logical_and(jnp.max(u) <= HIGH, jnp.max(v) <= HIGH))

    @pl.when(jnp.logical_not(fine))
    def _():
        across(f, wide)

        def weight(rows):
            fb = jnp.concatenate([wide[rows, :]] * (width // LANES), axis=1)
            return jnp.exp2((s_ref[rows, :] + fb) + g)

        project(weight, jnp.ones_like(v), jnp.ones_like(u))

    for copy in copies:
        copy.wait()


def join_kernel(*refs):
    parts, out_ref = refs[:-1], refs[-1]
    own, n = out_ref.shape
    for c in range(n // LANES):
        at = c * (own + 1)
        num = tree(jnp.add, [p[pl.ds(at, own), :] for p in parts])
        den = tree(jnp.add, [p[pl.ds(at + own, 1), :] for p in parts])
        out_ref[:, chunk(c)] = num / den


def call(kernel, outs, scratch, ins, out_specs=None, cost=None):
    return pl.pallas_call(
        kernel,
        out_shape=[o if isinstance(o, jax.ShapeDtypeStruct) else jax.ShapeDtypeStruct(o, F32) for o in outs],
        in_specs=[spec for spec, _ in ins],
        out_specs=out_specs or [VMEM] * len(outs),
        scratch_shapes=scratch,
        cost_estimate=cost,
        compiler_params=pltpu.CompilerParams(vmem_limit_bytes=20 * 2**20),
    )(*[a for _, a in ins])


def put(*arrays):
    return [(VMEM, a) for a in arrays]


def turn(v, axis, size, d):
    return lax.ppermute(v, axis, [(i, (i + d) % size) for i in range(size)])


def flip(v, axis, size, bit):
    return lax.ppermute(v, axis, [(i, i ^ bit) for i in range(size)])


def join_rows(v, axis, size):
    if spread(axis, size) > 1:
        return [lax.all_to_all(v, axis, 0, 0, tiled=True)]
    if axis == "tgt":
        return [v] + [turn(v, axis, size, d) for d in range(1, size)]
    if size > 2:
        (v,) = call(sum_kernel, [v.shape], [], put(v, *[turn(v, axis, size, d) for d in range(2, size, 2)]))
    return [v, flip(v, axis, size, 1)]


def spread(axis, size):
    return 1 if size in ((2, 4) if axis == "tgt" else (2, 4, 8)) else size


def gather_src(v, size):
    if v.shape[0] % 8 or size > 4:
        return [lax.all_gather(v, "tgt", axis=0, tiled=True)], [None]
    return [v] + [turn(v, "tgt", size, d) for d in range(1, size)], list(range(size))


def gather_tgt(v, own, size, other):
    if v.shape[0] % 8 or size & (size - 1):
        return [lax.all_gather(v, "src", axis=0, tiled=True)], [None], other
    order = list(range(0, size, 2))
    far = [flip(v, "src", size, d) for d in order[2:]]
    again, last = lax.optimization_barrier((v, other[-1]))
    near = [flip(again, "src", size, d) for d in order[1:2]]
    (mine,) = call(stack_kernel, [(len(order) * v.shape[0], v.shape[1])], [], put(own, *near, *far))
    mine, *other = lax.optimization_barrier([mine] + other[:-1] + [last])
    return [mine, flip(mine, "src", size, 1)], [order, [d + 1 for d in order]], other


def shards(peers_src, peers_tgt, src_pts, tgt_pts, src_mass, tgt_mass, init_pot):
    own = src_pts.shape[0]
    n, width = src_pts.shape[1], tgt_pts.shape[1]
    k = own * peers_tgt
    pack = (own + 1) * (n // LANES)
    row, col = (1, n), (1, width)
    rows, cols = (spread("tgt", peers_tgt), 1, n), (spread("src", peers_src), 1, width)
    lane = pltpu.VMEM((n, LANES), F32)
    me = lax.axis_index(("src", "tgt")).astype(jnp.int32).reshape(1)
    xs, xplan = gather_src(src_pts, peers_tgt)
    pot, x, y = call(
        early_kernel, [col, src_pts.shape, tgt_pts.shape], [], put(init_pot.reshape(col), src_pts, tgt_pts)
    )
    if xplan[0] is not None:
        xs[0] = x
    ys, yplan, xs = gather_tgt(tgt_pts, y, peers_src, xs)
    sm, tm = src_mass.reshape(row), tgt_mass.reshape(col)
    s, l, xn, yn, yo = call(
        functools.partial(first_kernel, peers_tgt, xplan, yplan),
        [(n, width), rows, row, col, (k, width)],
        [
            pltpu.VMEM((k, n), F32),
            pltpu.VMEM((4 * k, n), BF16),
            pltpu.VMEM((4 * k, width), BF16),
            lane,
            lane,
        ],
        [(SMEM, me)] + put(pot, *xs, *ys),
        cost=pl.CostEstimate(flops=8 * k * n * width, transcendentals=n * width, bytes_accessed=8 * n * width),
    )
    sm, l = lax.optimization_barrier((sm, l))
    (sm,) = call(log_kernel, [row], [], put(sm), cost=pl.CostEstimate(flops=n, transcendentals=n, bytes_accessed=8 * n))
    parts = join_rows(l, "tgt", peers_tgt)
    f, p, top, l = call(
        functools.partial(src_first_kernel, len(parts)), [row, (n, width), col, cols], [lane], put(s, sm, *parts)
    )
    parts = join_rows(l, "src", peers_src)
    g, w, l = call(
        functools.partial(tgt_kernel, True, len(parts)),
        [col, col, rows],
        [lane, lane],
        put(s, p, tm, f, top, *parts),
    )
    for step in range(1, ITERS):
        parts = join_rows(l, "tgt", peers_tgt)
        *u, l = call(
            functools.partial(src_kernel, len(parts)),
            [row, cols] if step == ITERS - 1 else [cols],
            [lane],
            put(s, p, sm, f, g, w, *parts),
        )
        parts = join_rows(l, "src", peers_src)
        if step < ITERS - 1:
            (l,) = call(
                functools.partial(tgt_kernel, False, len(parts)),
                [rows],
                [lane, lane],
                put(s, p, tm, f, g, w, *parts),
            )
    src_pot, tgt_pot, *blocks = call(
        functools.partial(last_kernel, len(parts)),
        [row, col] + [(pack, LANES)] * peers_tgt,
        [
            pltpu.VMEM(row, F32),
            pltpu.VMEM(col, F32),
            pltpu.VMEM((2 * LANES, width), BF16),
            lane,
            pltpu.VMEM((peers_tgt, pack, LANES), F32),
            lane,
            pltpu.SemaphoreType.DMA((2,)),
        ],
        [(SMEM, me)] + put(s, p, tm, f, g, w, *u, xn, yn, yo, *parts),
        [HBM, HBM] + [VMEM] * peers_tgt,
    )
    came = [blocks[0]] + [turn(blocks[d], "tgt", peers_tgt, d) for d in range(1, peers_tgt)]
    (mapped,) = call(join_kernel, [(own, n)], [], put(*came))
    return src_pot.reshape(n), tgt_pot.reshape(width), mapped


def solution(mesh):
    return jax.shard_map(
        functools.partial(shards, mesh.shape["src"], mesh.shape["tgt"]),
        mesh=mesh,
        in_specs=(P("tgt", "src"), P("src", "tgt"), P("src"), P("tgt"), P("tgt")),
        out_specs=(P("src"), P("tgt"), P("tgt", "src")),
        check_vma=False,
    )
```

```python
import functools
import math

import jax
import jax.numpy as jnp
from jax import lax
from jax.experimental import pallas as pl
from jax.experimental.pallas import tpu as pltpu
from jax.sharding import PartitionSpec as P

ITERS = 3
EPS = 0.1
UNIT = EPS * math.log(2.0)
LOW = 2.0**-40
HIGH = 2.0**20

F32 = jnp.float32
BF16 = jnp.bfloat16
VMEM = pl.BlockSpec(memory_space=pltpu.VMEM)
SMEM = pl.BlockSpec(memory_space=pltpu.SMEM)
HBM = pl.BlockSpec(memory_space=pltpu.HBM)
LANES = 128


def pieces(v):
    a = v.astype(BF16)
    r = v - a.astype(F32)
    b = r.astype(BF16)
    c = (r - b.astype(F32)).astype(BF16)
    return a, b, c


def tree(op, items):
    items = list(items)
    while len(items) > 1:
        half = (len(items) + 1) // 2
        rest = items[half:]
        items = [op(items[k], rest[k]) if k < len(rest) else items[k] for k in range(half)]
    return items[0]


def whole_log_sum(part_refs):
    if len(part_refs) == 1:
        parts = [part_refs[0][t] for t in range(part_refs[0].shape[0])]
    else:
        parts = [p[0] for p in part_refs]
    top = tree(jnp.maximum, parts)
    return top + jnp.log2(tree(jnp.add, [jnp.exp2(p - top) for p in parts]))


def to_row(wide):
    split = jnp.concatenate(pieces(wide), axis=1)
    ones = jnp.ones((16, split.shape[1]), BF16)
    return lax.dot_general(ones, split, (((1,), (1,)), ((), ())), preferred_element_type=F32)[0:1, :]


def across(row, out_ref):
    n = row.shape[1]
    a, b, c = [p.astype(F32) for p in pieces(row)]
    at = lax.broadcasted_iota(jnp.int32, (16, n), 0)
    split = jnp.where(at == 0, a, jnp.where(at == 1, b, jnp.where(at == 2, c, 0.0))).astype(BF16)
    ones = jnp.ones((16, LANES), BF16)
    out_ref[...] = lax.dot_general(split, ones, (((0,), (0,)), ((), ())), preferred_element_type=F32)


def diagonals():
    lane = lax.broadcasted_iota(jnp.int32, (8, LANES), 1)
    row = lax.broadcasted_iota(jnp.int32, (8, LANES), 0)
    return [lane == row + 8 * s for s in range(LANES // 8)]


def fold(part):
    return jnp.sum(part, axis=0, keepdims=True)


def eight(k):
    return pl.ds(pl.multiple_of(k * 8, 8), 8)


def chunk(c):
    return pl.ds(c * LANES, LANES)


def lanes_log_sum(s, rows, pot8, top_ref, sum_ref):
    z = [v + pot8[:, c * LANES : (c + 1) * LANES] for c, v in enumerate(s)]
    top = tree(jnp.maximum, z)
    top_ref[rows, :] = top
    sum_ref[rows, :] = tree(jnp.add, [jnp.exp2(v - top) for v in z])


def join_lanes(top_ref, sum_ref):
    def strip(k, _):
        rows = eight(k)
        part = top_ref[rows, :]
        top = jnp.broadcast_to(jnp.max(part, axis=1, keepdims=True), part.shape)
        sum_ref[rows, :] = sum_ref[rows, :] * jnp.exp2(part - top)
        top_ref[rows, :] = top * (1.0 / LANES)
        return 0

    lax.fori_loop(0, top_ref.shape[0] // 8, strip, 0, unroll=16)
    return to_row(top_ref[...]) + jnp.log2(to_row(sum_ref[...]))


def rows_log_sum(s_ref, pot, top_ref, sum_ref):
    n, width = s_ref.shape
    pot8 = jnp.broadcast_to(pot, (8, width))

    def strip(k, _):
        rows = eight(k)
        lanes_log_sum([s_ref[rows, chunk(c)] for c in range(width // LANES)], rows, pot8, top_ref, sum_ref)
        return 0

    lax.fori_loop(0, n // 8, strip, 0, unroll=4)
    return join_lanes(top_ref, sum_ref)


def cols_log_sum(s_ref, pot_ref):
    n, width = s_ref.shape
    cols = width // LANES

    def load(k):
        rows = eight(k)
        f = pot_ref[rows, :]
        return [s_ref[rows, chunk(c)] + f for c in range(cols)]

    def find(k, top):
        return tuple(jnp.maximum(t, v) for t, v in zip(top, load(k)))

    top = lax.fori_loop(1, n // 8, find, tuple(load(0)), unroll=4)

    def add(k, total):
        return tuple(a + jnp.exp2(v - t) for a, v, t in zip(total, load(k), top))

    zero = tuple(jnp.zeros((8, LANES), F32) for _ in range(cols))
    total = lax.fori_loop(0, n // 8, add, zero, unroll=4)
    out = []
    for t, a in zip(top, total):
        m = jnp.max(t, axis=0, keepdims=True)
        out.append(m + jnp.log2(jnp.sum(a * jnp.exp2(t - m), axis=0, keepdims=True)))
    return jnp.concatenate(out, axis=1)


def repeat(row, out_ref):
    for t in range(out_ref.shape[0]):
        out_ref[t] = row


def sum_kernel(*refs):
    refs[-1][0] = whole_log_sum(refs[:-1])


def early_kernel(*refs):
    for ref, out_ref in zip(refs[:3], refs[3:]):
        out_ref[...] = ref[...]


def log_kernel(mass_ref, out_ref):
    out_ref[...] = jnp.log2(mass_ref[...])


def stack_kernel(*refs):
    own = refs[0].shape[0]
    for b, ref in enumerate(refs[:-1]):
        refs[-1][pl.ds(b * own, own), :] = ref[...]


def first_kernel(peers, xplan, yplan, me_ref, pot_ref, *refs):
    xcount, ycount = len(xplan), len(yplan)
    xparts, yparts, refs = refs[:xcount], refs[xcount : xcount + ycount], refs[xcount + ycount :]
    s_ref, l_ref, xn_ref, yn_ref, yo_ref, xs, xw, yw = refs
    me_src, me_tgt = me_ref[0] // peers, lax.rem(me_ref[0], peers)
    for part, d in zip(xparts, xplan):
        if d is None:
            xs[...] = part[...]
            continue
        own = part.shape[0]
        xs[pl.ds(pl.multiple_of(lax.rem(me_tgt - d + peers, peers) * own, 8), own), :] = part[...]
    x = xs[...]
    xn_ref[...] = jnp.sum(x * x, axis=0, keepdims=True) / x.shape[0]
    x1, x2, _ = pieces(x)
    for part, owners in zip(yparts, yplan):
        if owners is None:
            yo_ref[...] = part[...]
            continue
        own = part.shape[0] // len(owners)
        for b, d in enumerate(owners):
            yo_ref[pl.ds(pl.multiple_of((me_src ^ d) * own, 8), own), :] = part[pl.ds(b * own, own), :]
    y = yo_ref[...]
    yn = jnp.sum(y * y, axis=0, keepdims=True) / y.shape[0]
    yn_ref[...] = yn
    k = y.shape[0]
    y1, y2, _ = pieces(y * (2.0 / (k * UNIT)))
    for p, (xp, yp) in enumerate(((x1, y1), (x1, y2), (x2, y1), (x2, y2))):
        xw[pl.ds(p * k, k), :] = xp
        yw[pl.ds(p * k, k), :] = yp
    n, width = s_ref.shape
    pot8 = jnp.broadcast_to((pot_ref[...] - yn) * (1.0 / UNIT), (8, width))
    step = 256
    for b in range(n // step + 1):
        if b < n // step:
            rows = pl.ds(b * step, step)
            s_ref[rows, :] = lax.dot_general(
                xw[:, rows], yw[...], (((0,), (0,)), ((), ())), preferred_element_type=F32
            )
        if b > 0:
            for r in range((b - 1) * step, b * step, LANES):
                tops = sums = jnp.zeros((8, LANES), F32)
                for i, own in enumerate(diagonals()):
                    rows = pl.ds(r + 8 * i, 8)
                    z = [s_ref[rows, chunk(c)] + pot8[:, c * LANES : (c + 1) * LANES] for c in range(width // LANES)]
                    part = tree(jnp.maximum, z)
                    total = tree(jnp.add, [jnp.exp2(v - part) for v in z])
                    top = jnp.max(part, axis=1, keepdims=True)
                    tops = jnp.where(own, top, tops)
                    sums = jnp.where(own, jnp.sum(total * jnp.exp2(part - top), axis=1, keepdims=True), sums)
                l_ref[0, :, pl.ds(r, LANES)] = fold(tops) + jnp.log2(fold(sums))


def src_first_kernel(count, s_ref, mass_ref, *refs):
    parts, (f_ref, p_ref, top_ref, l_ref, wide) = refs[:count], refs[count:]
    f = mass_ref[...] - whole_log_sum(parts)
    f_ref[...] = f
    n, width = s_ref.shape
    cols = width // LANES
    f8 = jnp.broadcast_to(f, (8, n))
    tops = [None] * cols
    for block in range(0, n, LANES):
        for i, own in enumerate(diagonals()):
            rows = pl.ds(block + 8 * i, 8)
            here = jnp.sum(jnp.where(own, f8[:, block : block + LANES], 0.0), axis=1, keepdims=True)
            wide[rows, :] = jnp.broadcast_to(here, (8, LANES))
            z = [s_ref[rows, chunk(c)] + here for c in range(cols)]
            tops = [v if t is None else jnp.maximum(t, v) for t, v in zip(tops, z)]
    top = jnp.concatenate([jnp.max(t, axis=0, keepdims=True) for t in tops], axis=1)
    top8 = jnp.broadcast_to(top, (8, width))

    def add(k, total):
        rows = eight(k)
        here = wide[rows, :]
        out = []
        for c, a in enumerate(total):
            e = jnp.exp2((s_ref[rows, chunk(c)] + here) - top8[:, c * LANES : (c + 1) * LANES])
            p_ref[rows, chunk(c)] = e
            out.append(a + e)
        return tuple(out)

    zero = tuple(jnp.zeros((8, LANES), F32) for _ in range(cols))
    sums = lax.fori_loop(0, n // 8, add, zero, unroll=16)
    total = jnp.concatenate([jnp.sum(a, axis=0, keepdims=True) for a in sums], axis=1)
    top_ref[...] = top
    repeat(top + jnp.log2(total), l_ref)


def src_kernel(count, s_ref, p_ref, mass_ref, f_ref, g_ref, w_ref, *refs):
    parts, (*u_refs, l_ref, wide) = refs[:count], refs[count:]
    n, width = p_ref.shape
    cols = width // LANES
    change = mass_ref[...] - whole_log_sum(parts)
    for u_ref in u_refs:
        u_ref[...] = change
    u = jnp.exp2(change)
    u8 = jnp.broadcast_to(u, (8, n))
    sums = [None] * cols
    for block in range(0, n, LANES):
        for i, own in enumerate(diagonals()):
            rows = pl.ds(block + 8 * i, 8)
            here = jnp.sum(jnp.where(own, u8[:, block : block + LANES], 0.0), axis=1, keepdims=True)
            z = [p_ref[rows, chunk(c)] * here for c in range(cols)]
            sums = [v if a is None else a + v for a, v in zip(sums, z)]
    total = jnp.concatenate([jnp.sum(a, axis=0, keepdims=True) for a in sums], axis=1)
    repeat(jnp.log2(total) + w_ref[...], l_ref)
    fine = jnp.logical_and(jnp.min(total) >= LOW, jnp.max(u) <= HIGH)

    @pl.when(jnp.logical_not(fine))
    def _():
        across(f_ref[...] + change, wide)
        repeat(g_ref[...] + cols_log_sum(s_ref, wide), l_ref)


def tgt_kernel(first, count, s_ref, p_ref, mass_ref, f_ref, *refs):
    if first:
        top_ref, *refs = refs
        parts, (g_ref, w_ref, l_ref, top8_ref, sum_ref) = refs[:count], refs[count:]
        g = jnp.log2(mass_ref[...]) - whole_log_sum(parts)
        g_ref[...] = g
        w = g + top_ref[...]
        w_ref[...] = w
    else:
        g_ref, w_ref, *refs = refs
        parts, (l_ref, top8_ref, sum_ref) = refs[:count], refs[count:]
        change = jnp.log2(mass_ref[...]) - whole_log_sum(parts)
        g = g_ref[...] + change
        w = w_ref[...] + change
    n, width = p_ref.shape
    v = jnp.exp2(w)
    v8 = jnp.broadcast_to(v, (8, width))
    out = []
    for block in range(0, n, LANES):
        sums = jnp.zeros((8, LANES), F32)
        for i, own in enumerate(diagonals()):
            rows = pl.ds(block + 8 * i, 8)
            z = [p_ref[rows, chunk(c)] * v8[:, c * LANES : (c + 1) * LANES] for c in range(width // LANES)]
            sums = jnp.where(own, jnp.sum(tree(jnp.add, z), axis=1, keepdims=True), sums)
        out.append(fold(sums))
    total = jnp.concatenate(out, axis=1)
    l_ref[0] = jnp.log2(total)
    fine = jnp.logical_and(jnp.min(total) >= LOW, jnp.max(v) <= HIGH)

    @pl.when(jnp.logical_not(fine))
    def _():
        l_ref[0] = f_ref[...] + rows_log_sum(s_ref, g, top8_ref, sum_ref)


def last_kernel(count, me_ref, s_ref, p_ref, mass_ref, f_ref, g_ref, w_ref, u_ref, xn_ref, yn_ref, y_ref, *refs):
    parts, refs = refs[:count], refs[count:]
    sp_any, tp_any, outs = refs[0], refs[1], refs[2:-7]
    sp, tp, yw, acc, flat, wide, sem = refs[-7:]
    k = y_ref.shape[0]
    n, width = s_ref.shape
    peers = len(outs)
    own = k // peers
    block = own + 1
    change = jnp.log2(mass_ref[...]) - whole_log_sum(parts)
    g = g_ref[...] + change
    f = f_ref[...] + u_ref[...]
    sp[...] = f * UNIT + xn_ref[...]
    tp[...] = g * UNIT + yn_ref[...]
    copies = [pltpu.make_async_copy(sp, sp_any, sem.at[0]), pltpu.make_async_copy(tp, tp_any, sem.at[1])]
    for copy in copies:
        copy.start()
    u = jnp.exp2(u_ref[...])
    v = jnp.exp2(w_ref[...] + change)
    step = 256

    def project(weight, scale, rescale):
        y1, y2, _ = pieces(y_ref[...] * scale)
        s1, s2, _ = [p.astype(F32) for p in pieces(scale)]
        yw[pl.ds(0, k), :] = y1
        at = lax.broadcasted_iota(jnp.int32, (LANES - k, width), 0)
        yw[pl.ds(k, LANES - k), :] = jnp.where(at == 0, s1, jnp.where(at == 1, s2, 0.0)).astype(BF16)
        yw[pl.ds(LANES, k), :] = y2
        yw[pl.ds(LANES + k, LANES - k), :] = jnp.zeros((LANES - k, width), BF16)
        dims = (((1,), (1,)), ((), ()))
        for b in range(n // step):
            rows = pl.ds(b * step, step)
            w = weight(rows)
            w1 = w.astype(BF16)
            w2 = (w - w1.astype(F32)).astype(BF16)
            out = lax.dot_general(w1, yw[...], dims, preferred_element_type=F32) + lax.dot_general(
                w2, yw[...], dims, preferred_element_type=F32
            )
            acc[rows, :] = out[:, :LANES] + out[:, LANES:]
        total = acc[...].T * rescale
        den = total[k : k + 1, :] + total[k + 1 : k + 2, :]
        for t in range(peers):
            for c in range(n // LANES):
                at = slice(c * LANES, (c + 1) * LANES)
                flat[t, pl.ds(c * block, own), :] = total[t * own : (t + 1) * own, at]
                flat[t, pl.ds(c * block + own, 1), :] = den[:, at]
        for d, out in enumerate(outs):
            out[...] = flat[lax.rem(me_ref[0] + d, peers)]
        return den

    den = project(lambda rows: p_ref[rows, :], v, u)
    fine = jnp.logical_and(jnp.min(den) >= LOW, jnp.logical_and(jnp.max(u) <= HIGH, jnp.max(v) <= HIGH))

    @pl.when(jnp.logical_not(fine))
    def _():
        across(f, wide)

        def weight(rows):
            fb = jnp.concatenate([wide[rows, :]] * (width // LANES), axis=1)
            return jnp.exp2((s_ref[rows, :] + fb) + g)

        project(weight, jnp.ones_like(v), jnp.ones_like(u))

    for copy in copies:
        copy.wait()


def join_kernel(*refs):
    parts, out_ref = refs[:-1], refs[-1]
    own, n = out_ref.shape
    for c in range(n // LANES):
        at = c * (own + 1)
        num = tree(jnp.add, [p[pl.ds(at, own), :] for p in parts])
        den = tree(jnp.add, [p[pl.ds(at + own, 1), :] for p in parts])
        out_ref[:, chunk(c)] = num / den


def call(kernel, outs, scratch, ins, out_specs=None, cost=None):
    return pl.pallas_call(
        kernel,
        out_shape=[o if isinstance(o, jax.ShapeDtypeStruct) else jax.ShapeDtypeStruct(o, F32) for o in outs],
        in_specs=[spec for spec, _ in ins],
        out_specs=out_specs or [VMEM] * len(outs),
        scratch_shapes=scratch,
        cost_estimate=cost,
        compiler_params=pltpu.CompilerParams(vmem_limit_bytes=20 * 2**20),
    )(*[a for _, a in ins])


def put(*arrays):
    return [(VMEM, a) for a in arrays]


def turn(v, axis, size, d):
    return lax.ppermute(v, axis, [(i, (i + d) % size) for i in range(size)])


def flip(v, axis, size, bit):
    return lax.ppermute(v, axis, [(i, i ^ bit) for i in range(size)])


def join_rows(v, axis, size):
    if spread(axis, size) > 1:
        return [lax.all_to_all(v, axis, 0, 0, tiled=True)]
    if axis == "tgt":
        return [v] + [turn(v, axis, size, d) for d in range(1, size)]
    if size > 2:
        (v,) = call(sum_kernel, [v.shape], [], put(v, *[turn(v, axis, size, d) for d in range(2, size, 2)]))
    return [v, flip(v, axis, size, 1)]


def spread(axis, size):
    return 1 if size in ((2, 4) if axis == "tgt" else (2, 4, 8)) else size


def gather_src(v, size):
    if v.shape[0] % 8 or size > 4:
        return [lax.all_gather(v, "tgt", axis=0, tiled=True)], [None]
    return [v] + [turn(v, "tgt", size, d) for d in range(1, size)], list(range(size))


def gather_tgt(v, own, size, other):
    if v.shape[0] % 8 or size & (size - 1):
        return [lax.all_gather(v, "src", axis=0, tiled=True)], [None], other
    order = list(range(0, size, 2))
    far = [flip(v, "src", size, d) for d in order[2:]]
    again, last = lax.optimization_barrier((v, other[-1]))
    near = [flip(again, "src", size, d) for d in order[1:2]]
    (mine,) = call(stack_kernel, [(len(order) * v.shape[0], v.shape[1])], [], put(own, *near, *far))
    mine, *other = lax.optimization_barrier([mine] + other[:-1] + [last])
    return [mine, flip(mine, "src", size, 1)], [order, [d + 1 for d in order]], other


def shards(peers_src, peers_tgt, src_pts, tgt_pts, src_mass, tgt_mass, init_pot):
    own = src_pts.shape[0]
    n, width = src_pts.shape[1], tgt_pts.shape[1]
    k = own * peers_tgt
    pack = (own + 1) * (n // LANES)
    row, col = (1, n), (1, width)
    rows, cols = (spread("tgt", peers_tgt), 1, n), (spread("src", peers_src), 1, width)
    lane = pltpu.VMEM((n, LANES), F32)
    me = lax.axis_index(("src", "tgt")).astype(jnp.int32).reshape(1)
    xs, xplan = gather_src(src_pts, peers_tgt)
    pot, x, y = call(
        early_kernel, [col, src_pts.shape, tgt_pts.shape], [], put(init_pot.reshape(col), src_pts, tgt_pts)
    )
    if xplan[0] is not None:
        xs[0] = x
    ys, yplan, xs = gather_tgt(tgt_pts, y, peers_src, xs)
    sm, tm = src_mass.reshape(row), tgt_mass.reshape(col)
    s, l, xn, yn, yo = call(
        functools.partial(first_kernel, peers_tgt, xplan, yplan),
        [(n, width), rows, row, col, (k, width)],
        [
            pltpu.VMEM((k, n), F32),
            pltpu.VMEM((4 * k, n), BF16),
            pltpu.VMEM((4 * k, width), BF16),
        ],
        [(SMEM, me)] + put(pot, *xs, *ys),
        cost=pl.CostEstimate(flops=8 * k * n * width, transcendentals=n * width, bytes_accessed=8 * n * width),
    )
    sm, l = lax.optimization_barrier((sm, l))
    (sm,) = call(log_kernel, [row], [], put(sm), cost=pl.CostEstimate(flops=n, transcendentals=n, bytes_accessed=8 * n))
    parts = join_rows(l, "tgt", peers_tgt)
    f, p, top, l = call(
        functools.partial(src_first_kernel, len(parts)), [row, (n, width), col, cols], [lane], put(s, sm, *parts)
    )
    parts = join_rows(l, "src", peers_src)
    g, w, l = call(
        functools.partial(tgt_kernel, True, len(parts)),
        [col, col, rows],
        [lane, lane],
        put(s, p, tm, f, top, *parts),
    )
    for step in range(1, ITERS):
        parts = join_rows(l, "tgt", peers_tgt)
        *u, l = call(
            functools.partial(src_kernel, len(parts)),
            [row, cols] if step == ITERS - 1 else [cols],
            [lane],
            put(s, p, sm, f, g, w, *parts),
        )
        parts = join_rows(l, "src", peers_src)
        if step < ITERS - 1:
            (l,) = call(
                functools.partial(tgt_kernel, False, len(parts)),
                [rows],
                [lane, lane],
                put(s, p, tm, f, g, w, *parts),
            )
    src_pot, tgt_pot, *blocks = call(
        functools.partial(last_kernel, len(parts)),
        [row, col] + [(pack, LANES)] * peers_tgt,
        [
            pltpu.VMEM(row, F32),
            pltpu.VMEM(col, F32),
            pltpu.VMEM((2 * LANES, width), BF16),
            lane,
            pltpu.VMEM((peers_tgt, pack, LANES), F32),
            lane,
            pltpu.SemaphoreType.DMA((2,)),
        ],
        [(SMEM, me)] + put(s, p, tm, f, g, w, *u, xn, yn, yo, *parts),
        [HBM, HBM] + [VMEM] * peers_tgt,
    )
    came = [blocks[0]] + [turn(blocks[d], "tgt", peers_tgt, d) for d in range(1, peers_tgt)]
    (mapped,) = call(join_kernel, [(own, n)], [], put(*came))
    return src_pot.reshape(n), tgt_pot.reshape(width), mapped


def solution(mesh):
    return jax.shard_map(
        functools.partial(shards, mesh.shape["src"], mesh.shape["tgt"]),
        mesh=mesh,
        in_specs=(P("tgt", "src"), P("src", "tgt"), P("src"), P("tgt"), P("tgt")),
        out_specs=(P("src"), P("tgt"), P("tgt", "src")),
        check_vma=False,
    )
```
